32 devices in a mesh: row: 2 (over y), col: 16 (over z, x, core).
Axes of the slice: x: 2, y: 2, z: 4, core: 2. Of those that a mesh axis runs over, the one named last changes fastest.
Arguments:
- positions: float32 [3, 32768], P(None, ('row', 'col')), may hold values from -6 to 6
- types: int32 [32768], P(('row', 'col')), may hold values from 0 to 4
- radius_type: float32 [5], replicated, may hold values from 0.6 to 1.2
- valence_type: float32 [5], replicated, may hold values from 5 to 60
- bond_depth: float32 [5, 5], replicated, may hold values from 0.02 to 0.2
- pair_tiles: int32 [2, 16, 96, 2], P('row', 'col'), may hold values from 0 to 127, as said below
- tile_count: int32 [2, 16], P('row', 'col'), may hold values from 24 to 96, as said below
Outputs:
- force_energy: float32 [4, 32768], P(None, ('row', 'col'))
The draws below stay inside these ranges and needn't reach their ends.
Inputs may be any that keep to these rules, and one draw needn't show every extreme that they name: `pair_tiles`: each entry is (a, b) with a below 128 and b below 16; the 96 tiles of one device are distinct. Only the first tile_count[r, c] tiles of device (r, c) are live; the most, 96, is reached on some device in every draw.
All inputs are finite; a program needn't handle non-finite values.
Results may differ from the reference program's by a relative error of at most 0.0003.
Values sent between devices are 32-bit elements; how exact they have to be, the bound alone decides.
No kernel may reach another device: no remote copies, remote signals or barrier semaphores. Data moves between devices by JAX's collectives and lax.ppermute only.
A program may use at most 64 MiB of HBM per device.

```python
import math
import jax
import jax.numpy as jnp
from jax import lax

ATOM_DEV = 1024
TILES_DEV = 96
TILE = 128
ELEMENTS = 5
ATOMS = 32768
ROW_BLOCKS = 128
COL_BLOCKS = 16
N_ROW = 2
N_COL = 16


def draw_pair_tiles(key, part):
    subkeys = jax.random.split(jax.random.fold_in(key, 11), N_ROW * N_COL)
    chosen = jax.vmap(lambda single: jax.random.permutation(single, ROW_BLOCKS * COL_BLOCKS)[:TILES_DEV])(subkeys)
    chosen = chosen.astype(jnp.int32)
    stacked = jnp.stack([chosen // COL_BLOCKS, chosen % COL_BLOCKS], axis=-1)
    return stacked.reshape(N_ROW, N_COL, TILES_DEV, 2).astype(jnp.int32)


def draw_tile_count(key, part):
    first_key, second_key = jax.random.split(jax.random.fold_in(key, 23))
    counts = jax.random.randint(first_key, (N_ROW * N_COL,), TILES_DEV // 4, TILES_DEV // 2 + 1)
    busiest = jax.random.randint(second_key, (), 0, N_ROW * N_COL)
    spread = counts.at[busiest].set(TILES_DEV)
    return spread.reshape(N_ROW, N_COL).astype(jnp.int32)


def set_ends(drawn, own_key, smallest, high):
    shape = drawn.shape
    place = [jax.random.randint(jax.random.fold_in(own_key, axis), (), 0, shape[axis]) for axis in range(len(shape))]
    drawn = drawn.at[tuple(place)].set(smallest)
    longest = shape.index(max(shape))
    place[longest] = (place[longest] + 1) % shape[longest]
    return drawn.at[tuple(place)].set(high)


def levels(rng, dims, shards, smallest, high):
    def one(position, shards_of):
        draws = jax.random.uniform(jax.random.fold_in(jax.random.fold_in(rng, 6), position), (shards_of,), jnp.float32, smallest / len(shards), high / len(shards))
        return jnp.repeat(jnp.exp(draws), dims[position] // shards_of).reshape((-1,) + (1,) * (len(dims) - position - 1))

    level = one(*shards[0])
    for cut in shards[1:]:
        level = level * one(*cut)
    return level


def gaussian(key, extent, scale, reach, shards=(), held_as=jnp.bfloat16):
    factor_of = levels(key, extent, shards, -0.22, 0.18) if shards else 1.0
    drawn = jax.random.normal(key, extent, jnp.float32) * scale * factor_of
    return jnp.minimum(jnp.maximum(drawn, -reach), reach).astype(held_as)


def setup_inputs(seed: int = 0) -> dict:
    seeds = jax.random.split(jax.random.key(seed), 8)
    positions = gaussian(seeds[0], (3, ATOMS), 1.0, 6.0, ((1, 32),), jnp.float32)
    types = set_ends(jax.random.randint(seeds[1], (ATOMS,), 0, ELEMENTS), jax.random.fold_in(seeds[1], 1), 0, ELEMENTS - 1).astype(jnp.int32)
    radius_type = jnp.clip(jnp.exp(jax.random.uniform(seeds[2], (ELEMENTS,), jnp.float32, math.log(0.6), math.log(1.2))), 0.6, 1.2)
    valence_type = jnp.clip(jnp.exp(jax.random.uniform(seeds[3], (ELEMENTS,), jnp.float32, math.log(5.0), math.log(60.0))), 5.0, 60.0)
    bond_depth = jnp.clip(jnp.exp(jax.random.uniform(seeds[4], (ELEMENTS, ELEMENTS), jnp.float32, math.log(0.02), math.log(0.2))), 0.02, 0.2)
    pair_tiles = draw_pair_tiles(jax.random.fold_in(seeds[7], 71), 0)
    tile_count = draw_tile_count(jax.random.fold_in(seeds[7], 71), 0)
    return {"positions": positions, "types": types, "radius_type": radius_type, "valence_type": valence_type, "bond_depth": bond_depth, "pair_tiles": pair_tiles, "tile_count": tile_count}


def geometry(pos_blocks, radius_blocks, id_blocks, row_idx, col_idx, live_now):
    near_pos = pos_blocks[:, row_idx]
    far_pos = pos_blocks[:, col_idx]
    offset = near_pos[:, :, :, None] - far_pos[:, :, None, :]
    dist_sq = jnp.sum(offset * offset, axis=0)
    rho = 0.5 * (radius_blocks[row_idx][:, :, None] + radius_blocks[col_idx][:, None, :])
    ratio = dist_sq / (rho * rho)
    valid = (id_blocks[row_idx][:, :, None] != id_blocks[col_idx][:, None, :]) & live_now[:, None, None]
    bond_raw = jnp.where(valid, jnp.exp(-(ratio * ratio * ratio)), jnp.float32(0.0))
    return offset, rho, ratio, bond_raw


def reference(positions, types, radius_type, valence_type, bond_depth, pair_tiles, tile_count):
    blocks = ATOMS // TILE
    per_block = ATOM_DEV // TILE
    row_axis = jnp.arange(N_ROW, dtype=jnp.int32)[:, None, None]
    col_axis = jnp.arange(N_COL, dtype=jnp.int32)[None, :, None]
    first = pair_tiles[..., 0]
    second = pair_tiles[..., 1]
    row_global = (row_axis * ROW_BLOCKS + first).astype(jnp.int32)
    col_global = (((second // per_block) * N_COL + col_axis) * per_block + second % per_block).astype(jnp.int32)
    slots = jnp.arange(TILES_DEV, dtype=jnp.int32)[None, None, :]
    live = slots < tile_count[:, :, None]
    row_global = row_global.reshape(-1, 8)
    col_global = col_global.reshape(-1, 8)
    live = live.reshape(-1, 8)
    pos_blocks = positions.reshape(3, blocks, TILE)
    radius_blocks = radius_type[types].reshape(blocks, TILE)
    valence_blocks = valence_type[types].reshape(blocks, TILE)
    type_blocks = types.reshape(blocks, TILE)
    id_blocks = jnp.arange(ATOMS, dtype=jnp.int32).reshape(blocks, TILE)

    def first_pass(total, inputs):
        row_idx, col_idx, live_now = inputs
        offset, rho, ratio, bond_raw = geometry(pos_blocks, radius_blocks, id_blocks, row_idx, col_idx, live_now)
        return total.at[row_idx].add(jnp.sum(bond_raw, axis=2)), None

    coordination, unused = lax.scan(first_pass, jnp.zeros((blocks, TILE), jnp.float32), (row_global, col_global, live))

    def second_pass(total, inputs):
        row_idx, col_idx, live_now = inputs
        offset, rho, ratio, bond_raw = geometry(pos_blocks, radius_blocks, id_blocks, row_idx, col_idx, live_now)
        val_sum = valence_blocks[row_idx][:, :, None] + valence_blocks[col_idx][:, None, :]
        coupling = val_sum / (val_sum + coordination[row_idx][:, :, None] + coordination[col_idx][:, None, :])
        depth_pair = bond_depth[type_blocks[row_idx][:, :, None], type_blocks[col_idx][:, None, :]]
        weight = depth_pair * coupling * bond_raw
        pull = 6.0 * weight * ratio * ratio / (rho * rho)
        forces = -jnp.sum(pull[None] * offset, axis=3)
        energy = -jnp.sum(weight, axis=2)
        terms = jnp.concatenate([forces, energy[None]], axis=0)
        return total.at[:, row_idx].add(terms), None

    result, unused = lax.scan(second_pass, jnp.zeros((4, blocks, TILE), jnp.float32), (row_global, col_global, live))
    return result.reshape(4, ATOMS)
```

```python
import functools
import math

import jax
import jax.numpy as jnp
from jax import lax
from jax.experimental import pallas as pl
from jax.experimental.pallas import tpu as pltpu
from jax.sharding import PartitionSpec as P

TILE = 128
SUB = 8
UNROLL = 4
LOG2E = math.log2(math.e)
SCALE = LOG2E ** (1.0 / 3.0)


def stage_bits(col_size, row_size):
    order = []
    bit = col_size // 2
    while bit >= 2:
        order.append(("col", bit))
        bit //= 2
    bit = row_size // 2
    while bit >= 1:
        order.append(("row", bit))
        bit //= 2
    if col_size > 1:
        order.append(("col", 1))
    return order


def virtual(order, row, col):
    total = 0 * row
    for place, (axis, bit) in enumerate(order):
        index = row if axis == "row" else col
        total = total + ((index // bit) % 2) * (1 << place)
    return total


def pieces(value):
    high = value.astype(jnp.bfloat16).astype(jnp.float32)
    rest = value - high
    mid = rest.astype(jnp.bfloat16).astype(jnp.float32)
    return high, mid, rest - mid


def left_form(base, onehot):
    high, mid, low = pieces(base)
    zero = jnp.zeros_like(base)
    stack = jnp.concatenate([high, high, mid, high, low, mid, onehot, onehot, onehot, zero], axis=0)
    return stack.astype(jnp.bfloat16)


def right_geometry(base):
    high, mid, low = pieces(base)
    zero = jnp.zeros_like(base)
    stack = jnp.concatenate([high, mid, high, low, high, mid, zero, zero, zero, zero], axis=0)
    return stack.astype(jnp.bfloat16)


def right_table(rows):
    high, mid, low = pieces(rows)
    zero = jnp.zeros_like(rows)
    stack = jnp.concatenate([zero] * 6 + [high, mid, low, zero], axis=0)
    return stack.astype(jnp.bfloat16)


def cross(left, right):
    return lax.dot_general(left, right, (((0,), (0,)), ((), ())), preferred_element_type=jnp.float32)


def fold(value):
    return jnp.sum(value.reshape(TILE // SUB, SUB, TILE), axis=0)


def kernel(
    row_place,
    row_bits,
    elements,
    rho_table,
    depth_table,
    valence,
    lists,
    atoms,
    out,
    left_base,
    right_base,
    onehot,
    rho_rows,
    coord,
    right_own,
    total,
    needed,
    own_list,
    work_list,
):
    slots, payload, lanes = atoms.shape
    blocks_dev = SUB
    blocks = slots * blocks_dev
    ones = jnp.ones((SUB, TILE), jnp.float32)
    zeros = jnp.zeros((SUB, TILE), jnp.float32)

    def put(ref, slot, row, value):
        ref[pl.ds(slot * blocks_dev * SUB + row, blocks_dev, stride=SUB), :] = value

    def prepare(slot, carry):
        x = atoms[slot, 0:8, :]
        y = atoms[slot, 8:16, :]
        z = atoms[slot, 16:24, :]
        kind = atoms[slot, 24:32, :]
        square = x * x + y * y + z * z
        hot = [jnp.where(kind == float(t), 1.0, 0.0) for t in range(elements)]
        value = zeros
        for t in range(elements):
            value = value + hot[t] * valence[t]
        for row, item in enumerate((x, y, z, square, ones, value, zeros, zeros)):
            put(left_base, slot, row, item)
        for row, item in enumerate((-2.0 * x, -2.0 * y, -2.0 * z, ones, square, zeros, zeros, zeros)):
            put(right_base, slot, row, item)
        for row in range(SUB):
            put(onehot, slot, row, hot[row] if row < elements else zeros)
            if row < elements:
                mixed = hot[0] * rho_table[row, 0]
                for t in range(1, elements):
                    mixed = mixed + hot[t] * rho_table[row, t]
            else:
                mixed = zeros
            put(rho_rows, slot, row, mixed)
        for block in range(blocks_dev):
            coord[slot * blocks_dev + block] = zeros
        return carry

    lax.fori_loop(0, slots, prepare, 0)

    def clear(block, carry):
        needed[block] = 0
        return carry

    lax.fori_loop(0, 2 * blocks, clear, 0)

    def scan_own(turn, count):
        slot = ((turn >> row_place) << (row_place + row_bits)) | (turn & ((1 << row_place) - 1))
        live = lists[slot * 3 + 2, 0]

        def entry(index, count):
            first = lists[slot * 3, index]
            second = lists[slot * 3 + 1, index]
            mine = first < blocks_dev
            own_list[2 * count] = first
            own_list[2 * count + 1] = second

            @pl.when(mine)
            def _():
                needed[first] = 1
                needed[second] = 1

            return count + mine.astype(jnp.int32)

        return lax.fori_loop(0, live, entry, count)

    own_count = lax.fori_loop(0, slots >> row_bits, scan_own, 0)

    def scan_all(slot, count):
        live = lists[slot * 3 + 2, 0]

        def entry(index, count):
            first = lists[slot * 3, index]
            second = lists[slot * 3 + 1, index]
            work_list[2 * count] = first
            work_list[2 * count + 1] = second
            return count + needed[first]

        return lax.fori_loop(0, live, entry, count)

    work_count = lax.fori_loop(0, slots, scan_all, 0)
    for extra in range(UNROLL):
        work_list[2 * (work_count + extra)] = blocks
        work_list[2 * (work_count + extra) + 1] = 0

    def at(ref, block):
        return ref[pl.ds(pl.multiple_of(block * SUB, SUB), SUB), :]

    def first_pass(group, carry):
        for step in range(UNROLL):
            place = 2 * (group * UNROLL + step)
            first = work_list[place]
            second = work_list[place + 1]
            source = jnp.minimum(first, blocks - 1)
            left = left_form(at(left_base, second), at(onehot, second))
            right = jnp.concatenate(
                [right_geometry(at(right_base, source)), right_table(at(rho_rows, source))], axis=1
            )
            both = cross(left, right)
            ratio = both[:, :TILE] * both[:, TILE:]
            bond = jnp.exp2(ratio * ratio * ratio)
            same = jnp.where(first == second, 1.0 / SUB, 0.0)
            coord[first] = coord[first] + (fold(bond) - same)
        return carry

    lax.fori_loop(0, (work_count + UNROLL - 1) // UNROLL, first_pass, 0)

    sub_index = lax.broadcasted_iota(jnp.int32, (SUB, TILE), 0)

    for block in range(blocks_dev):
        base = at(left_base, block)
        hot = at(onehot, block)
        load = jnp.sum(coord[block], axis=0, keepdims=True) + base[5:6]
        depth_rows = zeros
        for row in range(elements):
            mixed = hot[0:1] * depth_table[row, 0]
            for t in range(1, elements):
                mixed = mixed + hot[t : t + 1] * depth_table[row, t]
            depth_rows = jnp.where(sub_index == row, mixed, depth_rows)
        load_rows = jnp.where(sub_index == 4, load, jnp.where(sub_index == 5, 1.0, 0.0))
        forms = [
            right_geometry(at(right_base, block)),
            right_table(at(rho_rows, block)),
            right_table(depth_rows),
            right_geometry(load_rows),
        ]
        for d in range(3):
            shift = jnp.where(sub_index == d, 1.0, jnp.where(sub_index == 4, -base[d : d + 1], 0.0))
            forms.append(right_geometry(shift))
        right_own[block] = jnp.concatenate(forms, axis=1)
        for d in range(4):
            total[block, d] = zeros

    step_index = lax.broadcasted_iota(jnp.int32, (TILE, TILE), 0) - lax.broadcasted_iota(
        jnp.int32, (TILE, TILE), 1
    )

    def second_pass(index, carry):
        first = own_list[2 * index]
        second = own_list[2 * index + 1]
        load = jnp.sum(coord[second], axis=0, keepdims=True)
        base = at(left_base, second)
        base = base + jnp.where(sub_index == 5, load, 0.0)
        left = left_form(base, at(onehot, second))
        mixed = cross(left, right_own[first])
        parts = [mixed[:, k * TILE : (k + 1) * TILE] for k in range(7)]
        dist, rho, depth, both_load = parts[:4]
        ratio = dist * rho
        squared = ratio * ratio
        bond = jnp.exp2(squared * ratio)
        bond = jnp.where(step_index == jnp.where(first == second, 0, TILE), 0.0, bond)
        weight = depth * bond / both_load
        pull = weight * squared * rho
        for d in range(3):
            total[first, d] = total[first, d] + fold(pull * parts[4 + d])
        total[first, 3] = total[first, 3] + fold(weight)
        return carry

    lax.fori_loop(0, own_count, second_pass, 0)

    for block in range(blocks_dev):
        for d in range(4):
            factor = -6.0 / LOG2E if d < 3 else -1.0
            out[d, block : block + 1, :] = factor * jnp.sum(total[block, d], axis=0, keepdims=True)


def local(order, positions, types, radius_type, valence_type, bond_depth, pair_tiles, tile_count):
    atom_dev = positions.shape[1]
    blocks_dev = atom_dev // TILE
    rows = lax.axis_size("row")
    cols = lax.axis_size("col")
    slots = rows * cols
    blocks = slots * blocks_dev
    tiles_dev = pair_tiles.shape[2]
    row_index = lax.axis_index("row")
    col_index = lax.axis_index("col")
    me = virtual(order, row_index, col_index)

    tiles = pair_tiles[0, 0]
    first = virtual(order, row_index, tiles[:, 0] // blocks_dev) * blocks_dev + tiles[:, 0] % blocks_dev
    second = virtual(order, tiles[:, 1] // blocks_dev, col_index) * blocks_dev + tiles[:, 1] % blocks_dev
    fill = TILE - tiles_dev
    meta = jnp.stack(
        [jnp.pad(first, (0, fill)), jnp.pad(second, (0, fill)), jnp.broadcast_to(tile_count[0, 0], (TILE,))]
    )
    packed = jnp.concatenate(
        [
            positions.reshape(3 * blocks_dev, TILE),
            types.astype(jnp.float32).reshape(blocks_dev, TILE),
            meta.astype(jnp.float32),
            jnp.zeros((5, TILE), jnp.float32),
        ]
    )
    gathered = packed[None]
    for axis, bit in order:
        size = lax.axis_size(axis)
        other = lax.ppermute(gathered, axis, [(i, i ^ bit) for i in range(size)])
        gathered = jnp.concatenate([gathered, other], axis=0)

    flip = jnp.where(jnp.arange(3) < 2, me * blocks_dev, 0).astype(jnp.int32)
    lists = gathered[:, 4 * blocks_dev : 4 * blocks_dev + 3, :].astype(jnp.int32) ^ flip[None, :, None]
    lists = lists.reshape(slots * 3, TILE)

    rho = 0.5 * (radius_type[:, None] + radius_type[None, :])
    rho_table = -SCALE / (rho * rho)
    depth_table = (bond_depth * (valence_type[:, None] + valence_type[None, :])).T

    elements = radius_type.shape[0]
    row_place = [axis for axis, bit in order].index("row") if rows > 1 else 0
    row_bits = sum(axis == "row" for axis, bit in order)
    smem = pl.BlockSpec(memory_space=pltpu.SMEM)
    vmem = pl.BlockSpec(memory_space=pltpu.VMEM)
    force = pl.pallas_call(
        functools.partial(kernel, row_place, row_bits, elements),
        out_shape=jax.ShapeDtypeStruct((4, blocks_dev, TILE), jnp.float32),
        in_specs=[smem, smem, smem, smem, vmem],
        out_specs=vmem,
        scratch_shapes=[
            pltpu.VMEM((blocks * SUB, TILE), jnp.float32),
            pltpu.VMEM((blocks * SUB, TILE), jnp.float32),
            pltpu.VMEM((blocks * SUB, TILE), jnp.float32),
            pltpu.VMEM((blocks * SUB, TILE), jnp.float32),
            pltpu.VMEM((blocks + 1, SUB, TILE), jnp.float32),
            pltpu.VMEM((blocks_dev, 10 * SUB, 7 * TILE), jnp.bfloat16),
            pltpu.VMEM((blocks_dev, 4, SUB, TILE), jnp.float32),
            pltpu.SMEM((2 * blocks,), jnp.int32),
            pltpu.SMEM((2 * (cols * tiles_dev + 1),), jnp.int32),
            pltpu.SMEM((2 * (slots * tiles_dev + UNROLL),), jnp.int32),
        ],
        compiler_params=pltpu.CompilerParams(vmem_limit_bytes=56 * 1024 * 1024),
    )(rho_table, depth_table, valence_type, lists, gathered)
    return force.reshape(4, atom_dev)


def solution(mesh):
    order = stage_bits(mesh.shape["col"], mesh.shape["row"])
    in_specs = (
        P(None, ("row", "col")),
        P(("row", "col")),
        P(),
        P(),
        P(),
        P("row", "col", None, None),
        P("row", "col"),
    )
    out_specs = P(None, ("row", "col"))
    return jax.shard_map(
        functools.partial(local, order), mesh=mesh, in_specs=in_specs, out_specs=out_specs, check_vma=False
    )
```

```python
import functools
import math

import jax
import jax.numpy as jnp
from jax import lax
from jax.experimental import pallas as pl
from jax.experimental.pallas import tpu as pltpu
from jax.sharding import PartitionSpec as P

TILE = 128
SUB = 8
UNROLL = 16
UNROLL2 = 4
LOG2E = math.log2(math.e)
SCALE = LOG2E ** (1.0 / 3.0)


def stage_bits(col_size, row_size):
    order = []
    bit = col_size // 2
    while bit >= 2:
        order.append(("col", bit))
        bit //= 2
    bit = row_size // 2
    while bit >= 1:
        order.append(("row", bit))
        bit //= 2
    if col_size > 1:
        order.append(("col", 1))
    return order


def virtual(order, row, col):
    total = 0 * row
    for place, (axis, bit) in enumerate(order):
        index = row if axis == "row" else col
        total = total + ((index // bit) % 2) * (1 << place)
    return total


def pieces(value):
    high = value.astype(jnp.bfloat16).astype(jnp.float32)
    rest = value - high
    mid = rest.astype(jnp.bfloat16).astype(jnp.float32)
    return high, mid, rest - mid


def left_form(base, onehot):
    high, mid, low = pieces(base)
    zero = jnp.zeros_like(base)
    stack = jnp.concatenate([high, high, mid, high, low, mid, onehot, onehot, onehot, zero], axis=0)
    return stack.astype(jnp.bfloat16)


def right_geometry(base):
    high, mid, low = pieces(base)
    zero = jnp.zeros_like(base)
    stack = jnp.concatenate([high, mid, high, low, high, mid, zero, zero, zero, zero], axis=0)
    return stack.astype(jnp.bfloat16)


def right_table(rows):
    high, mid, low = pieces(rows)
    zero = jnp.zeros_like(rows)
    stack = jnp.concatenate([zero] * 6 + [high, mid, low, zero], axis=0)
    return stack.astype(jnp.bfloat16)


def cross(left, right):
    return lax.dot_general(left, right, (((0,), (0,)), ((), ())), preferred_element_type=jnp.float32)


def fold(value):
    return jnp.sum(value.reshape(TILE // SUB, SUB, TILE), axis=0)


def kernel(
    elements,
    shift,
    flip_ref,
    rho_table,
    depth_table,
    valence,
    atoms,
    out,
    left_base,
    right_base,
    onehot,
    rho_rows,
    coord,
    right_own,
    total,
    ranks,
    marks,
    firsts,
    second_cols,
    flat,
    own_list,
    work_list,
    sem,
):
    payload = 5 * SUB
    slots = atoms.shape[0] // payload
    blocks_dev = SUB
    blocks = slots * blocks_dev
    flip = flip_ref[0]
    ones = jnp.ones((SUB, TILE), jnp.float32)
    zeros = jnp.zeros((SUB, TILE), jnp.float32)

    def put(ref, slot, row, value):
        ref[pl.ds(slot * blocks_dev * SUB + row, blocks_dev, stride=SUB), :] = value

    def prepare(slot, carry):
        start = pl.multiple_of(slot * payload, SUB)
        x = atoms[pl.ds(start, SUB), :]
        y = atoms[pl.ds(start + SUB, SUB), :]
        z = atoms[pl.ds(start + 2 * SUB, SUB), :]
        kind = atoms[pl.ds(start + 3 * SUB, SUB), :]
        square = x * x + y * y + z * z
        hot = [jnp.where(kind == float(t), 1.0, 0.0) for t in range(elements)]
        value = zeros
        for t in range(elements):
            value = value + hot[t] * valence[t]
        for row, item in enumerate((x, y, z, square, ones, value, zeros, zeros)):
            put(left_base, slot, row, item)
        for row, item in enumerate((-2.0 * x, -2.0 * y, -2.0 * z, ones, square, zeros, zeros, zeros)):
            put(right_base, slot, row, item)
        for row in range(SUB):
            put(onehot, slot, row, hot[row] if row < elements else zeros)
            if row < elements:
                mixed = hot[0] * rho_table[row, 0]
                for t in range(1, elements):
                    mixed = mixed + hot[t] * rho_table[row, t]
            else:
                mixed = zeros
            put(rho_rows, slot, row, mixed)
        for block in range(blocks_dev):
            coord[slot * blocks_dev + block + 1] = zeros
        return carry

    lax.fori_loop(0, slots, prepare, 0)

    lane = lax.broadcasted_iota(jnp.int32, (TILE, TILE), 1)
    sublane = lax.broadcasted_iota(jnp.int32, (TILE, TILE), 0)
    before = jnp.where(sublane < lane, 1.0, 0.0).astype(jnp.bfloat16)
    slot_col = lax.broadcasted_iota(jnp.int32, (slots, slots), 1)
    slot_row = lax.broadcasted_iota(jnp.int32, (slots, slots), 0)
    above = jnp.where(slot_col < slot_row, 1.0, 0.0).astype(jnp.bfloat16)

    def meta(row):
        return atoms[pl.ds(4 * SUB + row, slots, stride=payload), :]

    first_all = (meta(0) + 256.0 * meta(1)).astype(jnp.int32) ^ flip
    live_all = meta(4)
    firsts[...] = first_all.astype(jnp.float32)

    def rank(mark):
        count = mark.astype(jnp.bfloat16)
        inside = jnp.dot(count, before, preferred_element_type=jnp.float32)
        earlier = jnp.dot(above, count, preferred_element_type=jnp.float32)
        place = inside + jnp.sum(earlier, axis=1, keepdims=True)
        ranks[...] = jnp.where(mark > 0.0, place, -1.0)
        return jnp.sum(mark).astype(jnp.int32)

    position = sublane.astype(jnp.float32)

    def compact(chunk, columns):
        offset = (chunk * TILE).astype(jnp.float32)

        def some(group, carry):
            start = pl.multiple_of(group * SUB, SUB)
            wanted = ranks[pl.ds(start, SUB), :] - offset
            picks = [
                jnp.where(wanted[k : k + 1] == position, 1.0, 0.0).astype(jnp.bfloat16) for k in range(SUB)
            ]
            entries = [
                atoms[pl.ds(pl.multiple_of((start + k) * payload + 4 * SUB, SUB), SUB), :].astype(jnp.bfloat16)
                for k in range(SUB)
            ]
            pick = jnp.concatenate(picks, axis=1)
            entry = jnp.concatenate(entries, axis=1)
            along = lax.dot_general(
                entry, pick, (((1,), (1,)), ((), ())), preferred_element_type=jnp.float32
            )
            if not columns:
                return (carry[0] + along,)
            down = lax.dot_general(
                pick, entry, (((1,), (1,)), ((), ())), preferred_element_type=jnp.float32
            )
            return carry[0] + along, carry[1] + down

        start = (jnp.zeros((SUB, TILE), jnp.float32),)
        if columns:
            start = start + (jnp.zeros((TILE, SUB), jnp.float32),)
        got = lax.fori_loop(0, slots // SUB, some, start)
        row = got[0]
        first = (row[0:1] + 256.0 * row[1:2]).astype(jnp.int32) ^ flip
        second = (row[2:3] + 256.0 * row[3:4]).astype(jnp.int32) ^ flip
        flat[pl.ds(chunk, 1), :] = jnp.where(row[4:5] > 0.0, ((first + 1) << shift) | second, 0)
        if columns:
            col = got[1]
            second = (col[:, 2:3] + 256.0 * col[:, 3:4]).astype(jnp.int32) ^ flip
            second = jnp.where(col[:, 4:5] > 0.0, second, -1).astype(jnp.float32)
            second_cols[...] = jnp.broadcast_to(second, (TILE, TILE))

    def send(chunk, target):
        return pltpu.make_async_copy(flat.at[pl.ds(chunk, 1)], target.at[pl.ds(chunk, 1)], sem)

    own_mark = jnp.where(first_all < blocks_dev, live_all, 0.0)
    marks[...] = own_mark
    own_count = rank(own_mark)

    def own_chunk(chunk, carry):
        compact(chunk, True)
        copy = send(chunk, own_list)
        copy.start()
        part = 4 * SUB
        filled = jnp.minimum(own_count - chunk * TILE, TILE)

        def some(group, carry):
            cols = second_cols[pl.ds(pl.multiple_of(group * part, part), part), :]

            def rows(slot_group, carry):
                start = pl.multiple_of(slot_group * SUB, SUB)
                here = firsts[pl.ds(start, SUB), :]
                found = []
                for k in range(SUB):
                    hit = jnp.where(cols == here[k : k + 1], 1.0, 0.0)
                    found.append(jnp.max(hit, axis=0, keepdims=True))
                old = marks[pl.ds(start, SUB), :]
                marks[pl.ds(start, SUB), :] = jnp.maximum(old, jnp.concatenate(found, axis=0))
                return carry

            return lax.fori_loop(0, slots // SUB, rows, carry)

        lax.fori_loop(0, (filled + part - 1) // part, some, 0)
        copy.wait()
        return carry

    lax.fori_loop(0, (own_count + TILE - 1) // TILE, own_chunk, 0)

    work_count = rank(marks[...] * live_all)

    def work_chunk(chunk, carry):
        compact(chunk, False)
        copy = send(chunk, work_list)
        copy.start()
        copy.wait()
        return carry

    lax.fori_loop(0, (work_count + TILE - 1) // TILE, work_chunk, 0)

    def at(ref, block):
        return ref[pl.ds(pl.multiple_of(block * SUB, SUB), SUB), :]

    def fetch(ref, index):
        code = ref[index // TILE, index % TILE]
        place = code >> shift
        return place, jnp.maximum(place, 1) - 1, code & ((1 << shift) - 1)

    def first_pass(group, carry):
        for step in range(UNROLL):
            place, first, second = fetch(work_list, group * UNROLL + step)
            left = left_form(at(left_base, second), at(onehot, second))
            right = jnp.concatenate(
                [right_geometry(at(right_base, first)), right_table(at(rho_rows, first))], axis=1
            )
            both = cross(left, right)
            ratio = both[:, :TILE] * both[:, TILE:]
            bond = jnp.exp2(ratio * ratio * ratio)
            same = jnp.where(first == second, 1.0 / SUB, 0.0)
            coord[place] = coord[place] + (fold(bond) - same)
        return carry

    lax.fori_loop(0, (work_count + UNROLL - 1) // UNROLL, first_pass, 0)

    sub_index = lax.broadcasted_iota(jnp.int32, (SUB, TILE), 0)

    for block in range(blocks_dev):
        base = at(left_base, block)
        hot = at(onehot, block)
        load = jnp.sum(coord[block + 1], axis=0, keepdims=True) + base[5:6]
        depth_rows = zeros
        for row in range(elements):
            mixed = hot[0:1] * depth_table[row, 0]
            for t in range(1, elements):
                mixed = mixed + hot[t : t + 1] * depth_table[row, t]
            depth_rows = jnp.where(sub_index == row, mixed, depth_rows)
        load_rows = jnp.where(sub_index == 4, load, jnp.where(sub_index == 5, 1.0, 0.0))
        forms = [
            right_geometry(at(right_base, block)),
            right_table(at(rho_rows, block)),
            right_table(depth_rows),
            right_geometry(load_rows),
        ]
        for d in range(3):
            shifted = jnp.where(sub_index == d, 1.0, jnp.where(sub_index == 4, -base[d : d + 1], 0.0))
            forms.append(right_geometry(shifted))
        right_own[block] = jnp.concatenate(forms, axis=1)
    for block in range(blocks_dev + 1):
        for d in range(4):
            total[block, d] = zeros

    step_index = sublane - lane

    def second_pass(group, carry):
        for step in range(UNROLL2):
            place, first, second = fetch(own_list, group * UNROLL2 + step)
            load = jnp.sum(coord[second + 1], axis=0, keepdims=True)
            base = at(left_base, second)
            base = base + jnp.where(sub_index == 5, load, 0.0)
            left = left_form(base, at(onehot, second))
            mixed = cross(left, right_own[first])
            parts = [mixed[:, k * TILE : (k + 1) * TILE] for k in range(7)]
            dist, rho, depth, both_load = parts[:4]
            ratio = dist * rho
            squared = ratio * ratio
            bond = jnp.exp2(squared * ratio)
            bond = jnp.where(step_index == jnp.where(first == second, 0, TILE), 0.0, bond)
            weight = depth * bond / both_load
            pull = weight * squared * rho
            for d in range(3):
                total[place, d] = total[place, d] + fold(pull * parts[4 + d])
            total[place, 3] = total[place, 3] + fold(weight)
        return carry

    lax.fori_loop(0, (own_count + UNROLL2 - 1) // UNROLL2, second_pass, 0)

    for block in range(blocks_dev):
        for d in range(4):
            factor = -6.0 / LOG2E if d < 3 else -1.0
            out[d : d + 1, block * TILE : (block + 1) * TILE] = factor * jnp.sum(
                total[block + 1, d], axis=0, keepdims=True
            )


def local(order, positions, types, radius_type, valence_type, bond_depth, pair_tiles, tile_count):
    atom_dev = positions.shape[1]
    blocks_dev = atom_dev // TILE
    rows = lax.axis_size("row")
    cols = lax.axis_size("col")
    slots = rows * cols
    blocks = slots * blocks_dev
    tiles_dev = pair_tiles.shape[2]
    row_index = lax.axis_index("row")
    col_index = lax.axis_index("col")
    me = virtual(order, row_index, col_index)

    tiles = pair_tiles[0, 0]
    first = virtual(order, row_index, tiles[:, 0] // blocks_dev) * blocks_dev + tiles[:, 0] % blocks_dev
    second = virtual(order, tiles[:, 1] // blocks_dev, col_index) * blocks_dev + tiles[:, 1] % blocks_dev
    live = (jnp.arange(tiles_dev) < tile_count[0, 0]).astype(jnp.int32)
    meta = jnp.stack([first % 256, first // 256, second % 256, second // 256, live])
    meta = jnp.pad(meta, ((0, 3), (0, TILE - tiles_dev)))
    packed = jnp.concatenate(
        [
            positions.reshape(3 * blocks_dev, TILE),
            types.astype(jnp.float32).reshape(blocks_dev, TILE),
            meta.astype(jnp.float32),
        ]
    )
    gathered = packed
    for axis, bit in order:
        size = lax.axis_size(axis)
        other = lax.ppermute(gathered, axis, [(i, i ^ bit) for i in range(size)])
        gathered = jnp.concatenate([gathered, other], axis=0)

    rho = 0.5 * (radius_type[:, None] + radius_type[None, :])
    rho_table = -SCALE / (rho * rho)
    depth_table = (bond_depth * (valence_type[:, None] + valence_type[None, :])).T

    elements = radius_type.shape[0]
    shift = blocks.bit_length()
    chunks = -(-slots * tiles_dev // TILE)
    own_chunks = -(-cols * tiles_dev // TILE)
    smem = pl.BlockSpec(memory_space=pltpu.SMEM)
    vmem = pl.BlockSpec(memory_space=pltpu.VMEM)
    return pl.pallas_call(
        functools.partial(kernel, elements, shift),
        out_shape=jax.ShapeDtypeStruct((4, atom_dev), jnp.float32),
        in_specs=[smem, smem, smem, smem, vmem],
        out_specs=vmem,
        scratch_shapes=[
            pltpu.VMEM((blocks * SUB, TILE), jnp.float32),
            pltpu.VMEM((blocks * SUB, TILE), jnp.float32),
            pltpu.VMEM((blocks * SUB, TILE), jnp.float32),
            pltpu.VMEM((blocks * SUB, TILE), jnp.float32),
            pltpu.VMEM((blocks + 1, SUB, TILE), jnp.float32),
            pltpu.VMEM((blocks_dev, 10 * SUB, 7 * TILE), jnp.bfloat16),
            pltpu.VMEM((blocks_dev + 1, 4, SUB, TILE), jnp.float32),
            pltpu.VMEM((slots, TILE), jnp.float32),
            pltpu.VMEM((slots, TILE), jnp.float32),
            pltpu.VMEM((slots, TILE), jnp.float32),
            pltpu.VMEM((TILE, TILE), jnp.float32),
            pltpu.VMEM((chunks, TILE), jnp.int32),
            pltpu.SMEM((own_chunks, TILE), jnp.int32),
            pltpu.SMEM((chunks, TILE), jnp.int32),
            pltpu.SemaphoreType.DMA,
        ],
        compiler_params=pltpu.CompilerParams(vmem_limit_bytes=56 * 1024 * 1024),
    )((me * blocks_dev)[None].astype(jnp.int32), rho_table, depth_table, valence_type, gathered)


def solution(mesh):
    order = stage_bits(mesh.shape["col"], mesh.shape["row"])
    in_specs = (
        P(None, ("row", "col")),
        P(("row", "col")),
        P(),
        P(),
        P(),
        P("row", "col", None, None),
        P("row", "col"),
    )
    out_specs = P(None, ("row", "col"))
    return jax.shard_map(
        functools.partial(local, order), mesh=mesh, in_specs=in_specs, out_specs=out_specs, check_vma=False
    )
```

```python
import functools
import math

import jax
import jax.numpy as jnp
from jax import lax
from jax.experimental import pallas as pl
from jax.experimental.pallas import tpu as pltpu
from jax.sharding import PartitionSpec as P

TILE = 128
SUB = 8
UNROLL = 16
UNROLL2 = 8
LOG2E = math.log2(math.e)
SCALE = LOG2E ** (1.0 / 3.0)


def stage_bits(col_size, row_size):
    order = []
    bit = col_size // 2
    while bit >= 2:
        order.append(("col", bit))
        bit //= 2
    bit = row_size // 2
    while bit >= 1:
        order.append(("row", bit))
        bit //= 2
    if col_size > 1:
        order.append(("col", 1))
    return order


def virtual(order, row, col):
    total = 0 * row
    for place, (axis, bit) in enumerate(order):
        index = row if axis == "row" else col
        total = total + ((index // bit) % 2) * (1 << place)
    return total


def pieces(value):
    high = value.astype(jnp.bfloat16).astype(jnp.float32)
    rest = value - high
    mid = rest.astype(jnp.bfloat16).astype(jnp.float32)
    return high, mid, rest - mid


def left_form(base, onehot):
    high, mid, low = pieces(base)
    zero = jnp.zeros_like(base)
    stack = jnp.concatenate([high, high, mid, high, low, mid, onehot, onehot, onehot, zero], axis=0)
    return stack.astype(jnp.bfloat16)


def right_geometry(base):
    high, mid, low = pieces(base)
    zero = jnp.zeros_like(base)
    stack = jnp.concatenate([high, mid, high, low, high, mid, zero, zero, zero, zero], axis=0)
    return stack.astype(jnp.bfloat16)


def right_table(rows):
    high, mid, low = pieces(rows)
    zero = jnp.zeros_like(rows)
    stack = jnp.concatenate([zero] * 6 + [high, mid, low, zero], axis=0)
    return stack.astype(jnp.bfloat16)


def cross(left, right):
    return lax.dot_general(left, right, (((0,), (0,)), ((), ())), preferred_element_type=jnp.float32)


def fold(value):
    return jnp.sum(value.reshape(TILE // SUB, SUB, TILE), axis=0)


def kernel(
    elements,
    shift,
    flip_ref,
    rho_table,
    depth_table,
    valence,
    atoms,
    out,
    left_base,
    right_base,
    onehot,
    rho_rows,
    coord,
    right_own,
    total,
    ranks,
    marks,
    firsts,
    second_cols,
    own_flat,
    work_flat,
    own_list,
    work_list,
    own_sem,
    work_sem,
):
    payload = 5 * SUB
    slots = atoms.shape[0] // payload
    blocks_dev = SUB
    blocks = slots * blocks_dev
    flip = flip_ref[0]
    ones = jnp.ones((SUB, TILE), jnp.float32)
    zeros = jnp.zeros((SUB, TILE), jnp.float32)

    def put(ref, slot, row, value):
        ref[pl.ds((slot * blocks_dev + 1) * SUB + row, blocks_dev, stride=SUB), :] = value

    def prepare(slot, carry):
        start = pl.multiple_of(slot * payload, SUB)
        x = atoms[pl.ds(start, SUB), :]
        y = atoms[pl.ds(start + SUB, SUB), :]
        z = atoms[pl.ds(start + 2 * SUB, SUB), :]
        kind = atoms[pl.ds(start + 3 * SUB, SUB), :]
        square = x * x + y * y + z * z
        hot = [jnp.where(kind == float(t), 1.0, 0.0) for t in range(elements)]
        value = zeros
        for t in range(elements):
            value = value + hot[t] * valence[t]
        for row, item in enumerate((x, y, z, square, ones, value, zeros, zeros)):
            put(left_base, slot, row, item)
        for row, item in enumerate((-2.0 * x, -2.0 * y, -2.0 * z, ones, square, zeros, zeros, zeros)):
            put(right_base, slot, row, item)
        for row in range(SUB):
            put(onehot, slot, row, hot[row] if row < elements else zeros)
            if row < elements:
                mixed = hot[0] * rho_table[row, 0]
                for t in range(1, elements):
                    mixed = mixed + hot[t] * rho_table[row, t]
            else:
                mixed = zeros
            put(rho_rows, slot, row, mixed)
        for block in range(blocks_dev):
            coord[slot * blocks_dev + block + 1] = zeros
        return carry

    lax.fori_loop(0, slots, prepare, 0)
    for ref in (left_base, right_base, onehot, rho_rows):
        ref[0:SUB, :] = zeros

    lane = lax.broadcasted_iota(jnp.int32, (TILE, TILE), 1)
    sublane = lax.broadcasted_iota(jnp.int32, (TILE, TILE), 0)
    before = jnp.where(sublane < lane, 1.0, 0.0).astype(jnp.bfloat16)
    slot_col = lax.broadcasted_iota(jnp.int32, (slots, slots), 1)
    slot_row = lax.broadcasted_iota(jnp.int32, (slots, slots), 0)
    above = jnp.where(slot_col < slot_row, 1.0, 0.0).astype(jnp.bfloat16)

    def meta(row):
        return atoms[pl.ds(4 * SUB + row, slots, stride=payload), :]

    first_all = (meta(0) + 256.0 * meta(1)).astype(jnp.int32) ^ flip
    live_all = meta(4)
    firsts[...] = first_all.astype(jnp.float32)

    def rank(mark):
        count = mark.astype(jnp.bfloat16)
        inside = jnp.dot(count, before, preferred_element_type=jnp.float32)
        earlier = jnp.dot(above, count, preferred_element_type=jnp.float32)
        place = inside + jnp.sum(earlier, axis=1, keepdims=True)
        ranks[...] = jnp.where(mark > 0.0, place, -1.0)
        return jnp.sum(mark).astype(jnp.int32)

    position = sublane.astype(jnp.float32)

    def compact(chunk, flat, columns):
        offset = (chunk * TILE).astype(jnp.float32)

        def some(group, carry):
            start = pl.multiple_of(group * SUB, SUB)
            wanted = ranks[pl.ds(start, SUB), :] - offset
            picks = [
                jnp.where(wanted[k : k + 1] == position, 1.0, 0.0).astype(jnp.bfloat16) for k in range(SUB)
            ]
            entries = [
                atoms[pl.ds(pl.multiple_of((start + k) * payload + 4 * SUB, SUB), SUB), :].astype(jnp.bfloat16)
                for k in range(SUB)
            ]
            pick = jnp.concatenate(picks, axis=1)
            entry = jnp.concatenate(entries, axis=1)
            along = lax.dot_general(
                entry, pick, (((1,), (1,)), ((), ())), preferred_element_type=jnp.float32
            )
            return carry + along

        row = lax.fori_loop(0, slots // SUB, some, zeros)
        first = (row[0:1] + 256.0 * row[1:2]).astype(jnp.int32) ^ flip
        second = (row[2:3] + 256.0 * row[3:4]).astype(jnp.int32) ^ flip
        valid = row[4:5] > 0.0
        flat[pl.ds(chunk, 1), :] = jnp.where(valid, ((first + 1) << shift) | (second + 1), 0)
        if columns:
            target = jnp.where(valid, second, -1).astype(jnp.float32)
            column = jnp.transpose(jnp.broadcast_to(target, (SUB, TILE)))[:, 0:1]
            second_cols[...] = jnp.broadcast_to(column, (TILE, TILE))

    def send(source, target, group, semaphore):
        start = pl.multiple_of(group * SUB, SUB)
        return pltpu.make_async_copy(source.at[pl.ds(start, SUB)], target.at[pl.ds(start, SUB)], semaphore)

    def send_rest(source, target, count, semaphore):
        def one(group, carry):
            copy = send(source, target, group, semaphore)
            copy.start()
            copy.wait()
            return carry

        lax.fori_loop(1, (count + SUB * TILE - 1) // (SUB * TILE), one, 0)

    own_mark = jnp.where(first_all < blocks_dev, live_all, 0.0)
    marks[...] = own_mark
    own_count = rank(own_mark)

    def own_chunk(chunk, carry):
        compact(chunk, own_flat, True)
        part = 4 * SUB
        filled = jnp.minimum(own_count - chunk * TILE, TILE)

        def some(group, carry):
            cols = second_cols[pl.ds(pl.multiple_of(group * part, part), part), :]

            def rows(slot_group, carry):
                start = pl.multiple_of(slot_group * SUB, SUB)
                here = firsts[pl.ds(start, SUB), :]
                found = []
                for k in range(SUB):
                    hit = jnp.where(cols == here[k : k + 1], 1.0, 0.0)
                    found.append(jnp.max(hit, axis=0, keepdims=True))
                old = marks[pl.ds(start, SUB), :]
                marks[pl.ds(start, SUB), :] = jnp.maximum(old, jnp.concatenate(found, axis=0))
                return carry

            return lax.fori_loop(0, slots // SUB, rows, carry)

        lax.fori_loop(0, (filled + part - 1) // part, some, 0)
        return carry

    lax.fori_loop(0, (own_count + TILE - 1) // TILE, own_chunk, 0)
    send_rest(own_flat, own_list, own_count, own_sem)
    own_copy = send(own_flat, own_list, 0, own_sem)
    own_copy.start()

    work_count = rank(marks[...] * live_all)

    def work_chunk(chunk, carry):
        compact(chunk, work_flat, False)
        return carry

    lax.fori_loop(0, (work_count + TILE - 1) // TILE, work_chunk, 0)
    send_rest(work_flat, work_list, work_count, work_sem)
    work_copy = send(work_flat, work_list, 0, work_sem)
    work_copy.start()
    work_copy.wait()
    own_copy.wait()

    def at(ref, block):
        return ref[pl.ds(pl.multiple_of(block * SUB, SUB), SUB), :]

    def fetch(ref, group, size, step):
        per_row = TILE // size
        code = ref[lax.div(group, per_row), lax.rem(group, per_row) * size + step]
        return code >> shift, code & ((1 << shift) - 1)

    def first_pass(group, carry):
        for step in range(UNROLL):
            first, second = fetch(work_list, group, UNROLL, step)
            left = left_form(at(left_base, second), at(onehot, second))
            right = jnp.concatenate(
                [right_geometry(at(right_base, first)), right_table(at(rho_rows, first))], axis=1
            )
            both = cross(left, right)
            ratio = both[:, :TILE] * both[:, TILE:]
            bond = jnp.exp2(ratio * ratio * ratio)
            same = jnp.where(first == second, 1.0 / SUB, 0.0)
            coord[first] = coord[first] + (fold(bond) - same)
        return carry

    lax.fori_loop(0, (work_count + UNROLL - 1) // UNROLL, first_pass, 0)

    sub_index = lax.broadcasted_iota(jnp.int32, (SUB, TILE), 0)

    for block in range(blocks_dev):
        base = at(left_base, block + 1)
        hot = at(onehot, block + 1)
        load = jnp.sum(coord[block + 1], axis=0, keepdims=True) + base[5:6]
        depth_rows = zeros
        for row in range(elements):
            mixed = hot[0:1] * depth_table[row, 0]
            for t in range(1, elements):
                mixed = mixed + hot[t : t + 1] * depth_table[row, t]
            depth_rows = jnp.where(sub_index == row, mixed, depth_rows)
        load_rows = jnp.where(sub_index == 4, load, jnp.where(sub_index == 5, 1.0, 0.0))
        forms = [
            right_geometry(at(right_base, block + 1)),
            right_table(at(rho_rows, block + 1)),
            right_table(depth_rows),
            right_geometry(load_rows),
        ]
        for d in range(3):
            shifted = jnp.where(sub_index == d, 1.0, jnp.where(sub_index == 4, -base[d : d + 1], 0.0))
            forms.append(right_geometry(shifted))
        right_own[block + 1] = jnp.concatenate(forms, axis=1)
    right_own[0] = jnp.zeros(right_own.shape[1:], jnp.bfloat16)
    for block in range(blocks_dev + 1):
        for d in range(4):
            total[block, d] = zeros

    step_index = sublane - lane

    def second_pass(group, carry):
        for step in range(UNROLL2):
            first, second = fetch(own_list, group, UNROLL2, step)
            load = jnp.sum(coord[second], axis=0, keepdims=True)
            base = at(left_base, second)
            base = base + jnp.where(sub_index == 5, load, 0.0)
            left = left_form(base, at(onehot, second))
            mixed = cross(left, right_own[first])
            parts = [mixed[:, k * TILE : (k + 1) * TILE] for k in range(7)]
            dist, rho, depth, both_load = parts[:4]
            ratio = dist * rho
            squared = ratio * ratio
            bond = jnp.exp2(squared * ratio)
            bond = jnp.where(step_index == jnp.where(first == second, 0, TILE), 0.0, bond)
            weight = depth * bond / both_load
            pull = weight * squared * rho
            for d in range(3):
                total[first, d] = total[first, d] + fold(pull * parts[4 + d])
            total[first, 3] = total[first, 3] + fold(weight)
        return carry

    lax.fori_loop(0, (own_count + UNROLL2 - 1) // UNROLL2, second_pass, 0)

    for block in range(blocks_dev):
        for d in range(4):
            factor = -6.0 / LOG2E if d < 3 else -1.0
            out[d : d + 1, block * TILE : (block + 1) * TILE] = factor * jnp.sum(
                total[block + 1, d], axis=0, keepdims=True
            )


def local(order, positions, types, radius_type, valence_type, bond_depth, pair_tiles, tile_count):
    atom_dev = positions.shape[1]
    blocks_dev = atom_dev // TILE
    rows = lax.axis_size("row")
    cols = lax.axis_size("col")
    slots = rows * cols
    blocks = slots * blocks_dev
    tiles_dev = pair_tiles.shape[2]
    row_index = lax.axis_index("row")
    col_index = lax.axis_index("col")
    me = virtual(order, row_index, col_index)

    tiles = pair_tiles[0, 0]
    first = virtual(order, row_index, tiles[:, 0] // blocks_dev) * blocks_dev + tiles[:, 0] % blocks_dev
    second = virtual(order, tiles[:, 1] // blocks_dev, col_index) * blocks_dev + tiles[:, 1] % blocks_dev
    live = (jnp.arange(tiles_dev) < tile_count[0, 0]).astype(jnp.int32)
    meta = jnp.stack([first % 256, first // 256, second % 256, second // 256, live])
    meta = jnp.pad(meta, ((0, 3), (0, TILE - tiles_dev)))
    packed = jnp.concatenate(
        [
            positions.reshape(3 * blocks_dev, TILE),
            types.astype(jnp.float32).reshape(blocks_dev, TILE),
            meta.astype(jnp.float32),
        ]
    )
    gathered = packed
    for axis, bit in order:
        size = lax.axis_size(axis)
        other = lax.ppermute(gathered, axis, [(i, i ^ bit) for i in range(size)])
        gathered = jnp.concatenate([gathered, other], axis=0)

    rho = 0.5 * (radius_type[:, None] + radius_type[None, :])
    rho_table = -SCALE / (rho * rho)
    depth_table = (bond_depth * (valence_type[:, None] + valence_type[None, :])).T

    elements = radius_type.shape[0]
    shift = (blocks + 1).bit_length()
    chunks = -(-slots * tiles_dev // (SUB * TILE)) * SUB
    own_chunks = -(-cols * tiles_dev // (SUB * TILE)) * SUB
    smem = pl.BlockSpec(memory_space=pltpu.SMEM)
    vmem = pl.BlockSpec(memory_space=pltpu.VMEM)
    return pl.pallas_call(
        functools.partial(kernel, elements, shift),
        out_shape=jax.ShapeDtypeStruct((4, atom_dev), jnp.float32),
        in_specs=[smem, smem, smem, smem, vmem],
        out_specs=vmem,
        scratch_shapes=[
            pltpu.VMEM((blocks * SUB + SUB, TILE), jnp.float32),
            pltpu.VMEM((blocks * SUB + SUB, TILE), jnp.float32),
            pltpu.VMEM((blocks * SUB + SUB, TILE), jnp.float32),
            pltpu.VMEM((blocks * SUB + SUB, TILE), jnp.float32),
            pltpu.VMEM((blocks + 1, SUB, TILE), jnp.float32),
            pltpu.VMEM((blocks_dev + 1, 10 * SUB, 7 * TILE), jnp.bfloat16),
            pltpu.VMEM((blocks_dev + 1, 4, SUB, TILE), jnp.float32),
            pltpu.VMEM((slots, TILE), jnp.float32),
            pltpu.VMEM((slots, TILE), jnp.float32),
            pltpu.VMEM((slots, TILE), jnp.float32),
            pltpu.VMEM((TILE, TILE), jnp.float32),
            pltpu.VMEM((own_chunks, TILE), jnp.int32),
            pltpu.VMEM((chunks, TILE), jnp.int32),
            pltpu.SMEM((own_chunks, TILE), jnp.int32),
            pltpu.SMEM((chunks, TILE), jnp.int32),
            pltpu.SemaphoreType.DMA,
            pltpu.SemaphoreType.DMA,
        ],
        compiler_params=pltpu.CompilerParams(vmem_limit_bytes=56 * 1024 * 1024),
    )((me * blocks_dev)[None].astype(jnp.int32), rho_table, depth_table, valence_type, gathered)


def solution(mesh):
    order = stage_bits(mesh.shape["col"], mesh.shape["row"])
    in_specs = (
        P(None, ("row", "col")),
        P(("row", "col")),
        P(),
        P(),
        P(),
        P("row", "col", None, None),
        P("row", "col"),
    )
    out_specs = P(None, ("row", "col"))
    return jax.shard_map(
        functools.partial(local, order), mesh=mesh, in_specs=in_specs, out_specs=out_specs, check_vma=False
    )
```

```python
import functools
import math

import jax
import jax.numpy as jnp
from jax import lax
from jax.experimental import pallas as pl
from jax.experimental.pallas import tpu as pltpu
from jax.sharding import PartitionSpec as P

TILE = 128
SUB = 8
LARGE = 32
SMALL = 8
LOG2E = math.log2(math.e)
SCALE = LOG2E ** (1.0 / 3.0)


def stage_bits(col_size, row_size):
    order = []
    bit = col_size // 2
    while bit >= 2:
        order.append(("col", bit))
        bit //= 2
    bit = row_size // 2
    while bit >= 1:
        order.append(("row", bit))
        bit //= 2
    if col_size > 1:
        order.append(("col", 1))
    return order


def virtual(order, row, col):
    total = 0 * row
    for place, (axis, bit) in enumerate(order):
        index = row if axis == "row" else col
        total = total + ((index // bit) % 2) * (1 << place)
    return total


def pieces(value):
    high = value.astype(jnp.bfloat16).astype(jnp.float32)
    rest = value - high
    mid = rest.astype(jnp.bfloat16).astype(jnp.float32)
    return high, mid, rest - mid


def left_form(base, onehot):
    high, mid, low = pieces(base)
    zero = jnp.zeros_like(base)
    stack = jnp.concatenate([high, high, mid, high, low, mid, onehot, onehot, onehot, zero], axis=0)
    return stack.astype(jnp.bfloat16)


def right_geometry(base):
    high, mid, low = pieces(base)
    zero = jnp.zeros_like(base)
    stack = jnp.concatenate([high, mid, high, low, high, mid, zero, zero, zero, zero], axis=0)
    return stack.astype(jnp.bfloat16)


def right_table(rows):
    high, mid, low = pieces(rows)
    zero = jnp.zeros_like(rows)
    stack = jnp.concatenate([zero] * 6 + [high, mid, low, zero], axis=0)
    return stack.astype(jnp.bfloat16)


def force_form(base, sub_index):
    high, mid, low = pieces(base)
    rest = jnp.where(sub_index < 3, mid, jnp.where(sub_index < 6, jnp.roll(low, 3, axis=0), 0.0))
    return jnp.concatenate([high, rest], axis=0).astype(jnp.bfloat16)


def cross(left, right):
    return lax.dot_general(left, right, (((0,), (0,)), ((), ())), preferred_element_type=jnp.float32)


def fold(value):
    return jnp.sum(value.reshape(TILE // SUB, SUB, TILE), axis=0)


def kernel(
    elements,
    shift,
    flip_ref,
    rho_table,
    depth_table,
    valence,
    atoms,
    out,
    left_base,
    right_base,
    onehot,
    rho_rows,
    coord,
    right_own,
    self_weight,
    total,
    energy,
    pulls,
    ranks,
    marks,
    firsts,
    second_cols,
    own_flat,
    work_flat,
    own_list,
    work_list,
    own_sem,
    work_sem,
):
    payload = 5 * SUB
    slots = atoms.shape[0] // payload
    blocks_dev = SUB
    blocks = slots * blocks_dev
    flip = flip_ref[0]
    ones = jnp.ones((SUB, TILE), jnp.float32)
    zeros = jnp.zeros((SUB, TILE), jnp.float32)

    def put(ref, slot, row, value):
        ref[pl.ds((slot * blocks_dev + 1) * SUB + row, blocks_dev, stride=SUB), :] = value

    def prepare(slot, carry):
        start = pl.multiple_of(slot * payload, SUB)
        x = atoms[pl.ds(start, SUB), :]
        y = atoms[pl.ds(start + SUB, SUB), :]
        z = atoms[pl.ds(start + 2 * SUB, SUB), :]
        kind = atoms[pl.ds(start + 3 * SUB, SUB), :]
        square = x * x + y * y + z * z
        hot = [jnp.where(kind == float(t), 1.0, 0.0) for t in range(elements)]
        value = zeros
        for t in range(elements):
            value = value + hot[t] * valence[t]
        for row, item in enumerate((x, y, z, square, ones, value, zeros, zeros)):
            put(left_base, slot, row, item)
        for row, item in enumerate((-2.0 * x, -2.0 * y, -2.0 * z, ones, square, zeros, zeros, zeros)):
            put(right_base, slot, row, item)
        for row in range(SUB):
            put(onehot, slot, row, hot[row] if row < elements else zeros)
            if row < elements:
                mixed = hot[0] * rho_table[row, 0]
                for t in range(1, elements):
                    mixed = mixed + hot[t] * rho_table[row, t]
            else:
                mixed = zeros
            put(rho_rows, slot, row, mixed)
        for block in range(blocks_dev):
            coord[slot * blocks_dev + block + 1] = zeros
        return carry

    lax.fori_loop(0, slots, prepare, 0)
    for ref in (left_base, right_base, onehot, rho_rows):
        ref[0:SUB, :] = zeros

    lane = lax.broadcasted_iota(jnp.int32, (TILE, TILE), 1)
    sublane = lax.broadcasted_iota(jnp.int32, (TILE, TILE), 0)
    before = jnp.where(sublane < lane, 1.0, 0.0).astype(jnp.bfloat16)
    slot_col = lax.broadcasted_iota(jnp.int32, (slots, slots), 1)
    slot_row = lax.broadcasted_iota(jnp.int32, (slots, slots), 0)
    above = jnp.where(slot_col < slot_row, 1.0, 0.0).astype(jnp.bfloat16)

    def meta(row):
        return atoms[pl.ds(4 * SUB + row, slots, stride=payload), :]

    first_all = (meta(0) + 256.0 * meta(1)).astype(jnp.int32) ^ flip
    live_all = meta(4)
    firsts[...] = first_all.astype(jnp.float32)

    def rank(mark):
        count = mark.astype(jnp.bfloat16)
        inside = jnp.dot(count, before, preferred_element_type=jnp.float32)
        earlier = jnp.dot(above, count, preferred_element_type=jnp.float32)
        place = inside + jnp.sum(earlier, axis=1, keepdims=True)
        ranks[...] = jnp.where(mark > 0.0, place, -1.0)
        return jnp.sum(mark).astype(jnp.int32)

    position = sublane.astype(jnp.float32)

    def compact(chunk, flat, columns):
        offset = (chunk * TILE).astype(jnp.float32)

        def some(group, carry):
            start = pl.multiple_of(group * SUB, SUB)
            wanted = ranks[pl.ds(start, SUB), :] - offset
            picks = [
                jnp.where(wanted[k : k + 1] == position, 1.0, 0.0).astype(jnp.bfloat16) for k in range(SUB)
            ]
            entries = [
                atoms[pl.ds(pl.multiple_of((start + k) * payload + 4 * SUB, SUB), SUB), :].astype(jnp.bfloat16)
                for k in range(SUB)
            ]
            pick = jnp.concatenate(picks, axis=1)
            entry = jnp.concatenate(entries, axis=1)
            along = lax.dot_general(
                entry, pick, (((1,), (1,)), ((), ())), preferred_element_type=jnp.float32
            )
            return carry + along

        row = lax.fori_loop(0, slots // SUB, some, zeros)
        first = (row[0:1] + 256.0 * row[1:2]).astype(jnp.int32) ^ flip
        second = (row[2:3] + 256.0 * row[3:4]).astype(jnp.int32) ^ flip
        valid = row[4:5] > 0.0
        flat[pl.ds(chunk, 1), :] = jnp.where(valid, ((first + 1) << shift) | (second + 1), 0)
        if columns:
            target = jnp.where(valid, second, -1).astype(jnp.float32)
            column = jnp.transpose(jnp.broadcast_to(target, (SUB, TILE)))[:, 0:1]
            second_cols[...] = jnp.broadcast_to(column, (TILE, TILE))

    def send(source, target, group, semaphore):
        start = pl.multiple_of(group * SUB, SUB)
        return pltpu.make_async_copy(source.at[pl.ds(start, SUB)], target.at[pl.ds(start, SUB)], semaphore)

    def send_rest(source, target, count, semaphore):
        def one(group, carry):
            copy = send(source, target, group, semaphore)
            copy.start()
            copy.wait()
            return carry

        lax.fori_loop(1, (count + SUB * TILE - 1) // (SUB * TILE), one, 0)

    own_mark = jnp.where(first_all < blocks_dev, live_all, 0.0)
    marks[...] = own_mark
    own_count = rank(own_mark)

    def own_chunk(chunk, carry):
        compact(chunk, own_flat, True)
        part = 4 * SUB
        filled = jnp.minimum(own_count - chunk * TILE, TILE)

        def some(group, carry):
            cols = second_cols[pl.ds(pl.multiple_of(group * part, part), part), :]

            def rows(slot_group, carry):
                start = pl.multiple_of(slot_group * SUB, SUB)
                here = firsts[pl.ds(start, SUB), :]
                found = []
                for k in range(SUB):
                    hit = jnp.where(cols == here[k : k + 1], 1.0, 0.0)
                    found.append(jnp.max(hit, axis=0, keepdims=True))
                old = marks[pl.ds(start, SUB), :]
                marks[pl.ds(start, SUB), :] = jnp.maximum(old, jnp.concatenate(found, axis=0))
                return carry

            return lax.fori_loop(0, slots // SUB, rows, carry)

        lax.fori_loop(0, (filled + part - 1) // part, some, 0)
        return carry

    lax.fori_loop(0, (own_count + TILE - 1) // TILE, own_chunk, 0)
    send_rest(own_flat, own_list, own_count, own_sem)
    own_copy = send(own_flat, own_list, 0, own_sem)
    own_copy.start()

    work_count = rank(marks[...] * live_all)

    def work_chunk(chunk, carry):
        compact(chunk, work_flat, False)
        return carry

    lax.fori_loop(0, (work_count + TILE - 1) // TILE, work_chunk, 0)
    send_rest(work_flat, work_list, work_count, work_sem)
    work_copy = send(work_flat, work_list, 0, work_sem)
    work_copy.start()
    work_copy.wait()
    own_copy.wait()

    def at(ref, block):
        return ref[pl.ds(pl.multiple_of(block * SUB, SUB), SUB), :]

    def fetch(ref, start):
        row = lax.shift_right_logical(start, TILE.bit_length() - 1)
        column = start & (TILE - 1)

        def at_step(step):
            code = ref[row, column + step]
            return code >> shift, code & ((1 << shift) - 1)

        return at_step

    def first_pass(start, size):
        pair = fetch(work_list, start)
        for step in range(size):
            first, second = pair(step)
            left = left_form(at(left_base, second), at(onehot, second))
            right = jnp.concatenate(
                [right_geometry(at(right_base, first)), right_table(at(rho_rows, first))], axis=1
            )
            both = cross(left, right)
            ratio = both[:, :TILE] * both[:, TILE:]
            bond = jnp.exp2(ratio * ratio * ratio)
            same = jnp.where(first == second, 1.0 / SUB, 0.0)
            coord[first] = coord[first] + (fold(bond) - same)

    def large(group, carry):
        first_pass(group * LARGE, LARGE)
        return carry

    def small(group, carry):
        first_pass(group * SMALL, SMALL)
        return carry

    fulls = work_count // LARGE
    lax.fori_loop(0, fulls, large, 0)
    lax.fori_loop(fulls * (LARGE // SMALL), (work_count + SMALL - 1) // SMALL, small, 0)

    sub_index = lax.broadcasted_iota(jnp.int32, (SUB, TILE), 0)

    for block in range(blocks_dev):
        base = at(left_base, block + 1)
        hot = at(onehot, block + 1)
        load = jnp.sum(coord[block + 1], axis=0, keepdims=True) + base[5:6]
        depth_rows = zeros
        for row in range(elements):
            mixed = hot[0:1] * depth_table[row, 0]
            for t in range(1, elements):
                mixed = mixed + hot[t : t + 1] * depth_table[row, t]
            depth_rows = jnp.where(sub_index == row, mixed, depth_rows)
        load_rows = jnp.where(sub_index == 4, load, jnp.where(sub_index == 5, 1.0, 0.0))
        forms = [
            right_geometry(at(right_base, block + 1)),
            right_table(at(rho_rows, block + 1)),
            right_table(depth_rows),
            right_geometry(load_rows),
        ]
        alone = hot[0:1] * depth_table[0, 0]
        for t in range(1, elements):
            alone = alone + hot[t : t + 1] * depth_table[t, t]
        self_weight[block + 1] = jnp.where(sub_index == 0, alone / (load + load), 0.0)
        right_own[block + 1] = jnp.concatenate(forms, axis=1)
    self_weight[0] = zeros
    right_own[0] = jnp.zeros(right_own.shape[1:], jnp.bfloat16)
    for block in range(blocks_dev + 1):
        total[block] = jnp.zeros(total.shape[1:], jnp.float32)
        energy[block] = zeros

    def second_pass(start, size):
        pair = fetch(own_list, start)
        for step in range(size):
            first, second = pair(step)
            load = jnp.sum(coord[second], axis=0, keepdims=True)
            base = at(left_base, second)
            base = base + jnp.where(sub_index == 5, load, 0.0)
            left = left_form(base, at(onehot, second))
            mixed = cross(left, right_own[first])
            dist, rho, depth, both_load = [mixed[:, k * TILE : (k + 1) * TILE] for k in range(4)]
            ratio = dist * rho
            squared = ratio * ratio
            bond = jnp.exp2(squared * ratio)
            weight = depth * bond / both_load
            pull = weight * squared * rho
            pull_high = pull.astype(jnp.bfloat16)
            pulls[step, :, 0:TILE] = pull_high
            pulls[step, :, TILE:] = (pull - pull_high.astype(jnp.float32)).astype(jnp.bfloat16)
            same = jnp.where(first == second, 1.0, 0.0)
            energy[first] = energy[first] + (fold(weight) - same * self_weight[first])
        for step in range(size):
            first, second = pair(step)
            form = force_form(at(left_base, second), sub_index)
            total[first] = total[first] + jnp.dot(form, pulls[step], preferred_element_type=jnp.float32)

    def second_group(group, carry):
        second_pass(group * SMALL, SMALL)
        return carry

    lax.fori_loop(0, (own_count + SMALL - 1) // SMALL, second_group, 0)

    for block in range(blocks_dev):
        both = total[block + 1]
        sums = both[:, :TILE] + both[:, TILE:]
        here = at(left_base, block + 1)
        lanes = slice(block * TILE, (block + 1) * TILE)
        for d in range(3):
            moment = sums[d : d + 1] + sums[8 + d : 9 + d] + sums[11 + d : 12 + d]
            out[d : d + 1, lanes] = (-6.0 / LOG2E) * (moment - here[d : d + 1] * sums[4:5])
        out[3:4, lanes] = -jnp.sum(energy[block + 1], axis=0, keepdims=True)


def local(order, positions, types, radius_type, valence_type, bond_depth, pair_tiles, tile_count):
    atom_dev = positions.shape[1]
    blocks_dev = atom_dev // TILE
    rows = lax.axis_size("row")
    cols = lax.axis_size("col")
    slots = rows * cols
    blocks = slots * blocks_dev
    tiles_dev = pair_tiles.shape[2]
    row_index = lax.axis_index("row")
    col_index = lax.axis_index("col")
    me = virtual(order, row_index, col_index)

    tiles = pair_tiles[0, 0]
    first = virtual(order, row_index, tiles[:, 0] // blocks_dev) * blocks_dev + tiles[:, 0] % blocks_dev
    second = virtual(order, tiles[:, 1] // blocks_dev, col_index) * blocks_dev + tiles[:, 1] % blocks_dev
    live = (jnp.arange(tiles_dev) < tile_count[0, 0]).astype(jnp.int32)
    meta = jnp.stack([first % 256, first // 256, second % 256, second // 256, live])
    meta = jnp.pad(meta, ((0, 3), (0, TILE - tiles_dev)))
    packed = jnp.concatenate(
        [
            positions.reshape(3 * blocks_dev, TILE),
            types.astype(jnp.float32).reshape(blocks_dev, TILE),
            meta.astype(jnp.float32),
        ]
    )
    gathered = packed
    for axis, bit in order:
        size = lax.axis_size(axis)
        other = lax.ppermute(gathered, axis, [(i, i ^ bit) for i in range(size)])
        gathered = jnp.concatenate([gathered, other], axis=0)

    rho = 0.5 * (radius_type[:, None] + radius_type[None, :])
    rho_table = -SCALE / (rho * rho)
    depth_table = (bond_depth * (valence_type[:, None] + valence_type[None, :])).T

    elements = radius_type.shape[0]
    shift = (blocks + 1).bit_length()
    chunks = -(-slots * tiles_dev // (SUB * TILE)) * SUB
    own_chunks = -(-cols * tiles_dev // (SUB * TILE)) * SUB
    smem = pl.BlockSpec(memory_space=pltpu.SMEM)
    vmem = pl.BlockSpec(memory_space=pltpu.VMEM)
    return pl.pallas_call(
        functools.partial(kernel, elements, shift),
        out_shape=jax.ShapeDtypeStruct((4, atom_dev), jnp.float32),
        in_specs=[smem, smem, smem, smem, vmem],
        out_specs=vmem,
        scratch_shapes=[
            pltpu.VMEM((blocks * SUB + SUB, TILE), jnp.float32),
            pltpu.VMEM((blocks * SUB + SUB, TILE), jnp.float32),
            pltpu.VMEM((blocks * SUB + SUB, TILE), jnp.float32),
            pltpu.VMEM((blocks * SUB + SUB, TILE), jnp.float32),
            pltpu.VMEM((blocks + 1, SUB, TILE), jnp.float32),
            pltpu.VMEM((blocks_dev + 1, 10 * SUB, 4 * TILE), jnp.bfloat16),
            pltpu.VMEM((blocks_dev + 1, SUB, TILE), jnp.float32),
            pltpu.VMEM((blocks_dev + 1, 2 * SUB, 2 * TILE), jnp.float32),
            pltpu.VMEM((blocks_dev + 1, SUB, TILE), jnp.float32),
            pltpu.VMEM((SMALL, TILE, 2 * TILE), jnp.bfloat16),
            pltpu.VMEM((slots, TILE), jnp.float32),
            pltpu.VMEM((slots, TILE), jnp.float32),
            pltpu.VMEM((slots, TILE), jnp.float32),
            pltpu.VMEM((TILE, TILE), jnp.float32),
            pltpu.VMEM((own_chunks, TILE), jnp.int32),
            pltpu.VMEM((chunks, TILE), jnp.int32),
            pltpu.SMEM((own_chunks, TILE), jnp.int32),
            pltpu.SMEM((chunks, TILE), jnp.int32),
            pltpu.SemaphoreType.DMA,
            pltpu.SemaphoreType.DMA,
        ],
        compiler_params=pltpu.CompilerParams(vmem_limit_bytes=56 * 1024 * 1024),
    )((me * blocks_dev)[None].astype(jnp.int32), rho_table, depth_table, valence_type, gathered)


def solution(mesh):
    order = stage_bits(mesh.shape["col"], mesh.shape["row"])
    in_specs = (
        P(None, ("row", "col")),
        P(("row", "col")),
        P(),
        P(),
        P(),
        P("row", "col", None, None),
        P("row", "col"),
    )
    out_specs = P(None, ("row", "col"))
    return jax.shard_map(
        functools.partial(local, order), mesh=mesh, in_specs=in_specs, out_specs=out_specs, check_vma=False
    )
```

```python
import functools
import math

import jax
import jax.numpy as jnp
from jax import lax
from jax.experimental import pallas as pl
from jax.experimental.pallas import tpu as pltpu
from jax.sharding import PartitionSpec as P

TILE = 128
SUB = 8
LARGE = 32
SMALL = 8
LOG2E = math.log2(math.e)
SCALE = LOG2E ** (1.0 / 3.0)


def stage_bits(col_size, row_size):
    order = []
    bit = col_size // 2
    while bit >= 2:
        order.append(("col", bit))
        bit //= 2
    bit = row_size // 2
    while bit >= 1:
        order.append(("row", bit))
        bit //= 2
    if col_size > 1:
        order.append(("col", 1))
    return order


def row_part(order, row):
    total = row * 0
    for place, (axis, bit) in enumerate(order):
        if axis == "row":
            total = total | (((row >> (bit.bit_length() - 1)) & 1) << place)
    return total


def col_part(order, col):
    total = col * 0
    for place, (axis, bit) in enumerate(order):
        if axis == "col":
            total = total | (((col >> (bit.bit_length() - 1)) & 1) << place)
    return total


def pack(order, count, positions, types, tiles, packed):
    blocks_dev = types.shape[0]
    tiles_dev = tiles.shape[1]
    row = row_part(order, lax.axis_index("row"))
    col = col_part(order, lax.axis_index("col"))
    for d in range(3):
        for block in range(blocks_dev):
            place = d * blocks_dev + block
            packed[place : place + 1, :] = positions[d : d + 1, block * TILE : (block + 1) * TILE]
    packed[3 * blocks_dev : 4 * blocks_dev, :] = types[...].astype(jnp.float32)
    packed[4 * blocks_dev :, :] = jnp.zeros((SUB, TILE), jnp.float32)
    near, far = tiles[0:1, :], tiles[1:2, :]
    shift = blocks_dev.bit_length() - 1
    first = ((row | col_part(order, near >> shift)) << shift) | (near & (blocks_dev - 1))
    second = ((row_part(order, far >> shift) | col) << shift) | (far & (blocks_dev - 1))
    live = lax.broadcasted_iota(jnp.int32, (1, tiles_dev), 1) < count[0, 0]
    items = (first & 255, first >> 8, second & 255, second >> 8, jnp.where(live, 1, 0))
    for place, item in enumerate(items):
        start = 4 * blocks_dev + place
        packed[start : start + 1, 0:tiles_dev] = item.astype(jnp.float32)


def pieces(value):
    high = value.astype(jnp.bfloat16).astype(jnp.float32)
    rest = value - high
    mid = rest.astype(jnp.bfloat16).astype(jnp.float32)
    return high, mid, rest - mid


def left_form(base, onehot):
    high, mid, low = pieces(base)
    zero = jnp.zeros_like(base)
    stack = jnp.concatenate([high, high, mid, high, low, mid, onehot, onehot, onehot, zero], axis=0)
    return stack.astype(jnp.bfloat16)


def right_geometry(base):
    high, mid, low = pieces(base)
    zero = jnp.zeros_like(base)
    stack = jnp.concatenate([high, mid, high, low, high, mid, zero, zero, zero, zero], axis=0)
    return stack.astype(jnp.bfloat16)


def right_table(rows):
    high, mid, low = pieces(rows)
    zero = jnp.zeros_like(rows)
    stack = jnp.concatenate([zero] * 6 + [high, mid, low, zero], axis=0)
    return stack.astype(jnp.bfloat16)


def force_form(base, sub_index):
    high, mid, low = pieces(base)
    rest = jnp.where(sub_index < 3, mid, jnp.where(sub_index < 6, jnp.roll(low, 3, axis=0), 0.0))
    return jnp.concatenate([high, rest], axis=0).astype(jnp.bfloat16)


def cross(left, right):
    return lax.dot_general(left, right, (((0,), (0,)), ((), ())), preferred_element_type=jnp.float32)


def fold(value):
    return jnp.sum(value.reshape(TILE // SUB, SUB, TILE), axis=0)


def kernel(
    order,
    elements,
    shift,
    radius,
    valence,
    depth,
    atoms,
    out,
    rho_store,
    left_base,
    right_base,
    onehot,
    rho_rows,
    coord,
    right_own,
    self_weight,
    total,
    energy,
    pulls,
    ranks,
    marks,
    firsts,
    second_cols,
    own_flat,
    work_flat,
    own_list,
    work_list,
    own_sem,
    work_sem,
):
    payload = 5 * SUB
    slots = atoms.shape[0] // payload
    blocks_dev = SUB
    blocks = slots * blocks_dev
    flip = (row_part(order, lax.axis_index("row")) | col_part(order, lax.axis_index("col"))) * blocks_dev
    rho_table, depth_table = {}, {}
    for t in range(elements):
        for u in range(elements):
            rho = jnp.full((SUB, TILE), 0.5 * (radius[t] + radius[u]), jnp.float32)
            rho_table[t, u] = rho_table[u, t] if (u, t) in rho_table else -SCALE / (rho * rho)
            depth_table[t, u] = depth[u, t] * (valence[u] + valence[t])
    for index, (t, u) in enumerate(sorted(rho_table)):
        rho_store[index] = rho_table[t, u]
    ones = jnp.ones((SUB, TILE), jnp.float32)
    zeros = jnp.zeros((SUB, TILE), jnp.float32)

    def put(ref, slot, row, value):
        ref[pl.ds((slot * blocks_dev + 1) * SUB + row, blocks_dev, stride=SUB), :] = value

    def prepare(slot, carry):
        start = pl.multiple_of(slot * payload, SUB)
        x = atoms[pl.ds(start, SUB), :]
        y = atoms[pl.ds(start + SUB, SUB), :]
        z = atoms[pl.ds(start + 2 * SUB, SUB), :]
        kind = atoms[pl.ds(start + 3 * SUB, SUB), :]
        square = x * x + y * y + z * z
        hot = [jnp.where(kind == float(t), 1.0, 0.0) for t in range(elements)]
        value = zeros
        for t in range(elements):
            value = value + hot[t] * valence[t]
        for row, item in enumerate((x, y, z, square, ones, value, zeros, zeros)):
            put(left_base, slot, row, item)
        for row, item in enumerate((-2.0 * x, -2.0 * y, -2.0 * z, ones, square, zeros, zeros, zeros)):
            put(right_base, slot, row, item)
        for row in range(SUB):
            put(onehot, slot, row, hot[row] if row < elements else zeros)
            if row < elements:
                mixed = hot[0] * rho_store[row * elements]
                for t in range(1, elements):
                    mixed = mixed + hot[t] * rho_store[row * elements + t]
            else:
                mixed = zeros
            put(rho_rows, slot, row, mixed)
        for block in range(blocks_dev):
            coord[slot * blocks_dev + block + 1] = zeros
        return carry

    lax.fori_loop(0, slots, prepare, 0)
    for ref in (left_base, right_base, onehot, rho_rows):
        ref[0:SUB, :] = zeros

    lane = lax.broadcasted_iota(jnp.int32, (TILE, TILE), 1)
    sublane = lax.broadcasted_iota(jnp.int32, (TILE, TILE), 0)
    before = jnp.where(sublane < lane, 1.0, 0.0).astype(jnp.bfloat16)
    slot_col = lax.broadcasted_iota(jnp.int32, (slots, slots), 1)
    slot_row = lax.broadcasted_iota(jnp.int32, (slots, slots), 0)
    above = jnp.where(slot_col < slot_row, 1.0, 0.0).astype(jnp.bfloat16)

    def meta(row):
        return atoms[pl.ds(4 * SUB + row, slots, stride=payload), :]

    first_all = (meta(0) + 256.0 * meta(1)).astype(jnp.int32) ^ flip
    live_all = meta(4)
    firsts[...] = first_all.astype(jnp.float32)

    def rank(mark):
        count = mark.astype(jnp.bfloat16)
        inside = jnp.dot(count, before, preferred_element_type=jnp.float32)
        earlier = jnp.dot(above, count, preferred_element_type=jnp.float32)
        place = inside + jnp.sum(earlier, axis=1, keepdims=True)
        ranks[...] = jnp.where(mark > 0.0, place, -1.0)
        return jnp.sum(mark).astype(jnp.int32)

    position = sublane.astype(jnp.float32)

    def compact(chunk, flat, columns):
        offset = (chunk * TILE).astype(jnp.float32)

        def some(group, carry):
            start = pl.multiple_of(group * SUB, SUB)
            wanted = ranks[pl.ds(start, SUB), :] - offset
            picks = [
                jnp.where(wanted[k : k + 1] == position, 1.0, 0.0).astype(jnp.bfloat16) for k in range(SUB)
            ]
            entries = [
                atoms[pl.ds(pl.multiple_of((start + k) * payload + 4 * SUB, SUB), SUB), :].astype(jnp.bfloat16)
                for k in range(SUB)
            ]
            pick = jnp.concatenate(picks, axis=1)
            entry = jnp.concatenate(entries, axis=1)
            along = lax.dot_general(
                entry, pick, (((1,), (1,)), ((), ())), preferred_element_type=jnp.float32
            )
            return carry + along

        row = lax.fori_loop(0, slots // SUB, some, zeros)
        first = (row[0:1] + 256.0 * row[1:2]).astype(jnp.int32) ^ flip
        second = (row[2:3] + 256.0 * row[3:4]).astype(jnp.int32) ^ flip
        valid = row[4:5] > 0.0
        flat[pl.ds(chunk, 1), :] = jnp.where(valid, ((first + 1) << shift) | (second + 1), 0)
        if columns:
            target = jnp.where(valid, second, -1).astype(jnp.float32)
            column = jnp.transpose(jnp.broadcast_to(target, (SUB, TILE)))[:, 0:1]
            second_cols[...] = jnp.broadcast_to(column, (TILE, TILE))

    def send(source, target, group, semaphore):
        start = pl.multiple_of(group * SUB, SUB)
        return pltpu.make_async_copy(source.at[pl.ds(start, SUB)], target.at[pl.ds(start, SUB)], semaphore)

    def send_rest(source, target, count, semaphore):
        def one(group, carry):
            copy = send(source, target, group, semaphore)
            copy.start()
            copy.wait()
            return carry

        lax.fori_loop(1, (count + SUB * TILE - 1) // (SUB * TILE), one, 0)

    own_mark = jnp.where(first_all < blocks_dev, live_all, 0.0)
    marks[...] = own_mark
    own_count = rank(own_mark)

    def own_chunk(chunk, carry):
        compact(chunk, own_flat, True)
        part = 4 * SUB
        filled = jnp.minimum(own_count - chunk * TILE, TILE)

        def some(group, carry):
            cols = second_cols[pl.ds(pl.multiple_of(group * part, part), part), :]

            def rows(slot_group, carry):
                start = pl.multiple_of(slot_group * SUB, SUB)
                here = firsts[pl.ds(start, SUB), :]
                found = []
                for k in range(SUB):
                    hit = jnp.where(cols == here[k : k + 1], 1.0, 0.0)
                    found.append(jnp.max(hit, axis=0, keepdims=True))
                old = marks[pl.ds(start, SUB), :]
                marks[pl.ds(start, SUB), :] = jnp.maximum(old, jnp.concatenate(found, axis=0))
                return carry

            return lax.fori_loop(0, slots // SUB, rows, carry)

        lax.fori_loop(0, (filled + part - 1) // part, some, 0)
        return carry

    lax.fori_loop(0, (own_count + TILE - 1) // TILE, own_chunk, 0)
    send_rest(own_flat, own_list, own_count, own_sem)
    own_copy = send(own_flat, own_list, 0, own_sem)
    own_copy.start()

    work_count = rank(marks[...] * live_all)

    def work_chunk(chunk, carry):
        compact(chunk, work_flat, False)
        return carry

    lax.fori_loop(0, (work_count + TILE - 1) // TILE, work_chunk, 0)
    send_rest(work_flat, work_list, work_count, work_sem)
    work_copy = send(work_flat, work_list, 0, work_sem)
    work_copy.start()
    work_copy.wait()
    own_copy.wait()

    def at(ref, block):
        return ref[pl.ds(pl.multiple_of(block * SUB, SUB), SUB), :]

    def fetch(ref, start):
        row = lax.shift_right_logical(start, TILE.bit_length() - 1)
        column = start & (TILE - 1)

        def at_step(step):
            code = ref[row, column + step]
            return code >> shift, code & ((1 << shift) - 1)

        return at_step

    def first_pass(start, size):
        pair = fetch(work_list, start)
        for step in range(size):
            first, second = pair(step)
            left = left_form(at(left_base, second), at(onehot, second))
            right = jnp.concatenate(
                [right_geometry(at(right_base, first)), right_table(at(rho_rows, first))], axis=1
            )
            both = cross(left, right)
            ratio = both[:, :TILE] * both[:, TILE:]
            bond = jnp.exp2(ratio * ratio * ratio)
            same = jnp.where(first == second, 1.0 / SUB, 0.0)
            coord[first] = coord[first] + (fold(bond) - same)

    def large(group, carry):
        first_pass(group * LARGE, LARGE)
        return carry

    def small(group, carry):
        first_pass(group * SMALL, SMALL)
        return carry

    fulls = work_count // LARGE
    lax.fori_loop(0, fulls, large, 0)
    lax.fori_loop(fulls * (LARGE // SMALL), (work_count + SMALL - 1) // SMALL, small, 0)

    sub_index = lax.broadcasted_iota(jnp.int32, (SUB, TILE), 0)

    for block in range(blocks_dev):
        base = at(left_base, block + 1)
        hot = at(onehot, block + 1)
        load = jnp.sum(coord[block + 1], axis=0, keepdims=True) + base[5:6]
        depth_rows = zeros
        for row in range(elements):
            mixed = hot[0:1] * depth_table[row, 0]
            for t in range(1, elements):
                mixed = mixed + hot[t : t + 1] * depth_table[row, t]
            depth_rows = jnp.where(sub_index == row, mixed, depth_rows)
        load_rows = jnp.where(sub_index == 4, load, jnp.where(sub_index == 5, 1.0, 0.0))
        forms = [
            right_geometry(at(right_base, block + 1)),
            right_table(at(rho_rows, block + 1)),
            right_table(depth_rows),
            right_geometry(load_rows),
        ]
        alone = hot[0:1] * depth_table[0, 0]
        for t in range(1, elements):
            alone = alone + hot[t : t + 1] * depth_table[t, t]
        self_weight[block + 1] = jnp.where(sub_index == 0, alone / (load + load), 0.0)
        right_own[block + 1] = jnp.concatenate(forms, axis=1)
    self_weight[0] = zeros
    right_own[0] = jnp.zeros(right_own.shape[1:], jnp.bfloat16)
    for block in range(blocks_dev + 1):
        total[block] = jnp.zeros(total.shape[1:], jnp.float32)
        energy[block] = zeros

    def second_pass(start, size):
        pair = fetch(own_list, start)
        for step in range(size):
            first, second = pair(step)
            load = jnp.sum(coord[second], axis=0, keepdims=True)
            base = at(left_base, second)
            base = base + jnp.where(sub_index == 5, load, 0.0)
            left = left_form(base, at(onehot, second))
            mixed = cross(left, right_own[first])
            dist, rho, depth, both_load = [mixed[:, k * TILE : (k + 1) * TILE] for k in range(4)]
            ratio = dist * rho
            squared = ratio * ratio
            bond = jnp.exp2(squared * ratio)
            weight = depth * bond / both_load
            pull = weight * squared * rho
            pull_high = pull.astype(jnp.bfloat16)
            pulls[step, :, 0:TILE] = pull_high
            pulls[step, :, TILE:] = (pull - pull_high.astype(jnp.float32)).astype(jnp.bfloat16)
            same = jnp.where(first == second, 1.0, 0.0)
            energy[first] = energy[first] + (fold(weight) - same * self_weight[first])
        for step in range(size):
            first, second = pair(step)
            form = force_form(at(left_base, second), sub_index)
            total[first] = total[first] + jnp.dot(form, pulls[step], preferred_element_type=jnp.float32)

    def second_group(group, carry):
        second_pass(group * SMALL, SMALL)
        return carry

    lax.fori_loop(0, (own_count + SMALL - 1) // SMALL, second_group, 0)

    for block in range(blocks_dev):
        both = total[block + 1]
        sums = both[:, :TILE] + both[:, TILE:]
        here = at(left_base, block + 1)
        lanes = slice(block * TILE, (block + 1) * TILE)
        for d in range(3):
            moment = sums[d : d + 1] + sums[8 + d : 9 + d] + sums[11 + d : 12 + d]
            out[d : d + 1, lanes] = (-6.0 / LOG2E) * (moment - here[d : d + 1] * sums[4:5])
        out[3:4, lanes] = -jnp.sum(energy[block + 1], axis=0, keepdims=True)


def local(order, positions, types, radius_type, valence_type, bond_depth, pair_tiles, tile_count):
    atom_dev = positions.shape[1]
    blocks_dev = atom_dev // TILE
    rows = lax.axis_size("row")
    cols = lax.axis_size("col")
    slots = rows * cols
    blocks = slots * blocks_dev
    tiles_dev = pair_tiles.shape[2]

    smem = pl.BlockSpec(memory_space=pltpu.SMEM)
    vmem = pl.BlockSpec(memory_space=pltpu.VMEM)
    packed = pl.pallas_call(
        functools.partial(pack, order),
        out_shape=pltpu.VMEM((5 * SUB, TILE), jnp.float32),
        in_specs=[smem, vmem, vmem, vmem],
        out_specs=vmem,
    )(tile_count, positions, types.reshape(blocks_dev, TILE), jnp.transpose(pair_tiles[0, 0]))
    gathered = packed
    for axis, bit in order:
        size = lax.axis_size(axis)
        other = lax.ppermute(gathered, axis, [(i, i ^ bit) for i in range(size)])
        gathered = jnp.concatenate([gathered, other], axis=0)

    gathered = pltpu.with_memory_space_constraint(gathered, pltpu.VMEM)
    elements = radius_type.shape[0]
    shift = (blocks + 1).bit_length()
    chunks = -(-slots * tiles_dev // (SUB * TILE)) * SUB
    own_chunks = -(-cols * tiles_dev // (SUB * TILE)) * SUB
    return pl.pallas_call(
        functools.partial(kernel, order, elements, shift),
        out_shape=jax.ShapeDtypeStruct((4, atom_dev), jnp.float32),
        in_specs=[smem, smem, smem, vmem],
        out_specs=vmem,
        scratch_shapes=[
            pltpu.VMEM((elements * elements, SUB, TILE), jnp.float32),
            pltpu.VMEM((blocks * SUB + SUB, TILE), jnp.float32),
            pltpu.VMEM((blocks * SUB + SUB, TILE), jnp.float32),
            pltpu.VMEM((blocks * SUB + SUB, TILE), jnp.float32),
            pltpu.VMEM((blocks * SUB + SUB, TILE), jnp.float32),
            pltpu.VMEM((blocks + 1, SUB, TILE), jnp.float32),
            pltpu.VMEM((blocks_dev + 1, 10 * SUB, 4 * TILE), jnp.bfloat16),
            pltpu.VMEM((blocks_dev + 1, SUB, TILE), jnp.float32),
            pltpu.VMEM((blocks_dev + 1, 2 * SUB, 2 * TILE), jnp.float32),
            pltpu.VMEM((blocks_dev + 1, SUB, TILE), jnp.float32),
            pltpu.VMEM((SMALL, TILE, 2 * TILE), jnp.bfloat16),
            pltpu.VMEM((slots, TILE), jnp.float32),
            pltpu.VMEM((slots, TILE), jnp.float32),
            pltpu.VMEM((slots, TILE), jnp.float32),
            pltpu.VMEM((TILE, TILE), jnp.float32),
            pltpu.VMEM((own_chunks, TILE), jnp.int32),
            pltpu.VMEM((chunks, TILE), jnp.int32),
            pltpu.SMEM((own_chunks, TILE), jnp.int32),
            pltpu.SMEM((chunks, TILE), jnp.int32),
            pltpu.SemaphoreType.DMA,
            pltpu.SemaphoreType.DMA,
        ],
        compiler_params=pltpu.CompilerParams(vmem_limit_bytes=56 * 1024 * 1024),
    )(radius_type, valence_type, bond_depth, gathered)


def solution(mesh):
    order = stage_bits(mesh.shape["col"], mesh.shape["row"])
    in_specs = (
        P(None, ("row", "col")),
        P(("row", "col")),
        P(),
        P(),
        P(),
        P("row", "col", None, None),
        P("row", "col"),
    )
    out_specs = P(None, ("row", "col"))
    return jax.shard_map(
        functools.partial(local, order), mesh=mesh, in_specs=in_specs, out_specs=out_specs, check_vma=False
    )
```

```python
import functools
import math

import jax
import jax.numpy as jnp
from jax import lax
from jax.experimental import pallas as pl
from jax.experimental.pallas import tpu as pltpu
from jax.sharding import PartitionSpec as P

TILE = 128
SUB = 8
LARGE = 32
MIDDLE = 16
SMALL = 8
LOG2E = math.log2(math.e)
SCALE = LOG2E ** (1.0 / 3.0)


def stage_bits(col_size, row_size):
    order = []
    bit = col_size // 2
    while bit >= 2:
        order.append(("col", bit))
        bit //= 2
    bit = row_size // 2
    while bit >= 1:
        order.append(("row", bit))
        bit //= 2
    if col_size > 1:
        order.append(("col", 1))
    return order


def row_part(order, row):
    total = row * 0
    for place, (axis, bit) in enumerate(order):
        if axis == "row":
            total = total | (((row >> (bit.bit_length() - 1)) & 1) << place)
    return total


def col_part(order, col):
    total = col * 0
    for place, (axis, bit) in enumerate(order):
        if axis == "col":
            total = total | (((col >> (bit.bit_length() - 1)) & 1) << place)
    return total


def pack(order, count, positions, types, tiles, packed):
    blocks_dev = types.shape[0]
    tiles_dev = tiles.shape[1]
    row = row_part(order, lax.axis_index("row"))
    col = col_part(order, lax.axis_index("col"))
    for d in range(3):
        for block in range(blocks_dev):
            place = d * blocks_dev + block
            packed[place : place + 1, :] = positions[d : d + 1, block * TILE : (block + 1) * TILE]
    packed[3 * blocks_dev : 4 * blocks_dev, :] = types[...].astype(jnp.float32)
    packed[4 * blocks_dev :, :] = jnp.zeros((SUB, TILE), jnp.float32)
    near, far = tiles[0:1, :], tiles[1:2, :]
    shift = blocks_dev.bit_length() - 1
    first = ((row | col_part(order, near >> shift)) << shift) | (near & (blocks_dev - 1))
    second = ((row_part(order, far >> shift) | col) << shift) | (far & (blocks_dev - 1))
    live = lax.broadcasted_iota(jnp.int32, (1, tiles_dev), 1) < count[0, 0]
    items = (first & 255, first >> 8, second & 255, second >> 8, jnp.where(live, 1, 0))
    for place, item in enumerate(items):
        start = 4 * blocks_dev + place
        packed[start : start + 1, 0:tiles_dev] = item.astype(jnp.float32)


def pieces(value):
    high = value.astype(jnp.bfloat16).astype(jnp.float32)
    rest = value - high
    mid = rest.astype(jnp.bfloat16).astype(jnp.float32)
    return high, mid, rest - mid


def left_form(base, onehot):
    high, mid, low = pieces(base)
    zero = jnp.zeros_like(base)
    stack = jnp.concatenate([high, high, mid, high, low, mid, onehot, onehot, onehot, zero], axis=0)
    return stack.astype(jnp.bfloat16)


def right_geometry(base):
    high, mid, low = pieces(base)
    zero = jnp.zeros_like(base)
    stack = jnp.concatenate([high, mid, high, low, high, mid, zero, zero, zero, zero], axis=0)
    return stack.astype(jnp.bfloat16)


def right_table(rows):
    high, mid, low = pieces(rows)
    zero = jnp.zeros_like(rows)
    stack = jnp.concatenate([zero] * 6 + [high, mid, low, zero], axis=0)
    return stack.astype(jnp.bfloat16)


def force_form(base, sub_index):
    high, mid, low = pieces(base)
    rest = jnp.where(sub_index < 3, mid, jnp.where(sub_index < 6, jnp.roll(low, 3, axis=0), 0.0))
    return jnp.concatenate([high, rest], axis=0).astype(jnp.bfloat16)


def cross(left, right):
    return lax.dot_general(left, right, (((0,), (0,)), ((), ())), preferred_element_type=jnp.float32)


def fold(value):
    return jnp.sum(value.reshape(TILE // SUB, SUB, TILE), axis=0)


def kernel(
    order,
    elements,
    shift,
    radius,
    valence,
    depth,
    atoms,
    out,
    rho_store,
    left_base,
    right_base,
    onehot,
    rho_rows,
    coord,
    right_own,
    self_weight,
    total,
    energy,
    pulls,
    ranks,
    marks,
    firsts,
    second_cols,
    own_flat,
    work_flat,
    own_list,
    work_list,
    own_sem,
    head_sem,
    work_sem,
):
    payload = 5 * SUB
    slots = atoms.shape[0] // payload
    blocks_dev = SUB
    blocks = slots * blocks_dev
    flip = (row_part(order, lax.axis_index("row")) | col_part(order, lax.axis_index("col"))) * blocks_dev
    rho_table, depth_table = {}, {}
    for t in range(elements):
        for u in range(elements):
            rho = jnp.full((SUB, TILE), 0.5 * (radius[t] + radius[u]), jnp.float32)
            rho_table[t, u] = rho_table[u, t] if (u, t) in rho_table else -SCALE / (rho * rho)
            depth_table[t, u] = depth[u, t] * (valence[u] + valence[t])
    for index, (t, u) in enumerate(sorted(rho_table)):
        rho_store[index] = rho_table[t, u]
    ones = jnp.ones((SUB, TILE), jnp.float32)
    zeros = jnp.zeros((SUB, TILE), jnp.float32)

    def put(ref, slot, row, value):
        ref[pl.ds((slot * blocks_dev + 1) * SUB + row, blocks_dev, stride=SUB), :] = value

    def prepare(slot, carry):
        start = pl.multiple_of(slot * payload, SUB)
        x = atoms[pl.ds(start, SUB), :]
        y = atoms[pl.ds(start + SUB, SUB), :]
        z = atoms[pl.ds(start + 2 * SUB, SUB), :]
        kind = atoms[pl.ds(start + 3 * SUB, SUB), :]
        square = x * x + y * y + z * z
        hot = [jnp.where(kind == float(t), 1.0, 0.0) for t in range(elements)]
        value = zeros
        for t in range(elements):
            value = value + hot[t] * valence[t]
        for row, item in enumerate((x, y, z, square, ones, value, zeros, zeros)):
            put(left_base, slot, row, item)
        for row, item in enumerate((-2.0 * x, -2.0 * y, -2.0 * z, ones, square, zeros, zeros, zeros)):
            put(right_base, slot, row, item)
        for row in range(SUB):
            put(onehot, slot, row, hot[row] if row < elements else zeros)
            if row < elements:
                mixed = hot[0] * rho_store[row * elements]
                for t in range(1, elements):
                    mixed = mixed + hot[t] * rho_store[row * elements + t]
            else:
                mixed = zeros
            put(rho_rows, slot, row, mixed)
        for block in range(blocks_dev):
            coord[slot * blocks_dev + block + 1] = zeros
        return carry

    lax.fori_loop(0, slots, prepare, 0)
    for ref in (left_base, right_base, onehot, rho_rows):
        ref[0:SUB, :] = zeros

    lane = lax.broadcasted_iota(jnp.int32, (TILE, TILE), 1)
    sublane = lax.broadcasted_iota(jnp.int32, (TILE, TILE), 0)
    before = jnp.where(sublane < lane, 1.0, 0.0).astype(jnp.bfloat16)
    slot_col = lax.broadcasted_iota(jnp.int32, (slots, slots), 1)
    slot_row = lax.broadcasted_iota(jnp.int32, (slots, slots), 0)
    above = jnp.where(slot_col < slot_row, 1.0, 0.0).astype(jnp.bfloat16)

    def meta(row):
        return atoms[pl.ds(4 * SUB + row, slots, stride=payload), :]

    first_all = (meta(0) + 256.0 * meta(1)).astype(jnp.int32) ^ flip
    live_all = meta(4)
    firsts[...] = first_all.astype(jnp.float32)

    def rank(mark):
        count = mark.astype(jnp.bfloat16)
        inside = jnp.dot(count, before, preferred_element_type=jnp.float32)
        earlier = jnp.dot(above, count, preferred_element_type=jnp.float32)
        place = inside + jnp.sum(earlier, axis=1, keepdims=True)
        ranks[...] = jnp.where(mark > 0.0, place, -1.0)
        return jnp.sum(mark).astype(jnp.int32)

    position = sublane.astype(jnp.float32)
    batch = min(slots, 4 * SUB)

    def compact(chunk, flat, columns):
        offset = jnp.float32(1.0) * (chunk * TILE)

        def some(group, carry):
            total = carry
            for part in range(batch // SUB):
                start = pl.multiple_of(group * batch + part * SUB, SUB)
                wanted = ranks[pl.ds(start, SUB), :] - offset
                picks = [
                    jnp.where(wanted[k : k + 1] == position, 1.0, 0.0).astype(jnp.bfloat16) for k in range(SUB)
                ]
                entries = [
                    atoms[pl.ds(pl.multiple_of((start + k) * payload + 4 * SUB, SUB), SUB), :].astype(
                        jnp.bfloat16
                    )
                    for k in range(SUB)
                ]
                total = total + lax.dot_general(
                    jnp.concatenate(entries, axis=1),
                    jnp.concatenate(picks, axis=1),
                    (((1,), (1,)), ((), ())),
                    preferred_element_type=jnp.float32,
                )
            return total

        row = lax.fori_loop(0, slots // batch, some, zeros)
        first = (row[0:1] + 256.0 * row[1:2]).astype(jnp.int32) ^ flip
        second = (row[2:3] + 256.0 * row[3:4]).astype(jnp.int32) ^ flip
        valid = row[4:5] > 0.0
        flat[pl.ds(chunk, 1), :] = jnp.where(valid, ((first + 1) << shift) | (second + 1), 0)
        if columns:
            target = jnp.where(valid, second, -1).astype(jnp.float32)
            column = jnp.transpose(jnp.broadcast_to(target, (SUB, TILE)))[:, 0:1]
            second_cols[...] = jnp.broadcast_to(column, (TILE, TILE))

    def send(source, target, group, semaphore):
        start = pl.multiple_of(group * SUB, SUB)
        return pltpu.make_async_copy(source.at[pl.ds(start, SUB)], target.at[pl.ds(start, SUB)], semaphore)

    def send_rest(source, target, count, semaphore):
        def one(group, carry):
            copy = send(source, target, group, semaphore)
            copy.start()
            copy.wait()
            return carry

        lax.fori_loop(1, (count + SUB * TILE - 1) // (SUB * TILE), one, 0)

    own_mark = jnp.where(first_all < blocks_dev, live_all, 0.0)
    marks[...] = own_mark
    own_count = rank(own_mark)

    def own_chunk(chunk, carry):
        compact(chunk, own_flat, True)
        part = 4 * SUB
        filled = jnp.minimum(own_count - chunk * TILE, TILE)

        def some(group, carry):
            cols = second_cols[pl.ds(pl.multiple_of(group * part, part), part), :]

            def rows(slot_group, carry):
                for piece in range(batch // SUB):
                    start = pl.multiple_of(slot_group * batch + piece * SUB, SUB)
                    here = firsts[pl.ds(start, SUB), :]
                    found = []
                    for k in range(SUB):
                        hit = jnp.where(cols == here[k : k + 1], 1.0, 0.0)
                        found.append(jnp.max(hit, axis=0, keepdims=True))
                    old = marks[pl.ds(start, SUB), :]
                    marks[pl.ds(start, SUB), :] = jnp.maximum(old, jnp.concatenate(found, axis=0))
                return carry

            return lax.fori_loop(0, slots // batch, rows, carry)

        lax.fori_loop(0, (filled + part - 1) // part, some, 0)
        return carry

    lax.fori_loop(0, (own_count + TILE - 1) // TILE, own_chunk, 0)
    send_rest(own_flat, own_list, own_count, own_sem)
    own_copy = send(own_flat, own_list, 0, own_sem)
    own_copy.start()

    work_count = rank(marks[...] * live_all)

    head_copy = pltpu.make_async_copy(work_flat.at[pl.ds(0, 1)], work_list.at[pl.ds(0, 1)], head_sem)
    compact(0, work_flat, False)
    head_copy.start()

    def work_chunk(chunk, carry):
        compact(chunk, work_flat, False)
        return carry

    lax.fori_loop(1, (work_count + TILE - 1) // TILE, work_chunk, 0)
    send_rest(work_flat, work_list, work_count, work_sem)
    rest_copy = pltpu.make_async_copy(
        work_flat.at[pl.ds(1, SUB - 1)], work_list.at[pl.ds(1, SUB - 1)], work_sem
    )
    rest_copy.start()
    head_copy.wait()
    own_copy.wait()

    def at(ref, block):
        return ref[pl.ds(pl.multiple_of(block * SUB, SUB), SUB), :]

    def fetch(ref, start):
        row = lax.shift_right_logical(start, TILE.bit_length() - 1)
        column = start & (TILE - 1)

        def at_step(step):
            code = ref[row, column + step]
            return code >> shift, code & ((1 << shift) - 1)

        return at_step

    def first_pass(start, size):
        pair = fetch(work_list, start)
        for step in range(size):
            first, second = pair(step)
            left = left_form(at(left_base, second), at(onehot, second))
            right = jnp.concatenate(
                [right_geometry(at(right_base, first)), right_table(at(rho_rows, first))], axis=1
            )
            both = cross(left, right)
            ratio = both[:, :TILE] * both[:, TILE:]
            bond = jnp.exp2(ratio * ratio * ratio)
            same = jnp.where(first == second, 1.0 / SUB, 0.0)
            coord[first] = coord[first] + (fold(bond) - same)

    fulls = work_count // LARGE
    early = TILE // LARGE

    def large(group, carry):
        first_pass(group * LARGE, LARGE)
        return carry

    def small(group, carry):
        first_pass(group * SMALL, SMALL)
        return carry

    lax.fori_loop(0, jnp.minimum(fulls, early), large, 0)
    rest_copy.wait()
    lax.fori_loop(jnp.minimum(fulls, early), fulls, large, 0)
    lax.fori_loop(fulls * (LARGE // SMALL), (work_count + SMALL - 1) // SMALL, small, 0)

    sub_index = lax.broadcasted_iota(jnp.int32, (SUB, TILE), 0)

    for block in range(blocks_dev):
        base = at(left_base, block + 1)
        hot = at(onehot, block + 1)
        load = jnp.sum(coord[block + 1], axis=0, keepdims=True) + base[5:6]
        depth_rows = zeros
        for row in range(elements):
            mixed = hot[0:1] * depth_table[row, 0]
            for t in range(1, elements):
                mixed = mixed + hot[t : t + 1] * depth_table[row, t]
            depth_rows = jnp.where(sub_index == row, mixed, depth_rows)
        load_rows = jnp.where(sub_index == 4, load, jnp.where(sub_index == 5, 1.0, 0.0))
        forms = [
            right_geometry(at(right_base, block + 1)),
            right_table(at(rho_rows, block + 1)),
            right_table(depth_rows),
            right_geometry(load_rows),
        ]
        alone = hot[0:1] * depth_table[0, 0]
        for t in range(1, elements):
            alone = alone + hot[t : t + 1] * depth_table[t, t]
        self_weight[block + 1] = jnp.where(sub_index == 0, alone / (load + load), 0.0)
        right_own[block + 1] = jnp.concatenate(forms, axis=1)
    self_weight[0] = zeros
    right_own[0] = jnp.zeros(right_own.shape[1:], jnp.bfloat16)
    for block in range(blocks_dev + 1):
        total[block] = jnp.zeros(total.shape[1:], jnp.float32)
        energy[block] = zeros

    def second_pass(start, size):
        pair = fetch(own_list, start)
        for step in range(size):
            first, second = pair(step)
            load = jnp.sum(coord[second], axis=0, keepdims=True)
            base = at(left_base, second)
            base = base + jnp.where(sub_index == 5, load, 0.0)
            left = left_form(base, at(onehot, second))
            mixed = cross(left, right_own[first])
            dist, rho, depth, both_load = [mixed[:, k * TILE : (k + 1) * TILE] for k in range(4)]
            ratio = dist * rho
            squared = ratio * ratio
            bond = jnp.exp2(squared * ratio)
            weight = depth * bond / both_load
            pull = weight * squared * rho
            pull_high = pull.astype(jnp.bfloat16)
            pulls[step, :, 0:TILE] = pull_high
            pulls[step, :, TILE:] = (pull - pull_high.astype(jnp.float32)).astype(jnp.bfloat16)
            same = jnp.where(first == second, 1.0, 0.0)
            energy[first] = energy[first] + (fold(weight) - same * self_weight[first])
        for step in range(size):
            first, second = pair(step)
            form = force_form(at(left_base, second), sub_index)
            total[first] = total[first] + jnp.dot(form, pulls[step], preferred_element_type=jnp.float32)

    def second_group(group, carry):
        second_pass(group * SMALL, SMALL)
        return carry

    def second_large(group, carry):
        second_pass(group * MIDDLE, MIDDLE)
        return carry

    middles = (own_count + MIDDLE - SMALL - 1) // MIDDLE
    lax.fori_loop(0, middles, second_large, 0)
    lax.fori_loop(middles * (MIDDLE // SMALL), (own_count + SMALL - 1) // SMALL, second_group, 0)

    for block in range(blocks_dev):
        both = total[block + 1]
        sums = both[:, :TILE] + both[:, TILE:]
        here = at(left_base, block + 1)
        lanes = slice(block * TILE, (block + 1) * TILE)
        for d in range(3):
            moment = sums[d : d + 1] + sums[8 + d : 9 + d] + sums[11 + d : 12 + d]
            out[d : d + 1, lanes] = (-6.0 / LOG2E) * (moment - here[d : d + 1] * sums[4:5])
        out[3:4, lanes] = -jnp.sum(energy[block + 1], axis=0, keepdims=True)


def local(order, positions, types, radius_type, valence_type, bond_depth, pair_tiles, tile_count):
    atom_dev = positions.shape[1]
    blocks_dev = atom_dev // TILE
    rows = lax.axis_size("row")
    cols = lax.axis_size("col")
    slots = rows * cols
    blocks = slots * blocks_dev
    tiles_dev = pair_tiles.shape[2]

    smem = pl.BlockSpec(memory_space=pltpu.SMEM)
    vmem = pl.BlockSpec(memory_space=pltpu.VMEM)
    packed = pl.pallas_call(
        functools.partial(pack, order),
        out_shape=pltpu.VMEM((5 * SUB, TILE), jnp.float32),
        in_specs=[smem, vmem, vmem, vmem],
        out_specs=vmem,
    )(tile_count, positions, types.reshape(blocks_dev, TILE), jnp.transpose(pair_tiles[0, 0]))
    gathered = packed
    for axis, bit in order:
        size = lax.axis_size(axis)
        other = lax.ppermute(gathered, axis, [(i, i ^ bit) for i in range(size)])
        gathered = jnp.concatenate([gathered, other], axis=0)

    gathered = pltpu.with_memory_space_constraint(gathered, pltpu.VMEM)
    elements = radius_type.shape[0]
    shift = (blocks + 1).bit_length()
    chunks = -(-slots * tiles_dev // (SUB * TILE)) * SUB
    own_chunks = -(-cols * tiles_dev // (SUB * TILE)) * SUB
    return pl.pallas_call(
        functools.partial(kernel, order, elements, shift),
        out_shape=jax.ShapeDtypeStruct((4, atom_dev), jnp.float32),
        in_specs=[smem, smem, smem, vmem],
        out_specs=vmem,
        scratch_shapes=[
            pltpu.VMEM((elements * elements, SUB, TILE), jnp.float32),
            pltpu.VMEM((blocks * SUB + SUB, TILE), jnp.float32),
            pltpu.VMEM((blocks * SUB + SUB, TILE), jnp.float32),
            pltpu.VMEM((blocks * SUB + SUB, TILE), jnp.float32),
            pltpu.VMEM((blocks * SUB + SUB, TILE), jnp.float32),
            pltpu.VMEM((blocks + 1, SUB, TILE), jnp.float32),
            pltpu.VMEM((blocks_dev + 1, 10 * SUB, 4 * TILE), jnp.bfloat16),
            pltpu.VMEM((blocks_dev + 1, SUB, TILE), jnp.float32),
            pltpu.VMEM((blocks_dev + 1, 2 * SUB, 2 * TILE), jnp.float32),
            pltpu.VMEM((blocks_dev + 1, SUB, TILE), jnp.float32),
            pltpu.VMEM((MIDDLE, TILE, 2 * TILE), jnp.bfloat16),
            pltpu.VMEM((slots, TILE), jnp.float32),
            pltpu.VMEM((slots, TILE), jnp.float32),
            pltpu.VMEM((slots, TILE), jnp.float32),
            pltpu.VMEM((TILE, TILE), jnp.float32),
            pltpu.VMEM((own_chunks, TILE), jnp.int32),
            pltpu.VMEM((chunks, TILE), jnp.int32),
            pltpu.SMEM((own_chunks, TILE), jnp.int32),
            pltpu.SMEM((chunks, TILE), jnp.int32),
            pltpu.SemaphoreType.DMA,
            pltpu.SemaphoreType.DMA,
            pltpu.SemaphoreType.DMA,
        ],
        compiler_params=pltpu.CompilerParams(vmem_limit_bytes=56 * 1024 * 1024),
    )(radius_type, valence_type, bond_depth, gathered)


def solution(mesh):
    order = stage_bits(mesh.shape["col"], mesh.shape["row"])
    in_specs = (
        P(None, ("row", "col")),
        P(("row", "col")),
        P(),
        P(),
        P(),
        P("row", "col", None, None),
        P("row", "col"),
    )
    out_specs = P(None, ("row", "col"))
    return jax.shard_map(
        functools.partial(local, order), mesh=mesh, in_specs=in_specs, out_specs=out_specs, check_vma=False
    )
```

```python
import functools
import math

import jax
import jax.numpy as jnp
from jax import lax
from jax.experimental import pallas as pl
from jax.experimental.pallas import tpu as pltpu
from jax.sharding import PartitionSpec as P

TILE = 128
SUB = 8
LARGE = 64
MIDDLE = 16
SMALL = 8
LOG2E = math.log2(math.e)
SCALE = LOG2E ** (1.0 / 3.0)


def stage_bits(col_size, row_size):
    order = []
    bit = col_size // 2
    while bit >= 2:
        order.append(("col", bit))
        bit //= 2
    bit = row_size // 2
    while bit >= 1:
        order.append(("row", bit))
        bit //= 2
    if col_size > 1:
        order.append(("col", 1))
    return order


def row_part(order, row):
    total = row * 0
    for place, (axis, bit) in enumerate(order):
        if axis == "row":
            total = total | (((row >> (bit.bit_length() - 1)) & 1) << place)
    return total


def col_part(order, col):
    total = col * 0
    for place, (axis, bit) in enumerate(order):
        if axis == "col":
            total = total | (((col >> (bit.bit_length() - 1)) & 1) << place)
    return total


def pack(order, count, positions, types, tiles, packed):
    blocks_dev = types.shape[0]
    tiles_dev = tiles.shape[1]
    row = row_part(order, lax.axis_index("row"))
    col = col_part(order, lax.axis_index("col"))
    for d in range(3):
        for block in range(blocks_dev):
            place = d * blocks_dev + block
            packed[place : place + 1, :] = positions[d : d + 1, block * TILE : (block + 1) * TILE]
    packed[3 * blocks_dev : 4 * blocks_dev, :] = types[...].astype(jnp.float32)
    packed[4 * blocks_dev :, :] = jnp.zeros((SUB, TILE), jnp.float32)
    near, far = tiles[0:1, :], tiles[1:2, :]
    shift = blocks_dev.bit_length() - 1
    first = ((row | col_part(order, near >> shift)) << shift) | (near & (blocks_dev - 1))
    second = ((row_part(order, far >> shift) | col) << shift) | (far & (blocks_dev - 1))
    live = lax.broadcasted_iota(jnp.int32, (1, tiles_dev), 1) < count[0, 0]
    items = (first & 255, first >> 8, second & 255, second >> 8, jnp.where(live, 1, 0))
    for place, item in enumerate(items):
        start = 4 * blocks_dev + place
        packed[start : start + 1, 0:tiles_dev] = item.astype(jnp.float32)


def tables(elements, radius, valence, depth, rho_store, depth_store, valence_store):
    shape = (SUB, TILE)
    for t in range(elements):
        valence_store[t] = jnp.full(shape, valence[t], jnp.float32)
        for u in range(elements):
            rho = jnp.full(shape, 0.5 * (radius[t] + radius[u]), jnp.float32)
            rho_store[t * elements + u] = -SCALE / (rho * rho)
            depth_store[t * elements + u] = jnp.full(shape, depth[u, t] * (valence[u] + valence[t]), jnp.float32)


def pieces(value):
    high = value.astype(jnp.bfloat16).astype(jnp.float32)
    rest = value - high
    mid = rest.astype(jnp.bfloat16).astype(jnp.float32)
    return high, mid, rest - mid


def left_form(base, onehot):
    high, mid, low = pieces(base)
    zero = jnp.zeros_like(base)
    stack = jnp.concatenate([high, high, mid, high, low, mid, onehot, onehot, onehot, zero], axis=0)
    return stack.astype(jnp.bfloat16)


def right_geometry(base):
    high, mid, low = pieces(base)
    zero = jnp.zeros_like(base)
    stack = jnp.concatenate([high, mid, high, low, high, mid, zero, zero, zero, zero], axis=0)
    return stack.astype(jnp.bfloat16)


def right_table(rows):
    high, mid, low = pieces(rows)
    zero = jnp.zeros_like(rows)
    stack = jnp.concatenate([zero] * 6 + [high, mid, low, zero], axis=0)
    return stack.astype(jnp.bfloat16)


def force_form(base, sub_index):
    high, mid, low = pieces(base)
    rest = jnp.where(sub_index < 3, mid, jnp.where(sub_index < 6, jnp.roll(low, 3, axis=0), 0.0))
    return jnp.concatenate([high, rest], axis=0).astype(jnp.bfloat16)


def cross(left, right):
    return lax.dot_general(left, right, (((0,), (0,)), ((), ())), preferred_element_type=jnp.float32)


def fold(value):
    return jnp.sum(value.reshape(TILE // SUB, SUB, TILE), axis=0)


def kernel(
    order,
    elements,
    shift,
    rho_store,
    depth_store,
    valence,
    atoms,
    out,
    left_base,
    right_base,
    onehot,
    rho_rows,
    coord,
    right_own,
    self_weight,
    total,
    energy,
    pulls,
    ranks,
    marks,
    firsts,
    second_cols,
    own_flat,
    work_flat,
    own_list,
    work_list,
    own_sem,
    head_sem,
    work_sem,
):
    payload = 5 * SUB
    slots = atoms.shape[0] // payload
    blocks_dev = SUB
    blocks = slots * blocks_dev
    flip = (row_part(order, lax.axis_index("row")) | col_part(order, lax.axis_index("col"))) * blocks_dev
    ones = jnp.ones((SUB, TILE), jnp.float32)
    zeros = jnp.zeros((SUB, TILE), jnp.float32)

    def put(ref, slot, row, value):
        ref[pl.ds((slot * blocks_dev + 1) * SUB + row, blocks_dev, stride=SUB), :] = value

    def prepare(slot, carry):
        start = pl.multiple_of(slot * payload, SUB)
        x = atoms[pl.ds(start, SUB), :]
        y = atoms[pl.ds(start + SUB, SUB), :]
        z = atoms[pl.ds(start + 2 * SUB, SUB), :]
        kind = atoms[pl.ds(start + 3 * SUB, SUB), :]
        square = x * x + y * y + z * z
        hot = [jnp.where(kind == float(t), 1.0, 0.0) for t in range(elements)]
        value = zeros
        for t in range(elements):
            value = value + hot[t] * valence[t]
        for row, item in enumerate((x, y, z, square, ones, value, zeros, zeros)):
            put(left_base, slot, row, item)
        for row, item in enumerate((-2.0 * x, -2.0 * y, -2.0 * z, ones, square, zeros, zeros, zeros)):
            put(right_base, slot, row, item)
        for row in range(SUB):
            put(onehot, slot, row, hot[row] if row < elements else zeros)
            if row < elements:
                mixed = hot[0] * rho_store[row * elements]
                for t in range(1, elements):
                    mixed = mixed + hot[t] * rho_store[row * elements + t]
            else:
                mixed = zeros
            put(rho_rows, slot, row, mixed)
        for block in range(blocks_dev):
            coord[slot * blocks_dev + block + 1] = zeros
        return carry

    lax.fori_loop(0, slots, prepare, 0)
    for ref in (left_base, right_base, onehot, rho_rows):
        ref[0:SUB, :] = zeros

    lane = lax.broadcasted_iota(jnp.int32, (TILE, TILE), 1)
    sublane = lax.broadcasted_iota(jnp.int32, (TILE, TILE), 0)
    before = jnp.where(sublane < lane, 1.0, 0.0).astype(jnp.bfloat16)
    slot_col = lax.broadcasted_iota(jnp.int32, (slots, slots), 1)
    slot_row = lax.broadcasted_iota(jnp.int32, (slots, slots), 0)
    above = jnp.where(slot_col < slot_row, 1.0, 0.0).astype(jnp.bfloat16)

    def meta(row):
        return atoms[pl.ds(4 * SUB + row, slots, stride=payload), :]

    first_all = (meta(0) + 256.0 * meta(1)).astype(jnp.int32) ^ flip
    live_all = meta(4)
    firsts[...] = first_all.astype(jnp.float32)

    def rank(mark):
        count = mark.astype(jnp.bfloat16)
        inside = jnp.dot(count, before, preferred_element_type=jnp.float32)
        earlier = jnp.dot(above, count, preferred_element_type=jnp.float32)
        place = inside + jnp.sum(earlier, axis=1, keepdims=True)
        ranks[...] = jnp.where(mark > 0.0, place, -1.0)
        return jnp.sum(mark).astype(jnp.int32)

    position = sublane.astype(jnp.float32)
    batch = min(slots, 4 * SUB)

    def compact(chunk, flat, columns):
        offset = jnp.float32(1.0) * (chunk * TILE)

        def some(group, carry):
            total = carry
            for part in range(batch // SUB):
                start = pl.multiple_of(group * batch + part * SUB, SUB)
                wanted = ranks[pl.ds(start, SUB), :] - offset
                picks = [
                    jnp.where(wanted[k : k + 1] == position, 1.0, 0.0).astype(jnp.bfloat16) for k in range(SUB)
                ]
                entries = [
                    atoms[pl.ds(pl.multiple_of((start + k) * payload + 4 * SUB, SUB), SUB), :].astype(
                        jnp.bfloat16
                    )
                    for k in range(SUB)
                ]
                total = total + lax.dot_general(
                    jnp.concatenate(entries, axis=1),
                    jnp.concatenate(picks, axis=1),
                    (((1,), (1,)), ((), ())),
                    preferred_element_type=jnp.float32,
                )
            return total

        row = lax.fori_loop(0, slots // batch, some, zeros)
        first = (row[0:1] + 256.0 * row[1:2]).astype(jnp.int32) ^ flip
        second = (row[2:3] + 256.0 * row[3:4]).astype(jnp.int32) ^ flip
        valid = row[4:5] > 0.0
        flat[pl.ds(chunk, 1), :] = jnp.where(valid, ((first + 1) << shift) | (second + 1), 0)
        if columns:
            target = jnp.where(valid, second, -1).astype(jnp.float32)
            column = jnp.transpose(jnp.broadcast_to(target, (SUB, TILE)))[:, 0:1]
            second_cols[...] = jnp.broadcast_to(column, (TILE, TILE))

    def send(source, target, group, semaphore):
        start = pl.multiple_of(group * SUB, SUB)
        return pltpu.make_async_copy(source.at[pl.ds(start, SUB)], target.at[pl.ds(start, SUB)], semaphore)

    def send_rest(source, target, count, semaphore):
        def one(group, carry):
            copy = send(source, target, group, semaphore)
            copy.start()
            copy.wait()
            return carry

        lax.fori_loop(1, (count + SUB * TILE - 1) // (SUB * TILE), one, 0)

    own_mark = jnp.where(first_all < blocks_dev, live_all, 0.0)
    marks[...] = own_mark
    own_count = rank(own_mark)

    def own_chunk(chunk, carry):
        compact(chunk, own_flat, True)
        part = 4 * SUB
        filled = jnp.minimum(own_count - chunk * TILE, TILE)

        def some(group, carry):
            cols = second_cols[pl.ds(pl.multiple_of(group * part, part), part), :]

            def rows(slot_group, carry):
                for piece in range(batch // SUB):
                    start = pl.multiple_of(slot_group * batch + piece * SUB, SUB)
                    here = firsts[pl.ds(start, SUB), :]
                    found = []
                    for k in range(SUB):
                        hit = jnp.where(cols == here[k : k + 1], 1.0, 0.0)
                        found.append(jnp.max(hit, axis=0, keepdims=True))
                    old = marks[pl.ds(start, SUB), :]
                    marks[pl.ds(start, SUB), :] = jnp.maximum(old, jnp.concatenate(found, axis=0))
                return carry

            return lax.fori_loop(0, slots // batch, rows, carry)

        lax.fori_loop(0, (filled + part - 1) // part, some, 0)
        return carry

    lax.fori_loop(0, (own_count + TILE - 1) // TILE, own_chunk, 0)
    send_rest(own_flat, own_list, own_count, own_sem)
    own_copy = send(own_flat, own_list, 0, own_sem)
    own_copy.start()

    work_count = rank(marks[...] * live_all)

    head_copy = pltpu.make_async_copy(work_flat.at[pl.ds(0, 1)], work_list.at[pl.ds(0, 1)], head_sem)
    compact(0, work_flat, False)
    head_copy.start()

    def work_chunk(chunk, carry):
        compact(chunk, work_flat, False)
        return carry

    lax.fori_loop(1, (work_count + TILE - 1) // TILE, work_chunk, 0)
    send_rest(work_flat, work_list, work_count, work_sem)
    rest_copy = pltpu.make_async_copy(
        work_flat.at[pl.ds(1, SUB - 1)], work_list.at[pl.ds(1, SUB - 1)], work_sem
    )
    rest_copy.start()
    head_copy.wait()
    own_copy.wait()

    def at(ref, block):
        return ref[pl.ds(pl.multiple_of(block * SUB, SUB), SUB), :]

    def fetch(ref, start):
        row = lax.shift_right_logical(start, TILE.bit_length() - 1)
        column = start & (TILE - 1)

        def at_step(step):
            code = ref[row, column + step]
            return code >> shift, code & ((1 << shift) - 1)

        return at_step

    def first_pass(start, size):
        pair = fetch(work_list, start)
        for step in range(size):
            first, second = pair(step)
            left = left_form(at(left_base, second), at(onehot, second))
            right = jnp.concatenate(
                [right_geometry(at(right_base, first)), right_table(at(rho_rows, first))], axis=1
            )
            both = cross(left, right)
            ratio = both[:, :TILE] * both[:, TILE:]
            bond = jnp.exp2(ratio * ratio * ratio)
            same = jnp.where(first == second, 1.0 / SUB, 0.0)
            coord[first] = coord[first] + (fold(bond) - same)

    fulls = work_count // LARGE
    early = TILE // LARGE

    def large(group, carry):
        first_pass(group * LARGE, LARGE)
        return carry

    def small(group, carry):
        first_pass(group * SMALL, SMALL)
        return carry

    lax.fori_loop(0, jnp.minimum(fulls, early), large, 0)
    rest_copy.wait()
    lax.fori_loop(jnp.minimum(fulls, early), fulls, large, 0)

    def middle(group, carry):
        first_pass(group * MIDDLE, MIDDLE)
        return carry

    edge = (work_count + MIDDLE - SMALL - 1) // MIDDLE
    lax.fori_loop(fulls * (LARGE // MIDDLE), edge, middle, 0)
    lax.fori_loop(edge * (MIDDLE // SMALL), (work_count + SMALL - 1) // SMALL, small, 0)

    sub_index = lax.broadcasted_iota(jnp.int32, (SUB, TILE), 0)

    for block in range(blocks_dev):
        base = at(left_base, block + 1)
        hot = at(onehot, block + 1)
        load = jnp.sum(coord[block + 1], axis=0, keepdims=True) + base[5:6]
        depth_rows = zeros
        for row in range(elements):
            mixed = hot[0:1] * depth_store[row * elements, 0:1]
            for t in range(1, elements):
                mixed = mixed + hot[t : t + 1] * depth_store[row * elements + t, 0:1]
            depth_rows = jnp.where(sub_index == row, mixed, depth_rows)
        load_rows = jnp.where(sub_index == 4, load, jnp.where(sub_index == 5, 1.0, 0.0))
        forms = [
            right_geometry(at(right_base, block + 1)),
            right_table(at(rho_rows, block + 1)),
            right_table(depth_rows),
            right_geometry(load_rows),
        ]
        alone = hot[0:1] * depth_store[0, 0:1]
        for t in range(1, elements):
            alone = alone + hot[t : t + 1] * depth_store[t * elements + t, 0:1]
        self_weight[block + 1] = jnp.where(sub_index == 0, alone / (load + load), 0.0)
        right_own[block + 1] = jnp.concatenate(forms, axis=1)
    self_weight[0] = zeros
    right_own[0] = jnp.zeros(right_own.shape[1:], jnp.bfloat16)
    for block in range(blocks_dev + 1):
        total[block] = jnp.zeros(total.shape[1:], jnp.float32)
        energy[block] = zeros

    def second_pass(start, size):
        pair = fetch(own_list, start)
        for step in range(size):
            first, second = pair(step)
            load = jnp.sum(coord[second], axis=0, keepdims=True)
            base = at(left_base, second)
            base = base + jnp.where(sub_index == 5, load, 0.0)
            left = left_form(base, at(onehot, second))
            mixed = cross(left, right_own[first])
            dist, rho, depth, both_load = [mixed[:, k * TILE : (k + 1) * TILE] for k in range(4)]
            ratio = dist * rho
            squared = ratio * ratio
            bond = jnp.exp2(squared * ratio)
            weight = depth * bond / both_load
            pull = weight * squared * rho
            pull_high = pull.astype(jnp.bfloat16)
            pulls[step, :, 0:TILE] = pull_high
            pulls[step, :, TILE:] = (pull - pull_high.astype(jnp.float32)).astype(jnp.bfloat16)
            same = jnp.where(first == second, 1.0, 0.0)
            energy[first] = energy[first] + (fold(weight) - same * self_weight[first])
        for step in range(size):
            first, second = pair(step)
            form = force_form(at(left_base, second), sub_index)
            total[first] = total[first] + jnp.dot(form, pulls[step], preferred_element_type=jnp.float32)

    def second_group(group, carry):
        second_pass(group * SMALL, SMALL)
        return carry

    def second_large(group, carry):
        second_pass(group * MIDDLE, MIDDLE)
        return carry

    middles = (own_count + MIDDLE - SMALL - 1) // MIDDLE
    lax.fori_loop(0, middles, second_large, 0)
    lax.fori_loop(middles * (MIDDLE // SMALL), (own_count + SMALL - 1) // SMALL, second_group, 0)

    for block in range(blocks_dev):
        both = total[block + 1]
        sums = both[:, :TILE] + both[:, TILE:]
        here = at(left_base, block + 1)
        lanes = slice(block * TILE, (block + 1) * TILE)
        for d in range(3):
            moment = sums[d : d + 1] + sums[8 + d : 9 + d] + sums[11 + d : 12 + d]
            out[d : d + 1, lanes] = (-6.0 / LOG2E) * (moment - here[d : d + 1] * sums[4:5])
        out[3:4, lanes] = -jnp.sum(energy[block + 1], axis=0, keepdims=True)


def local(order, positions, types, radius_type, valence_type, bond_depth, pair_tiles, tile_count):
    atom_dev = positions.shape[1]
    blocks_dev = atom_dev // TILE
    rows = lax.axis_size("row")
    cols = lax.axis_size("col")
    slots = rows * cols
    blocks = slots * blocks_dev
    tiles_dev = pair_tiles.shape[2]

    smem = pl.BlockSpec(memory_space=pltpu.SMEM)
    vmem = pl.BlockSpec(memory_space=pltpu.VMEM)
    packed = pl.pallas_call(
        functools.partial(pack, order),
        out_shape=pltpu.VMEM((5 * SUB, TILE), jnp.float32),
        in_specs=[smem, vmem, vmem, vmem],
        out_specs=vmem,
    )(tile_count, positions, types.reshape(blocks_dev, TILE), jnp.transpose(pair_tiles[0, 0]))
    elements = radius_type.shape[0]
    squares = (elements * elements, SUB, TILE)
    stores = pl.pallas_call(
        functools.partial(tables, elements),
        out_shape=(
            pltpu.VMEM(squares, jnp.float32),
            pltpu.VMEM(squares, jnp.float32),
            pltpu.VMEM((elements, SUB, TILE), jnp.float32),
        ),
        in_specs=[smem, smem, smem],
        out_specs=(vmem, vmem, vmem),
    )(radius_type, valence_type, bond_depth)

    gathered = packed
    for axis, bit in order:
        size = lax.axis_size(axis)
        other = lax.ppermute(gathered, axis, [(i, i ^ bit) for i in range(size)])
        gathered = jnp.concatenate([gathered, other], axis=0)

    gathered = pltpu.with_memory_space_constraint(gathered, pltpu.VMEM)
    stores = [pltpu.with_memory_space_constraint(store, pltpu.VMEM) for store in stores]
    shift = (blocks + 1).bit_length()
    chunks = -(-slots * tiles_dev // (SUB * TILE)) * SUB
    own_chunks = -(-cols * tiles_dev // (SUB * TILE)) * SUB
    return pl.pallas_call(
        functools.partial(kernel, order, elements, shift),
        out_shape=jax.ShapeDtypeStruct((4, atom_dev), jnp.float32),
        in_specs=[vmem, vmem, vmem, vmem],
        out_specs=vmem,
        scratch_shapes=[
            pltpu.VMEM((blocks * SUB + SUB, TILE), jnp.float32),
            pltpu.VMEM((blocks * SUB + SUB, TILE), jnp.float32),
            pltpu.VMEM((blocks * SUB + SUB, TILE), jnp.float32),
            pltpu.VMEM((blocks * SUB + SUB, TILE), jnp.float32),
            pltpu.VMEM((blocks + 1, SUB, TILE), jnp.float32),
            pltpu.VMEM((blocks_dev + 1, 10 * SUB, 4 * TILE), jnp.bfloat16),
            pltpu.VMEM((blocks_dev + 1, SUB, TILE), jnp.float32),
            pltpu.VMEM((blocks_dev + 1, 2 * SUB, 2 * TILE), jnp.float32),
            pltpu.VMEM((blocks_dev + 1, SUB, TILE), jnp.float32),
            pltpu.VMEM((MIDDLE, TILE, 2 * TILE), jnp.bfloat16),
            pltpu.VMEM((slots, TILE), jnp.float32),
            pltpu.VMEM((slots, TILE), jnp.float32),
            pltpu.VMEM((slots, TILE), jnp.float32),
            pltpu.VMEM((TILE, TILE), jnp.float32),
            pltpu.VMEM((own_chunks, TILE), jnp.int32),
            pltpu.VMEM((chunks, TILE), jnp.int32),
            pltpu.SMEM((own_chunks, TILE), jnp.int32),
            pltpu.SMEM((chunks, TILE), jnp.int32),
            pltpu.SemaphoreType.DMA,
            pltpu.SemaphoreType.DMA,
            pltpu.SemaphoreType.DMA,
        ],
        compiler_params=pltpu.CompilerParams(vmem_limit_bytes=56 * 1024 * 1024),
    )(*stores, gathered)


def solution(mesh):
    order = stage_bits(mesh.shape["col"], mesh.shape["row"])
    in_specs = (
        P(None, ("row", "col")),
        P(("row", "col")),
        P(),
        P(),
        P(),
        P("row", "col", None, None),
        P("row", "col"),
    )
    out_specs = P(None, ("row", "col"))
    return jax.shard_map(
        functools.partial(local, order), mesh=mesh, in_specs=in_specs, out_specs=out_specs, check_vma=False
    )
```

```python
import functools
import math

import jax
import jax.numpy as jnp
from jax import lax
from jax.experimental import pallas as pl
from jax.experimental.pallas import tpu as pltpu
from jax.sharding import PartitionSpec as P

TILE = 128
SUB = 8
LARGE = 64
MIDDLE = 16
SMALL = 8
LOG2E = math.log2(math.e)
SCALE = LOG2E ** (1.0 / 3.0)


def log2(size):
    return size.bit_length() - 1


def stage_bits(col_size, row_size):
    bits = [bit for bit in (col_size // 2, col_size // 4) if bit >= 2]
    return bits, col_size, row_size


def outer_part(order, col):
    total = col * 0
    for place, bit in enumerate(order[0]):
        total = total | (((col >> log2(bit)) & 1) << place)
    return total


def inner_part(order, col):
    bits, col_size, row_size = order
    return (col & ((col_size >> len(bits)) - 1)) << len(bits)


def row_part(order, row):
    return row << log2(order[1])


def col_part(order, col):
    return inner_part(order, col) | outer_part(order, col)


def pack(order, count, positions, types, tiles, packed):
    blocks_dev = types.shape[0]
    tiles_dev = tiles.shape[1]
    row = row_part(order, lax.axis_index("row"))
    col = col_part(order, lax.axis_index("col"))
    for d in range(3):
        for block in range(blocks_dev):
            place = d * blocks_dev + block
            packed[place : place + 1, :] = positions[d : d + 1, block * TILE : (block + 1) * TILE]
    packed[3 * blocks_dev : 4 * blocks_dev, :] = types[...].astype(jnp.float32)
    packed[4 * blocks_dev :, :] = jnp.zeros((SUB, TILE), jnp.float32)
    near, far = tiles[0:1, :], tiles[1:2, :]
    shift = blocks_dev.bit_length() - 1
    first = ((row | col_part(order, near >> shift)) << shift) | (near & (blocks_dev - 1))
    second = ((row_part(order, far >> shift) | col) << shift) | (far & (blocks_dev - 1))
    live = lax.broadcasted_iota(jnp.int32, (1, tiles_dev), 1) < count[0, 0]
    items = (first & 255, first >> 8, second & 255, second >> 8, jnp.where(live, 1, 0))
    for place, item in enumerate(items):
        start = 4 * blocks_dev + place
        packed[start : start + 1, 0:tiles_dev] = item.astype(jnp.float32)


def tables(elements, radius, valence, depth, rho_store, depth_store, valence_store):
    shape = (SUB, TILE)
    for t in range(elements):
        valence_store[t] = jnp.full(shape, valence[t], jnp.float32)
        for u in range(elements):
            rho = jnp.full(shape, 0.5 * (radius[t] + radius[u]), jnp.float32)
            rho_store[t * elements + u] = -SCALE / (rho * rho)
            depth_store[t * elements + u] = jnp.full(shape, depth[u, t] * (valence[u] + valence[t]), jnp.float32)


def pieces(value):
    high = value.astype(jnp.bfloat16).astype(jnp.float32)
    rest = value - high
    mid = rest.astype(jnp.bfloat16).astype(jnp.float32)
    return high, mid, rest - mid


def left_form(base, onehot):
    high, mid, low = pieces(base)
    zero = jnp.zeros_like(base)
    stack = jnp.concatenate([high, high, mid, high, low, mid, onehot, onehot, onehot, zero], axis=0)
    return stack.astype(jnp.bfloat16)


def right_geometry(base):
    high, mid, low = pieces(base)
    zero = jnp.zeros_like(base)
    stack = jnp.concatenate([high, mid, high, low, high, mid, zero, zero, zero, zero], axis=0)
    return stack.astype(jnp.bfloat16)


def right_table(rows):
    high, mid, low = pieces(rows)
    zero = jnp.zeros_like(rows)
    stack = jnp.concatenate([zero] * 6 + [high, mid, low, zero], axis=0)
    return stack.astype(jnp.bfloat16)


def force_form(base, sub_index):
    high, mid, low = pieces(base)
    rest = jnp.where(sub_index < 3, mid, jnp.where(sub_index < 6, jnp.roll(low, 3, axis=0), 0.0))
    return jnp.concatenate([high, rest], axis=0).astype(jnp.bfloat16)


def cross(left, right):
    return lax.dot_general(left, right, (((0,), (0,)), ((), ())), preferred_element_type=jnp.float32)


def fold(value):
    return jnp.sum(value.reshape(TILE // SUB, SUB, TILE), axis=0)


def kernel(
    order,
    elements,
    shift,
    rho_store,
    depth_store,
    valence,
    atoms,
    out,
    left_base,
    right_base,
    onehot,
    rho_rows,
    coord,
    right_own,
    self_weight,
    total,
    energy,
    pulls,
    ranks,
    marks,
    firsts,
    second_cols,
    own_flat,
    work_flat,
    own_list,
    work_list,
    own_sem,
    head_sem,
    work_sem,
):
    payload = 5 * SUB
    slots = atoms.shape[0] // payload
    blocks_dev = SUB
    blocks = slots * blocks_dev
    flip = outer_part(order, lax.axis_index("col")) * blocks_dev
    own_slot = row_part(order, lax.axis_index("row")) | inner_part(order, lax.axis_index("col"))
    own_base = own_slot * blocks_dev
    ones = jnp.ones((SUB, TILE), jnp.float32)
    zeros = jnp.zeros((SUB, TILE), jnp.float32)

    def put(ref, slot, row, value):
        ref[pl.ds((slot * blocks_dev + 1) * SUB + row, blocks_dev, stride=SUB), :] = value

    def prepare(slot, carry):
        start = pl.multiple_of(slot * payload, SUB)
        x = atoms[pl.ds(start, SUB), :]
        y = atoms[pl.ds(start + SUB, SUB), :]
        z = atoms[pl.ds(start + 2 * SUB, SUB), :]
        kind = atoms[pl.ds(start + 3 * SUB, SUB), :]
        square = x * x + y * y + z * z
        hot = [jnp.where(kind == float(t), 1.0, 0.0) for t in range(elements)]
        value = zeros
        for t in range(elements):
            value = value + hot[t] * valence[t]
        for row, item in enumerate((x, y, z, square, ones, value, zeros, zeros)):
            put(left_base, slot, row, item)
        for row, item in enumerate((-2.0 * x, -2.0 * y, -2.0 * z, ones, square, zeros, zeros, zeros)):
            put(right_base, slot, row, item)
        for row in range(SUB):
            put(onehot, slot, row, hot[row] if row < elements else zeros)
            if row < elements:
                mixed = hot[0] * rho_store[row * elements]
                for t in range(1, elements):
                    mixed = mixed + hot[t] * rho_store[row * elements + t]
            else:
                mixed = zeros
            put(rho_rows, slot, row, mixed)
        for block in range(blocks_dev):
            coord[slot * blocks_dev + block + 1] = zeros
        return carry

    lax.fori_loop(0, slots, prepare, 0)
    for ref in (left_base, right_base, onehot, rho_rows):
        ref[0:SUB, :] = zeros

    lane = lax.broadcasted_iota(jnp.int32, (TILE, TILE), 1)
    sublane = lax.broadcasted_iota(jnp.int32, (TILE, TILE), 0)
    before = jnp.where(sublane < lane, 1.0, 0.0).astype(jnp.bfloat16)
    slot_col = lax.broadcasted_iota(jnp.int32, (slots, slots), 1)
    slot_row = lax.broadcasted_iota(jnp.int32, (slots, slots), 0)
    above = jnp.where(slot_col < slot_row, 1.0, 0.0).astype(jnp.bfloat16)

    def meta(row):
        return atoms[pl.ds(4 * SUB + row, slots, stride=payload), :]

    first_all = (meta(0) + 256.0 * meta(1)).astype(jnp.int32) ^ flip
    live_all = meta(4)
    firsts[...] = first_all.astype(jnp.float32)

    def rank(mark):
        count = mark.astype(jnp.bfloat16)
        inside = jnp.dot(count, before, preferred_element_type=jnp.float32)
        earlier = jnp.dot(above, count, preferred_element_type=jnp.float32)
        place = inside + jnp.sum(earlier, axis=1, keepdims=True)
        ranks[...] = jnp.where(mark > 0.0, place, -1.0)
        return jnp.sum(mark).astype(jnp.int32)

    position = sublane.astype(jnp.float32)
    batch = min(slots, 4 * SUB)

    def compact(chunk, flat, columns):
        offset = jnp.float32(1.0) * (chunk * TILE)

        def some(group, carry):
            total = carry
            for part in range(batch // SUB):
                start = pl.multiple_of(group * batch + part * SUB, SUB)
                wanted = ranks[pl.ds(start, SUB), :] - offset
                picks = [
                    jnp.where(wanted[k : k + 1] == position, 1.0, 0.0).astype(jnp.bfloat16) for k in range(SUB)
                ]
                entries = [
                    atoms[pl.ds(pl.multiple_of((start + k) * payload + 4 * SUB, SUB), SUB), :].astype(
                        jnp.bfloat16
                    )
                    for k in range(SUB)
                ]
                total = total + lax.dot_general(
                    jnp.concatenate(entries, axis=1),
                    jnp.concatenate(picks, axis=1),
                    (((1,), (1,)), ((), ())),
                    preferred_element_type=jnp.float32,
                )
            return total

        row = lax.fori_loop(0, slots // batch, some, zeros)
        first = (row[0:1] + 256.0 * row[1:2]).astype(jnp.int32) ^ flip
        second = (row[2:3] + 256.0 * row[3:4]).astype(jnp.int32) ^ flip
        valid = row[4:5] > 0.0
        flat[pl.ds(chunk, 1), :] = jnp.where(valid, ((first + 1) << shift) | (second + 1), 0)
        if columns:
            target = jnp.where(valid, second, -1).astype(jnp.float32)
            column = jnp.transpose(jnp.broadcast_to(target, (SUB, TILE)))[:, 0:1]
            second_cols[...] = jnp.broadcast_to(column, (TILE, TILE))

    def send(source, target, group, semaphore):
        start = pl.multiple_of(group * SUB, SUB)
        return pltpu.make_async_copy(source.at[pl.ds(start, SUB)], target.at[pl.ds(start, SUB)], semaphore)

    def send_rest(source, target, count, semaphore):
        def one(group, carry):
            copy = send(source, target, group, semaphore)
            copy.start()
            copy.wait()
            return carry

        lax.fori_loop(1, (count + SUB * TILE - 1) // (SUB * TILE), one, 0)

    own_mark = jnp.where((first_all >> log2(blocks_dev)) == own_slot, live_all, 0.0)
    marks[...] = own_mark
    own_count = rank(own_mark)

    def own_chunk(chunk, carry):
        compact(chunk, own_flat, True)
        part = 4 * SUB
        filled = jnp.minimum(own_count - chunk * TILE, TILE)

        def some(group, carry):
            cols = second_cols[pl.ds(pl.multiple_of(group * part, part), part), :]

            def rows(slot_group, carry):
                for piece in range(batch // SUB):
                    start = pl.multiple_of(slot_group * batch + piece * SUB, SUB)
                    here = firsts[pl.ds(start, SUB), :]
                    found = []
                    for k in range(SUB):
                        hit = jnp.where(cols == here[k : k + 1], 1.0, 0.0)
                        found.append(jnp.max(hit, axis=0, keepdims=True))
                    old = marks[pl.ds(start, SUB), :]
                    marks[pl.ds(start, SUB), :] = jnp.maximum(old, jnp.concatenate(found, axis=0))
                return carry

            return lax.fori_loop(0, slots // batch, rows, carry)

        lax.fori_loop(0, (filled + part - 1) // part, some, 0)
        return carry

    lax.fori_loop(0, (own_count + TILE - 1) // TILE, own_chunk, 0)
    send_rest(own_flat, own_list, own_count, own_sem)
    own_copy = send(own_flat, own_list, 0, own_sem)
    own_copy.start()

    work_count = rank(marks[...] * live_all)

    head_copy = pltpu.make_async_copy(work_flat.at[pl.ds(0, 1)], work_list.at[pl.ds(0, 1)], head_sem)
    compact(0, work_flat, False)
    head_copy.start()

    def work_chunk(chunk, carry):
        compact(chunk, work_flat, False)
        return carry

    lax.fori_loop(1, (work_count + TILE - 1) // TILE, work_chunk, 0)
    send_rest(work_flat, work_list, work_count, work_sem)
    rest_copy = pltpu.make_async_copy(
        work_flat.at[pl.ds(1, SUB - 1)], work_list.at[pl.ds(1, SUB - 1)], work_sem
    )
    rest_copy.start()
    head_copy.wait()
    own_copy.wait()

    def at(ref, block):
        return ref[pl.ds(pl.multiple_of(block * SUB, SUB), SUB), :]

    def fetch(ref, start):
        row = lax.shift_right_logical(start, TILE.bit_length() - 1)
        column = start & (TILE - 1)

        def at_step(step):
            code = ref[row, column + step]
            return code >> shift, code & ((1 << shift) - 1)

        return at_step

    def first_pass(start, size):
        pair = fetch(work_list, start)
        for step in range(size):
            first, second = pair(step)
            left = left_form(at(left_base, second), at(onehot, second))
            right = jnp.concatenate(
                [right_geometry(at(right_base, first)), right_table(at(rho_rows, first))], axis=1
            )
            both = cross(left, right)
            ratio = both[:, :TILE] * both[:, TILE:]
            bond = jnp.exp2(ratio * ratio * ratio)
            same = jnp.where(first == second, 1.0 / SUB, 0.0)
            coord[first] = coord[first] + (fold(bond) - same)

    fulls = work_count // LARGE
    early = TILE // LARGE

    def large(group, carry):
        first_pass(group * LARGE, LARGE)
        return carry

    def small(group, carry):
        first_pass(group * SMALL, SMALL)
        return carry

    lax.fori_loop(0, jnp.minimum(fulls, early), large, 0)
    rest_copy.wait()
    lax.fori_loop(jnp.minimum(fulls, early), fulls, large, 0)

    def middle(group, carry):
        first_pass(group * MIDDLE, MIDDLE)
        return carry

    edge = (work_count + MIDDLE - SMALL - 1) // MIDDLE
    lax.fori_loop(fulls * (LARGE // MIDDLE), edge, middle, 0)
    lax.fori_loop(edge * (MIDDLE // SMALL), (work_count + SMALL - 1) // SMALL, small, 0)

    sub_index = lax.broadcasted_iota(jnp.int32, (SUB, TILE), 0)

    for block in range(blocks_dev):
        place = own_base + block + 1
        base = at(left_base, place)
        hot = at(onehot, place)
        load = jnp.sum(coord[place], axis=0, keepdims=True) + base[5:6]
        depth_rows = zeros
        for row in range(elements):
            mixed = hot[0:1] * depth_store[row * elements, 0:1]
            for t in range(1, elements):
                mixed = mixed + hot[t : t + 1] * depth_store[row * elements + t, 0:1]
            depth_rows = jnp.where(sub_index == row, mixed, depth_rows)
        load_rows = jnp.where(sub_index == 4, load, jnp.where(sub_index == 5, 1.0, 0.0))
        forms = [
            right_geometry(at(right_base, place)),
            right_table(at(rho_rows, place)),
            right_table(depth_rows),
            right_geometry(load_rows),
        ]
        alone = hot[0:1] * depth_store[0, 0:1]
        for t in range(1, elements):
            alone = alone + hot[t : t + 1] * depth_store[t * elements + t, 0:1]
        self_weight[block + 1] = jnp.where(sub_index == 0, alone / (load + load), 0.0)
        right_own[block + 1] = jnp.concatenate(forms, axis=1)
    self_weight[0] = zeros
    right_own[0] = jnp.zeros(right_own.shape[1:], jnp.bfloat16)
    for block in range(blocks_dev + 1):
        total[block] = jnp.zeros(total.shape[1:], jnp.float32)
        energy[block] = zeros

    def second_pass(start, size):
        pair = fetch(own_list, start)
        for step in range(size):
            first, second = pair(step)
            load = jnp.sum(coord[second], axis=0, keepdims=True)
            base = at(left_base, second)
            base = base + jnp.where(sub_index == 5, load, 0.0)
            left = left_form(base, at(onehot, second))
            local_first = jnp.maximum(first - own_base, 0)
            mixed = cross(left, right_own[local_first])
            dist, rho, depth, both_load = [mixed[:, k * TILE : (k + 1) * TILE] for k in range(4)]
            ratio = dist * rho
            squared = ratio * ratio
            bond = jnp.exp2(squared * ratio)
            weight = depth * bond / both_load
            pull = weight * squared * rho
            pull_high = pull.astype(jnp.bfloat16)
            pulls[step, :, 0:TILE] = pull_high
            pulls[step, :, TILE:] = (pull - pull_high.astype(jnp.float32)).astype(jnp.bfloat16)
            same = jnp.where(first == second, 1.0, 0.0)
            update = fold(weight) - same * self_weight[local_first]
            energy[local_first] = energy[local_first] + update
        for step in range(size):
            first, second = pair(step)
            form = force_form(at(left_base, second), sub_index)
            sums = jnp.dot(form, pulls[step], preferred_element_type=jnp.float32)
            local_first = jnp.maximum(first - own_base, 0)
            total[local_first] = total[local_first] + sums

    def second_group(group, carry):
        second_pass(group * SMALL, SMALL)
        return carry

    def second_large(group, carry):
        second_pass(group * MIDDLE, MIDDLE)
        return carry

    middles = (own_count + MIDDLE - SMALL - 1) // MIDDLE
    lax.fori_loop(0, middles, second_large, 0)
    lax.fori_loop(middles * (MIDDLE // SMALL), (own_count + SMALL - 1) // SMALL, second_group, 0)

    for block in range(blocks_dev):
        both = total[block + 1]
        sums = both[:, :TILE] + both[:, TILE:]
        here = at(left_base, own_base + block + 1)
        lanes = slice(block * TILE, (block + 1) * TILE)
        for d in range(3):
            moment = sums[d : d + 1] + sums[8 + d : 9 + d] + sums[11 + d : 12 + d]
            out[d : d + 1, lanes] = (-6.0 / LOG2E) * (moment - here[d : d + 1] * sums[4:5])
        out[3:4, lanes] = -jnp.sum(energy[block + 1], axis=0, keepdims=True)


def local(order, positions, types, radius_type, valence_type, bond_depth, pair_tiles, tile_count):
    atom_dev = positions.shape[1]
    blocks_dev = atom_dev // TILE
    rows = lax.axis_size("row")
    cols = lax.axis_size("col")
    slots = rows * cols
    blocks = slots * blocks_dev
    tiles_dev = pair_tiles.shape[2]

    smem = pl.BlockSpec(memory_space=pltpu.SMEM)
    vmem = pl.BlockSpec(memory_space=pltpu.VMEM)
    packed = pl.pallas_call(
        functools.partial(pack, order),
        out_shape=pltpu.VMEM((5 * SUB, TILE), jnp.float32),
        in_specs=[smem, vmem, vmem, vmem],
        out_specs=vmem,
    )(tile_count, positions, types.reshape(blocks_dev, TILE), jnp.transpose(pair_tiles[0, 0]))
    elements = radius_type.shape[0]
    squares = (elements * elements, SUB, TILE)
    stores = pl.pallas_call(
        functools.partial(tables, elements),
        out_shape=(
            pltpu.VMEM(squares, jnp.float32),
            pltpu.VMEM(squares, jnp.float32),
            pltpu.VMEM((elements, SUB, TILE), jnp.float32),
        ),
        in_specs=[smem, smem, smem],
        out_specs=(vmem, vmem, vmem),
    )(radius_type, valence_type, bond_depth)

    gathered = packed
    for bit in order[0]:
        other = lax.ppermute(gathered, "col", [(i, i ^ bit) for i in range(cols)])
        gathered = jnp.concatenate([gathered, other], axis=0)
    inner = cols >> len(order[0])
    groups = [
        [row * cols + start + k for row in range(rows) for k in range(inner)] for start in range(0, cols, inner)
    ]
    gathered = lax.all_gather(gathered, ("row", "col"), axis=0, axis_index_groups=groups, tiled=True)

    gathered = pltpu.with_memory_space_constraint(gathered, pltpu.VMEM)
    stores = [pltpu.with_memory_space_constraint(store, pltpu.VMEM) for store in stores]
    shift = (blocks + 1).bit_length()
    chunks = -(-slots * tiles_dev // (SUB * TILE)) * SUB
    own_chunks = -(-cols * tiles_dev // (SUB * TILE)) * SUB
    return pl.pallas_call(
        functools.partial(kernel, order, elements, shift),
        out_shape=jax.ShapeDtypeStruct((4, atom_dev), jnp.float32),
        in_specs=[vmem, vmem, vmem, vmem],
        out_specs=vmem,
        scratch_shapes=[
            pltpu.VMEM((blocks * SUB + SUB, TILE), jnp.float32),
            pltpu.VMEM((blocks * SUB + SUB, TILE), jnp.float32),
            pltpu.VMEM((blocks * SUB + SUB, TILE), jnp.float32),
            pltpu.VMEM((blocks * SUB + SUB, TILE), jnp.float32),
            pltpu.VMEM((blocks + 1, SUB, TILE), jnp.float32),
            pltpu.VMEM((blocks_dev + 1, 10 * SUB, 4 * TILE), jnp.bfloat16),
            pltpu.VMEM((blocks_dev + 1, SUB, TILE), jnp.float32),
            pltpu.VMEM((blocks_dev + 1, 2 * SUB, 2 * TILE), jnp.float32),
            pltpu.VMEM((blocks_dev + 1, SUB, TILE), jnp.float32),
            pltpu.VMEM((MIDDLE, TILE, 2 * TILE), jnp.bfloat16),
            pltpu.VMEM((slots, TILE), jnp.float32),
            pltpu.VMEM((slots, TILE), jnp.float32),
            pltpu.VMEM((slots, TILE), jnp.float32),
            pltpu.VMEM((TILE, TILE), jnp.float32),
            pltpu.VMEM((own_chunks, TILE), jnp.int32),
            pltpu.VMEM((chunks, TILE), jnp.int32),
            pltpu.SMEM((own_chunks, TILE), jnp.int32),
            pltpu.SMEM((chunks, TILE), jnp.int32),
            pltpu.SemaphoreType.DMA,
            pltpu.SemaphoreType.DMA,
            pltpu.SemaphoreType.DMA,
        ],
        compiler_params=pltpu.CompilerParams(vmem_limit_bytes=56 * 1024 * 1024),
    )(*stores, gathered)


def solution(mesh):
    order = stage_bits(mesh.shape["col"], mesh.shape["row"])
    in_specs = (
        P(None, ("row", "col")),
        P(("row", "col")),
        P(),
        P(),
        P(),
        P("row", "col", None, None),
        P("row", "col"),
    )
    out_specs = P(None, ("row", "col"))
    return jax.shard_map(
        functools.partial(local, order), mesh=mesh, in_specs=in_specs, out_specs=out_specs, check_vma=False
    )
```

```python
import functools
import math

import jax
import jax.numpy as jnp
from jax import lax
from jax.experimental import pallas as pl
from jax.experimental.pallas import tpu as pltpu
from jax.sharding import PartitionSpec as P

TILE = 128
SUB = 8
LARGE = 64
MIDDLE = 32
SMALL = 8
LOG2E = math.log2(math.e)
SCALE = LOG2E ** (1.0 / 3.0)


def log2(size):
    return size.bit_length() - 1


def stage_bits(col_size, row_size):
    bits = [bit for bit in (col_size // 2, col_size // 4) if bit >= 2]
    return bits, col_size, row_size


def outer_part(order, col):
    total = col * 0
    for place, bit in enumerate(order[0]):
        total = total | (((col >> log2(bit)) & 1) << place)
    return total


def inner_part(order, col):
    bits, col_size, row_size = order
    return (col & ((col_size >> len(bits)) - 1)) << len(bits)


def row_part(order, row):
    return row << log2(order[1])


def col_part(order, col):
    return inner_part(order, col) | outer_part(order, col)


def pack(order, count, positions, types, tiles, packed):
    blocks_dev = types.shape[0]
    tiles_dev = tiles.shape[1]
    row = row_part(order, lax.axis_index("row"))
    col = col_part(order, lax.axis_index("col"))
    for d in range(3):
        for block in range(blocks_dev):
            place = d * blocks_dev + block
            packed[place : place + 1, :] = positions[d : d + 1, block * TILE : (block + 1) * TILE]
    packed[3 * blocks_dev : 4 * blocks_dev, :] = types[...].astype(jnp.float32)
    packed[4 * blocks_dev :, :] = jnp.zeros((SUB, TILE), jnp.float32)
    near, far = tiles[0:1, :], tiles[1:2, :]
    shift = blocks_dev.bit_length() - 1
    first = ((row | col_part(order, near >> shift)) << shift) | (near & (blocks_dev - 1))
    second = ((row_part(order, far >> shift) | col) << shift) | (far & (blocks_dev - 1))
    live = lax.broadcasted_iota(jnp.int32, (1, tiles_dev), 1) < count[0, 0]
    items = (first & 255, first >> 8, second & 255, second >> 8, jnp.where(live, 1, 0))
    for place, item in enumerate(items):
        start = 4 * blocks_dev + place
        packed[start : start + 1, 0:tiles_dev] = item.astype(jnp.float32)


def tables(elements, radius, valence, depth, rho_store, depth_store, valence_store):
    shape = (SUB, TILE)
    for t in range(elements):
        valence_store[t] = jnp.full(shape, valence[t], jnp.float32)
        for u in range(elements):
            rho = jnp.full(shape, 0.5 * (radius[t] + radius[u]), jnp.float32)
            rho_store[t * elements + u] = -SCALE / (rho * rho)
            depth_store[t * elements + u] = jnp.full(shape, depth[u, t] * (valence[u] + valence[t]), jnp.float32)


def pieces(value):
    high = value.astype(jnp.bfloat16).astype(jnp.float32)
    rest = value - high
    mid = rest.astype(jnp.bfloat16).astype(jnp.float32)
    return high, mid, rest - mid


def left_form(base, onehot):
    high, mid, low = pieces(base)
    zero = jnp.zeros_like(base)
    stack = jnp.concatenate([high, high, mid, high, low, mid, onehot, onehot, onehot, zero], axis=0)
    return stack.astype(jnp.bfloat16)


def right_geometry(base):
    high, mid, low = pieces(base)
    zero = jnp.zeros_like(base)
    stack = jnp.concatenate([high, mid, high, low, high, mid, zero, zero, zero, zero], axis=0)
    return stack.astype(jnp.bfloat16)


def right_table(rows):
    high, mid, low = pieces(rows)
    zero = jnp.zeros_like(rows)
    stack = jnp.concatenate([zero] * 6 + [high, mid, low, zero], axis=0)
    return stack.astype(jnp.bfloat16)


def force_form(base, sub_index):
    high, mid, low = pieces(base)
    rest = jnp.where(sub_index < 3, mid, jnp.where(sub_index < 6, jnp.roll(low, 3, axis=0), 0.0))
    return jnp.concatenate([high, rest], axis=0).astype(jnp.bfloat16)


def cross(left, right):
    return lax.dot_general(left, right, (((0,), (0,)), ((), ())), preferred_element_type=jnp.float32)


def fold(value):
    return jnp.sum(value.reshape(TILE // SUB, SUB, TILE), axis=0)


def kernel(
    order,
    elements,
    shift,
    rho_store,
    depth_store,
    valence,
    atoms,
    out,
    left_base,
    right_base,
    onehot,
    rho_rows,
    coord,
    right_own,
    self_weight,
    total,
    energy,
    pulls,
    ranks,
    marks,
    firsts,
    second_cols,
    own_flat,
    work_flat,
    own_list,
    work_list,
    own_sem,
    head_sem,
    work_sem,
):
    payload = 5 * SUB
    slots = atoms.shape[0] // payload
    blocks_dev = SUB
    blocks = slots * blocks_dev
    flip = outer_part(order, lax.axis_index("col")) * blocks_dev
    own_slot = row_part(order, lax.axis_index("row")) | inner_part(order, lax.axis_index("col"))
    own_base = own_slot * blocks_dev
    ones = jnp.ones((SUB, TILE), jnp.float32)
    zeros = jnp.zeros((SUB, TILE), jnp.float32)

    def put(ref, slot, row, value):
        ref[pl.ds((slot * blocks_dev + 1) * SUB + row, blocks_dev, stride=SUB), :] = value

    def prepare(slot, carry):
        start = pl.multiple_of(slot * payload, SUB)
        x = atoms[pl.ds(start, SUB), :]
        y = atoms[pl.ds(start + SUB, SUB), :]
        z = atoms[pl.ds(start + 2 * SUB, SUB), :]
        kind = atoms[pl.ds(start + 3 * SUB, SUB), :]
        square = x * x + y * y + z * z
        hot = [jnp.where(kind == float(t), 1.0, 0.0) for t in range(elements)]
        value = zeros
        for t in range(elements):
            value = value + hot[t] * valence[t]
        for row, item in enumerate((x, y, z, square, ones, value, zeros, zeros)):
            put(left_base, slot, row, item)
        for row, item in enumerate((-2.0 * x, -2.0 * y, -2.0 * z, ones, square, zeros, zeros, zeros)):
            put(right_base, slot, row, item)
        for row in range(SUB):
            put(onehot, slot, row, hot[row] if row < elements else zeros)
            if row < elements:
                mixed = hot[0] * rho_store[row * elements]
                for t in range(1, elements):
                    mixed = mixed + hot[t] * rho_store[row * elements + t]
            else:
                mixed = zeros
            put(rho_rows, slot, row, mixed)
        for block in range(blocks_dev):
            coord[slot * blocks_dev + block + 1] = zeros
        return carry

    lax.fori_loop(0, slots, prepare, 0)
    for ref in (left_base, right_base, onehot, rho_rows):
        ref[0:SUB, :] = zeros

    lane = lax.broadcasted_iota(jnp.int32, (TILE, TILE), 1)
    sublane = lax.broadcasted_iota(jnp.int32, (TILE, TILE), 0)
    before = jnp.where(sublane < lane, 1.0, 0.0).astype(jnp.bfloat16)
    slot_col = lax.broadcasted_iota(jnp.int32, (slots, slots), 1)
    slot_row = lax.broadcasted_iota(jnp.int32, (slots, slots), 0)
    above = jnp.where(slot_col < slot_row, 1.0, 0.0).astype(jnp.bfloat16)

    def meta(row):
        return atoms[pl.ds(4 * SUB + row, slots, stride=payload), :]

    first_all = (meta(0) + 256.0 * meta(1)).astype(jnp.int32) ^ flip
    live_all = meta(4)
    firsts[...] = first_all.astype(jnp.float32)

    def rank(mark):
        count = mark.astype(jnp.bfloat16)
        inside = jnp.dot(count, before, preferred_element_type=jnp.float32)
        earlier = jnp.dot(above, count, preferred_element_type=jnp.float32)
        place = inside + jnp.sum(earlier, axis=1, keepdims=True)
        ranks[...] = jnp.where(mark > 0.0, place, -1.0)
        return jnp.sum(mark).astype(jnp.int32)

    position = sublane.astype(jnp.float32)
    batch = min(slots, 4 * SUB)

    def compact(chunk, flat, columns):
        offset = jnp.float32(1.0) * (chunk * TILE)

        def some(group, carry):
            total = carry
            for part in range(batch // SUB):
                start = pl.multiple_of(group * batch + part * SUB, SUB)
                wanted = ranks[pl.ds(start, SUB), :] - offset
                picks = [
                    jnp.where(wanted[k : k + 1] == position, 1.0, 0.0).astype(jnp.bfloat16) for k in range(SUB)
                ]
                entries = [
                    atoms[pl.ds(pl.multiple_of((start + k) * payload + 4 * SUB, SUB), SUB), :].astype(
                        jnp.bfloat16
                    )
                    for k in range(SUB)
                ]
                total = total + lax.dot_general(
                    jnp.concatenate(entries, axis=1),
                    jnp.concatenate(picks, axis=1),
                    (((1,), (1,)), ((), ())),
                    preferred_element_type=jnp.float32,
                )
            return total

        row = lax.fori_loop(0, slots // batch, some, zeros)
        first = (row[0:1] + 256.0 * row[1:2]).astype(jnp.int32) ^ flip
        second = (row[2:3] + 256.0 * row[3:4]).astype(jnp.int32) ^ flip
        valid = row[4:5] > 0.0
        flat[pl.ds(chunk, 1), :] = jnp.where(valid, ((first + 1) << shift) | (second + 1), 0)
        if columns:
            target = jnp.where(valid, second, -1).astype(jnp.float32)
            column = jnp.transpose(jnp.broadcast_to(target, (SUB, TILE)))[:, 0:1]
            second_cols[...] = jnp.broadcast_to(column, (TILE, TILE))

    def send(source, target, group, semaphore):
        start = pl.multiple_of(group * SUB, SUB)
        return pltpu.make_async_copy(source.at[pl.ds(start, SUB)], target.at[pl.ds(start, SUB)], semaphore)

    def send_rest(source, target, count, semaphore):
        def one(group, carry):
            copy = send(source, target, group, semaphore)
            copy.start()
            copy.wait()
            return carry

        lax.fori_loop(1, (count + SUB * TILE - 1) // (SUB * TILE), one, 0)

    own_mark = jnp.where((first_all >> log2(blocks_dev)) == own_slot, live_all, 0.0)
    marks[...] = own_mark
    own_count = rank(own_mark)

    def own_chunk(chunk, carry):
        compact(chunk, own_flat, True)
        part = 4 * SUB
        filled = jnp.minimum(own_count - chunk * TILE, TILE)

        def some(group, carry):
            cols = second_cols[pl.ds(pl.multiple_of(group * part, part), part), :]

            def rows(slot_group, carry):
                for piece in range(batch // SUB):
                    start = pl.multiple_of(slot_group * batch + piece * SUB, SUB)
                    here = firsts[pl.ds(start, SUB), :]
                    found = []
                    for k in range(SUB):
                        hit = jnp.where(cols == here[k : k + 1], 1.0, 0.0)
                        found.append(jnp.max(hit, axis=0, keepdims=True))
                    old = marks[pl.ds(start, SUB), :]
                    marks[pl.ds(start, SUB), :] = jnp.maximum(old, jnp.concatenate(found, axis=0))
                return carry

            return lax.fori_loop(0, slots // batch, rows, carry)

        lax.fori_loop(0, (filled + part - 1) // part, some, 0)
        return carry

    lax.fori_loop(0, (own_count + TILE - 1) // TILE, own_chunk, 0)
    send_rest(own_flat, own_list, own_count, own_sem)
    own_copy = send(own_flat, own_list, 0, own_sem)
    own_copy.start()

    work_count = rank(marks[...] * live_all)

    head_copy = pltpu.make_async_copy(work_flat.at[pl.ds(0, 1)], work_list.at[pl.ds(0, 1)], head_sem)
    compact(0, work_flat, False)
    head_copy.start()

    def work_chunk(chunk, carry):
        compact(chunk, work_flat, False)
        return carry

    lax.fori_loop(1, (work_count + TILE - 1) // TILE, work_chunk, 0)
    send_rest(work_flat, work_list, work_count, work_sem)
    rest_copy = pltpu.make_async_copy(
        work_flat.at[pl.ds(1, SUB - 1)], work_list.at[pl.ds(1, SUB - 1)], work_sem
    )
    rest_copy.start()
    head_copy.wait()
    own_copy.wait()

    def at(ref, block):
        return ref[pl.ds(pl.multiple_of(block * SUB, SUB), SUB), :]

    def fetch(ref, start):
        row = lax.shift_right_logical(start, TILE.bit_length() - 1)
        column = start & (TILE - 1)

        def at_step(step):
            code = ref[row, column + step]
            return code >> shift, code & ((1 << shift) - 1)

        return at_step

    def first_pass(start, size):
        pair = fetch(work_list, start)
        for step in range(size):
            first, second = pair(step)
            left = left_form(at(left_base, second), at(onehot, second))
            right = jnp.concatenate(
                [right_geometry(at(right_base, first)), right_table(at(rho_rows, first))], axis=1
            )
            both = cross(left, right)
            ratio = both[:, :TILE] * both[:, TILE:]
            bond = jnp.exp2(ratio * ratio * ratio)
            same = jnp.where(first == second, 1.0 / SUB, 0.0)
            coord[first] = coord[first] + (fold(bond) - same)

    fulls = work_count // LARGE
    early = TILE // LARGE

    def large(group, carry):
        first_pass(group * LARGE, LARGE)
        return carry

    def small(group, carry):
        first_pass(group * SMALL, SMALL)
        return carry

    lax.fori_loop(0, jnp.minimum(fulls, early), large, 0)
    rest_copy.wait()
    lax.fori_loop(jnp.minimum(fulls, early), fulls, large, 0)

    def middle(group, carry):
        first_pass(group * MIDDLE, MIDDLE)
        return carry

    edge = (work_count + MIDDLE - SMALL - 1) // MIDDLE
    lax.fori_loop(fulls * (LARGE // MIDDLE), edge, middle, 0)
    lax.fori_loop(edge * (MIDDLE // SMALL), (work_count + SMALL - 1) // SMALL, small, 0)

    sub_index = lax.broadcasted_iota(jnp.int32, (SUB, TILE), 0)

    for block in range(blocks_dev):
        place = own_base + block + 1
        base = at(left_base, place)
        hot = at(onehot, place)
        load = jnp.sum(coord[place], axis=0, keepdims=True) + base[5:6]
        depth_rows = zeros
        for row in range(elements):
            mixed = hot[0:1] * depth_store[row * elements, 0:1]
            for t in range(1, elements):
                mixed = mixed + hot[t : t + 1] * depth_store[row * elements + t, 0:1]
            depth_rows = jnp.where(sub_index == row, mixed, depth_rows)
        load_rows = jnp.where(sub_index == 4, load, jnp.where(sub_index == 5, 1.0, 0.0))
        forms = [
            right_geometry(at(right_base, place)),
            right_table(at(rho_rows, place)),
            right_table(depth_rows),
            right_geometry(load_rows),
        ]
        alone = hot[0:1] * depth_store[0, 0:1]
        for t in range(1, elements):
            alone = alone + hot[t : t + 1] * depth_store[t * elements + t, 0:1]
        self_weight[block + 1] = jnp.where(sub_index == 0, alone / (load + load), 0.0)
        right_own[block + 1] = jnp.concatenate(forms, axis=1)
    self_weight[0] = zeros
    right_own[0] = jnp.zeros(right_own.shape[1:], jnp.bfloat16)
    for block in range(blocks_dev + 1):
        total[block] = jnp.zeros(total.shape[1:], jnp.float32)
        energy[block] = zeros

    def second_pass(start, size):
        pair = fetch(own_list, start)
        for step in range(size):
            first, second = pair(step)
            load = jnp.sum(coord[second], axis=0, keepdims=True)
            base = at(left_base, second)
            base = base + jnp.where(sub_index == 5, load, 0.0)
            left = left_form(base, at(onehot, second))
            local_first = jnp.maximum(first - own_base, 0)
            mixed = cross(left, right_own[local_first])
            dist, rho, depth, both_load = [mixed[:, k * TILE : (k + 1) * TILE] for k in range(4)]
            ratio = dist * rho
            squared = ratio * ratio
            bond = jnp.exp2(squared * ratio)
            weight = depth * bond / both_load
            pull = weight * squared * rho
            pull_high = pull.astype(jnp.bfloat16)
            pulls[step, :, 0:TILE] = pull_high
            pulls[step, :, TILE:] = (pull - pull_high.astype(jnp.float32)).astype(jnp.bfloat16)
            same = jnp.where(first == second, 1.0, 0.0)
            update = fold(weight) - same * self_weight[local_first]
            energy[local_first] = energy[local_first] + update
        for step in range(size):
            first, second = pair(step)
            form = force_form(at(left_base, second), sub_index)
            sums = jnp.dot(form, pulls[step], preferred_element_type=jnp.float32)
            local_first = jnp.maximum(first - own_base, 0)
            total[local_first] = total[local_first] + sums

    def second_group(group, carry):
        second_pass(group * SMALL, SMALL)
        return carry

    def second_large(group, carry):
        second_pass(group * MIDDLE, MIDDLE)
        return carry

    middles = (own_count + MIDDLE - SMALL - 1) // MIDDLE
    lax.fori_loop(0, middles, second_large, 0)
    lax.fori_loop(middles * (MIDDLE // SMALL), (own_count + SMALL - 1) // SMALL, second_group, 0)

    for block in range(blocks_dev):
        both = total[block + 1]
        sums = both[:, :TILE] + both[:, TILE:]
        here = at(left_base, own_base + block + 1)
        lanes = slice(block * TILE, (block + 1) * TILE)
        for d in range(3):
            moment = sums[d : d + 1] + sums[8 + d : 9 + d] + sums[11 + d : 12 + d]
            out[d : d + 1, lanes] = (-6.0 / LOG2E) * (moment - here[d : d + 1] * sums[4:5])
        out[3:4, lanes] = -jnp.sum(energy[block + 1], axis=0, keepdims=True)


def local(order, positions, types, radius_type, valence_type, bond_depth, pair_tiles, tile_count):
    atom_dev = positions.shape[1]
    blocks_dev = atom_dev // TILE
    rows = lax.axis_size("row")
    cols = lax.axis_size("col")
    slots = rows * cols
    blocks = slots * blocks_dev
    tiles_dev = pair_tiles.shape[2]

    smem = pl.BlockSpec(memory_space=pltpu.SMEM)
    vmem = pl.BlockSpec(memory_space=pltpu.VMEM)
    packed = pl.pallas_call(
        functools.partial(pack, order),
        out_shape=pltpu.VMEM((5 * SUB, TILE), jnp.float32),
        in_specs=[smem, vmem, vmem, vmem],
        out_specs=vmem,
    )(tile_count, positions, types.reshape(blocks_dev, TILE), jnp.transpose(pair_tiles[0, 0]))
    elements = radius_type.shape[0]
    squares = (elements * elements, SUB, TILE)
    stores = pl.pallas_call(
        functools.partial(tables, elements),
        out_shape=(
            pltpu.VMEM(squares, jnp.float32),
            pltpu.VMEM(squares, jnp.float32),
            pltpu.VMEM((elements, SUB, TILE), jnp.float32),
        ),
        in_specs=[smem, smem, smem],
        out_specs=(vmem, vmem, vmem),
    )(radius_type, valence_type, bond_depth)

    gathered = packed
    for bit in order[0]:
        other = lax.ppermute(gathered, "col", [(i, i ^ bit) for i in range(cols)])
        gathered = jnp.concatenate([gathered, other], axis=0)
    inner = cols >> len(order[0])
    groups = [
        [row * cols + start + k for row in range(rows) for k in range(inner)] for start in range(0, cols, inner)
    ]
    gathered = lax.all_gather(gathered, ("row", "col"), axis=0, axis_index_groups=groups, tiled=True)

    gathered = pltpu.with_memory_space_constraint(gathered, pltpu.VMEM)
    stores = [pltpu.with_memory_space_constraint(store, pltpu.VMEM) for store in stores]
    shift = (blocks + 1).bit_length()
    chunks = -(-slots * tiles_dev // (SUB * TILE)) * SUB
    own_chunks = -(-cols * tiles_dev // (SUB * TILE)) * SUB
    return pl.pallas_call(
        functools.partial(kernel, order, elements, shift),
        out_shape=jax.ShapeDtypeStruct((4, atom_dev), jnp.float32),
        in_specs=[vmem, vmem, vmem, vmem],
        out_specs=vmem,
        scratch_shapes=[
            pltpu.VMEM((blocks * SUB + SUB, TILE), jnp.float32),
            pltpu.VMEM((blocks * SUB + SUB, TILE), jnp.float32),
            pltpu.VMEM((blocks * SUB + SUB, TILE), jnp.float32),
            pltpu.VMEM((blocks * SUB + SUB, TILE), jnp.float32),
            pltpu.VMEM((blocks + 1, SUB, TILE), jnp.float32),
            pltpu.VMEM((blocks_dev + 1, 10 * SUB, 4 * TILE), jnp.bfloat16),
            pltpu.VMEM((blocks_dev + 1, SUB, TILE), jnp.float32),
            pltpu.VMEM((blocks_dev + 1, 2 * SUB, 2 * TILE), jnp.float32),
            pltpu.VMEM((blocks_dev + 1, SUB, TILE), jnp.float32),
            pltpu.VMEM((MIDDLE, TILE, 2 * TILE), jnp.bfloat16),
            pltpu.VMEM((slots, TILE), jnp.float32),
            pltpu.VMEM((slots, TILE), jnp.float32),
            pltpu.VMEM((slots, TILE), jnp.float32),
            pltpu.VMEM((TILE, TILE), jnp.float32),
            pltpu.VMEM((own_chunks, TILE), jnp.int32),
            pltpu.VMEM((chunks, TILE), jnp.int32),
            pltpu.SMEM((own_chunks, TILE), jnp.int32),
            pltpu.SMEM((chunks, TILE), jnp.int32),
            pltpu.SemaphoreType.DMA,
            pltpu.SemaphoreType.DMA,
            pltpu.SemaphoreType.DMA,
        ],
        compiler_params=pltpu.CompilerParams(vmem_limit_bytes=56 * 1024 * 1024),
    )(*stores, gathered)


def solution(mesh):
    order = stage_bits(mesh.shape["col"], mesh.shape["row"])
    in_specs = (
        P(None, ("row", "col")),
        P(("row", "col")),
        P(),
        P(),
        P(),
        P("row", "col", None, None),
        P("row", "col"),
    )
    out_specs = P(None, ("row", "col"))
    return jax.shard_map(
        functools.partial(local, order), mesh=mesh, in_specs=in_specs, out_specs=out_specs, check_vma=False
    )
```

```python
import functools
import math

import jax
import jax.numpy as jnp
from jax import lax
from jax.experimental import pallas as pl
from jax.experimental.pallas import tpu as pltpu
from jax.sharding import PartitionSpec as P

TILE = 128
SUB = 8
LARGE = 64
MIDDLE = 16
SMALL = 8
LOG2E = math.log2(math.e)
SCALE = LOG2E ** (1.0 / 3.0)


def log2(size):
    return size.bit_length() - 1


def stage_bits(col_size, row_size):
    bits = [bit for bit in (col_size // 4, col_size // 2) if bit >= 2]
    return bits, col_size, row_size


def outer_part(order, col):
    total = col * 0
    for place, bit in enumerate(order[0]):
        total = total | (((col >> log2(bit)) & 1) << place)
    return total


def inner_part(order, col):
    bits, col_size, row_size = order
    return (col & ((col_size >> len(bits)) - 1)) << len(bits)


def row_part(order, row):
    return row << log2(order[1])


def col_part(order, col):
    return inner_part(order, col) | outer_part(order, col)


def pack(order, count, positions, types, tiles, packed):
    blocks_dev = types.shape[0]
    tiles_dev = tiles.shape[1]
    row = row_part(order, lax.axis_index("row"))
    col = col_part(order, lax.axis_index("col"))
    for d in range(3):
        for block in range(blocks_dev):
            place = d * blocks_dev + block
            packed[place : place + 1, :] = positions[d : d + 1, block * TILE : (block + 1) * TILE]
    packed[3 * blocks_dev : 4 * blocks_dev, :] = types[...].astype(jnp.float32)
    packed[4 * blocks_dev :, :] = jnp.zeros((SUB, TILE), jnp.float32)
    near, far = tiles[0:1, :], tiles[1:2, :]
    shift = blocks_dev.bit_length() - 1
    first = ((row | col_part(order, near >> shift)) << shift) | (near & (blocks_dev - 1))
    second = ((row_part(order, far >> shift) | col) << shift) | (far & (blocks_dev - 1))
    live = lax.broadcasted_iota(jnp.int32, (1, tiles_dev), 1) < count[0, 0]
    items = (first & 255, first >> 8, second & 255, second >> 8, jnp.where(live, 1, 0))
    for place, item in enumerate(items):
        start = 4 * blocks_dev + place
        packed[start : start + 1, 0:tiles_dev] = item.astype(jnp.float32)


def tables(elements, radius, valence, depth, rho_store, depth_store, valence_store):
    shape = (SUB, TILE)
    for t in range(elements):
        valence_store[t] = jnp.full(shape, valence[t], jnp.float32)
        for u in range(elements):
            rho = jnp.full(shape, 0.5 * (radius[t] + radius[u]), jnp.float32)
            rho_store[t * elements + u] = -SCALE / (rho * rho)
            depth_store[t * elements + u] = jnp.full(shape, depth[u, t] * (valence[u] + valence[t]), jnp.float32)


def pieces(value):
    high = value.astype(jnp.bfloat16).astype(jnp.float32)
    rest = value - high
    mid = rest.astype(jnp.bfloat16).astype(jnp.float32)
    return high, mid, rest - mid


def left_form(base, onehot):
    high, mid, low = pieces(base)
    zero = jnp.zeros_like(base)
    stack = jnp.concatenate([high, high, mid, high, low, mid, onehot, onehot, onehot, zero], axis=0)
    return stack.astype(jnp.bfloat16)


def right_geometry(base):
    high, mid, low = pieces(base)
    zero = jnp.zeros_like(base)
    stack = jnp.concatenate([high, mid, high, low, high, mid, zero, zero, zero, zero], axis=0)
    return stack.astype(jnp.bfloat16)


def right_table(rows):
    high, mid, low = pieces(rows)
    zero = jnp.zeros_like(rows)
    stack = jnp.concatenate([zero] * 6 + [high, mid, low, zero], axis=0)
    return stack.astype(jnp.bfloat16)


def force_form(base, sub_index):
    high, mid, low = pieces(base)
    rest = jnp.where(sub_index < 3, mid, jnp.where(sub_index < 6, jnp.roll(low, 3, axis=0), 0.0))
    return jnp.concatenate([high, rest], axis=0).astype(jnp.bfloat16)


def cross(left, right):
    return lax.dot_general(left, right, (((0,), (0,)), ((), ())), preferred_element_type=jnp.float32)


def fold(value):
    return jnp.sum(value.reshape(TILE // SUB, SUB, TILE), axis=0)


def kernel(
    order,
    elements,
    shift,
    rho_store,
    depth_store,
    valence,
    atoms,
    out,
    left_base,
    right_base,
    rho_rows,
    coord,
    right_own,
    self_weight,
    total,
    energy,
    pulls,
    ranks,
    marks,
    firsts,
    second_cols,
    own_flat,
    work_flat,
    own_list,
    work_list,
    own_sem,
    head_sem,
    work_sem,
):
    payload = 5 * SUB
    slots = atoms.shape[0] // payload
    blocks_dev = SUB
    blocks = slots * blocks_dev
    flip = outer_part(order, lax.axis_index("col")) * blocks_dev
    own_slot = row_part(order, lax.axis_index("row")) | inner_part(order, lax.axis_index("col"))
    own_base = own_slot * blocks_dev
    ones = jnp.ones((SUB, TILE), jnp.float32)
    zeros = jnp.zeros((SUB, TILE), jnp.float32)

    def put(ref, slot, row, value):
        ref[pl.ds((slot * blocks_dev + 1) * SUB + row, blocks_dev, stride=SUB), :] = value

    def prepare(slot, carry):
        start = pl.multiple_of(slot * payload, SUB)
        x = atoms[pl.ds(start, SUB), :]
        y = atoms[pl.ds(start + SUB, SUB), :]
        z = atoms[pl.ds(start + 2 * SUB, SUB), :]
        kind = atoms[pl.ds(start + 3 * SUB, SUB), :]
        square = x * x + y * y + z * z
        hot = [jnp.where(kind == float(t), 1.0, 0.0) for t in range(elements)]
        value = zeros
        for t in range(elements):
            value = value + hot[t] * valence[t]
        for row, item in enumerate((x, y, z, square, ones, value, kind)):
            put(left_base, slot, row, item)
        for row, item in enumerate((-2.0 * x, -2.0 * y, -2.0 * z, ones, square)):
            put(right_base, slot, row, item)
        for row in range(elements):
            mixed = hot[0] * rho_store[row * elements]
            for t in range(1, elements):
                mixed = mixed + hot[t] * rho_store[row * elements + t]
            put(rho_rows, slot, row, mixed)
        for block in range(blocks_dev):
            coord[slot * blocks_dev + block + 1] = zeros
        return carry

    lax.fori_loop(0, slots, prepare, 0)
    for ref in (left_base, right_base, rho_rows):
        ref[0:SUB, :] = zeros

    lane = lax.broadcasted_iota(jnp.int32, (TILE, TILE), 1)
    sublane = lax.broadcasted_iota(jnp.int32, (TILE, TILE), 0)
    before = jnp.where(sublane < lane, 1.0, 0.0).astype(jnp.bfloat16)
    slot_col = lax.broadcasted_iota(jnp.int32, (slots, slots), 1)
    slot_row = lax.broadcasted_iota(jnp.int32, (slots, slots), 0)
    above = jnp.where(slot_col < slot_row, 1.0, 0.0).astype(jnp.bfloat16)

    def meta(row):
        return atoms[pl.ds(4 * SUB + row, slots, stride=payload), :]

    first_all = (meta(0) + 256.0 * meta(1)).astype(jnp.int32) ^ flip
    live_all = meta(4)
    firsts[...] = first_all.astype(jnp.float32)

    def rank(mark):
        count = mark.astype(jnp.bfloat16)
        inside = jnp.dot(count, before, preferred_element_type=jnp.float32)
        earlier = jnp.dot(above, count, preferred_element_type=jnp.float32)
        place = inside + jnp.sum(earlier, axis=1, keepdims=True)
        ranks[...] = jnp.where(mark > 0.0, place, -1.0)
        return jnp.sum(mark).astype(jnp.int32)

    position = sublane.astype(jnp.float32)
    batch = min(slots, 4 * SUB)

    def compact(chunk, flat, columns):
        offset = jnp.float32(1.0) * (chunk * TILE)

        def some(group, carry):
            total = carry
            for part in range(batch // SUB):
                start = pl.multiple_of(group * batch + part * SUB, SUB)
                wanted = ranks[pl.ds(start, SUB), :] - offset
                picks = [
                    jnp.where(wanted[k : k + 1] == position, 1.0, 0.0).astype(jnp.bfloat16) for k in range(SUB)
                ]
                entries = [
                    atoms[pl.ds(pl.multiple_of((start + k) * payload + 4 * SUB, SUB), SUB), :].astype(
                        jnp.bfloat16
                    )
                    for k in range(SUB)
                ]
                total = total + lax.dot_general(
                    jnp.concatenate(entries, axis=1),
                    jnp.concatenate(picks, axis=1),
                    (((1,), (1,)), ((), ())),
                    preferred_element_type=jnp.float32,
                )
            return total

        row = lax.fori_loop(0, slots // batch, some, zeros)
        first = (row[0:1] + 256.0 * row[1:2]).astype(jnp.int32) ^ flip
        second = (row[2:3] + 256.0 * row[3:4]).astype(jnp.int32) ^ flip
        valid = row[4:5] > 0.0
        flat[pl.ds(chunk, 1), :] = jnp.where(valid, ((first + 1) << shift) | (second + 1), 0)
        if columns:
            target = jnp.where(valid, second, -1).astype(jnp.float32)
            column = jnp.transpose(jnp.broadcast_to(target, (SUB, TILE)))[:, 0:1]
            second_cols[...] = jnp.broadcast_to(column, (TILE, TILE))

    def send(source, target, group, semaphore):
        start = pl.multiple_of(group * SUB, SUB)
        return pltpu.make_async_copy(source.at[pl.ds(start, SUB)], target.at[pl.ds(start, SUB)], semaphore)

    def send_rest(source, target, count, semaphore):
        def one(group, carry):
            copy = send(source, target, group, semaphore)
            copy.start()
            copy.wait()
            return carry

        lax.fori_loop(1, (count + SUB * TILE - 1) // (SUB * TILE), one, 0)

    own_mark = jnp.where((first_all >> log2(blocks_dev)) == own_slot, live_all, 0.0)
    marks[...] = own_mark
    own_count = rank(own_mark)

    def own_chunk(chunk, carry):
        compact(chunk, own_flat, True)
        part = 4 * SUB
        filled = jnp.minimum(own_count - chunk * TILE, TILE)

        def some(group, carry):
            cols = second_cols[pl.ds(pl.multiple_of(group * part, part), part), :]

            def rows(slot_group, carry):
                for piece in range(batch // SUB):
                    start = pl.multiple_of(slot_group * batch + piece * SUB, SUB)
                    here = firsts[pl.ds(start, SUB), :]
                    found = []
                    for k in range(SUB):
                        hit = jnp.where(cols == here[k : k + 1], 1.0, 0.0)
                        found.append(jnp.max(hit, axis=0, keepdims=True))
                    old = marks[pl.ds(start, SUB), :]
                    marks[pl.ds(start, SUB), :] = jnp.maximum(old, jnp.concatenate(found, axis=0))
                return carry

            return lax.fori_loop(0, slots // batch, rows, carry)

        lax.fori_loop(0, (filled + part - 1) // part, some, 0)
        return carry

    lax.fori_loop(0, (own_count + TILE - 1) // TILE, own_chunk, 0)
    send_rest(own_flat, own_list, own_count, own_sem)
    own_copy = send(own_flat, own_list, 0, own_sem)
    own_copy.start()

    work_count = rank(marks[...] * live_all)

    head_copy = pltpu.make_async_copy(work_flat.at[pl.ds(0, 1)], work_list.at[pl.ds(0, 1)], head_sem)
    compact(0, work_flat, False)
    head_copy.start()

    def work_chunk(chunk, carry):
        compact(chunk, work_flat, False)
        return carry

    lax.fori_loop(1, (work_count + TILE - 1) // TILE, work_chunk, 0)
    send_rest(work_flat, work_list, work_count, work_sem)
    rest_copy = pltpu.make_async_copy(
        work_flat.at[pl.ds(1, SUB - 1)], work_list.at[pl.ds(1, SUB - 1)], work_sem
    )
    rest_copy.start()
    head_copy.wait()
    own_copy.wait()

    sub_index = lax.broadcasted_iota(jnp.int32, (SUB, TILE), 0)
    sub_value = sub_index.astype(jnp.float32)

    def at(ref, block, used):
        rows = ref[pl.ds(pl.multiple_of(block * SUB, SUB), SUB), :]
        return jnp.where(sub_index < used, rows, 0.0)

    def left_at(block):
        return at(left_base, block, 6)

    def right_at(block):
        return at(right_base, block, 5)

    def rho_at(block):
        return at(rho_rows, block, elements)

    def onehot_at(block):
        kind = left_base[pl.ds(block * SUB + 6, 1), :]
        return jnp.where(kind == sub_value, 1.0, 0.0)

    def fetch(ref, start):
        row = lax.shift_right_logical(start, TILE.bit_length() - 1)
        column = start & (TILE - 1)

        def at_step(step):
            code = ref[row, column + step]
            return code >> shift, code & ((1 << shift) - 1)

        return at_step

    def first_pass(start, size):
        pair = fetch(work_list, start)
        for step in range(size):
            first, second = pair(step)
            left = left_form(left_at(second), onehot_at(second))
            right = jnp.concatenate(
                [right_geometry(right_at(first)), right_table(rho_at(first))], axis=1
            )
            both = cross(left, right)
            ratio = both[:, :TILE] * both[:, TILE:]
            bond = jnp.exp2(ratio * ratio * ratio)
            same = jnp.where(first == second, 1.0 / SUB, 0.0)
            coord[first] = coord[first] + (fold(bond) - same)

    fulls = work_count // LARGE
    early = TILE // LARGE

    def large(group, carry):
        first_pass(group * LARGE, LARGE)
        return carry

    def small(group, carry):
        first_pass(group * SMALL, SMALL)
        return carry

    lax.fori_loop(0, jnp.minimum(fulls, early), large, 0)
    rest_copy.wait()
    lax.fori_loop(jnp.minimum(fulls, early), fulls, large, 0)

    def middle(group, carry):
        first_pass(group * MIDDLE, MIDDLE)
        return carry

    edge = (work_count + MIDDLE - SMALL - 1) // MIDDLE
    lax.fori_loop(fulls * (LARGE // MIDDLE), edge, middle, 0)
    lax.fori_loop(edge * (MIDDLE // SMALL), (work_count + SMALL - 1) // SMALL, small, 0)


    for block in range(blocks_dev):
        place = own_base + block + 1
        base = left_at(place)
        hot = onehot_at(place)
        load = jnp.sum(coord[place], axis=0, keepdims=True) + base[5:6]
        depth_rows = zeros
        for row in range(elements):
            mixed = hot[0:1] * depth_store[row * elements, 0:1]
            for t in range(1, elements):
                mixed = mixed + hot[t : t + 1] * depth_store[row * elements + t, 0:1]
            depth_rows = jnp.where(sub_index == row, mixed, depth_rows)
        load_rows = jnp.where(sub_index == 4, load, jnp.where(sub_index == 5, 1.0, 0.0))
        forms = [
            right_geometry(right_at(place)),
            right_table(rho_at(place)),
            right_table(depth_rows),
            right_geometry(load_rows),
        ]
        alone = hot[0:1] * depth_store[0, 0:1]
        for t in range(1, elements):
            alone = alone + hot[t : t + 1] * depth_store[t * elements + t, 0:1]
        self_weight[block + 1] = jnp.where(sub_index == 0, alone / (load + load), 0.0)
        right_own[block + 1] = jnp.concatenate(forms, axis=1)
    self_weight[0] = zeros
    right_own[0] = jnp.zeros(right_own.shape[1:], jnp.bfloat16)
    for block in range(blocks_dev + 1):
        total[block] = jnp.zeros(total.shape[1:], jnp.float32)
        energy[block] = zeros

    def second_pass(start, size):
        pair = fetch(own_list, start)
        for step in range(size):
            first, second = pair(step)
            load = jnp.sum(coord[second], axis=0, keepdims=True)
            base = left_at(second)
            base = base + jnp.where(sub_index == 5, load, 0.0)
            left = left_form(base, onehot_at(second))
            local_first = jnp.maximum(first - own_base, 0)
            mixed = cross(left, right_own[local_first])
            dist, rho, depth, both_load = [mixed[:, k * TILE : (k + 1) * TILE] for k in range(4)]
            ratio = dist * rho
            squared = ratio * ratio
            bond = jnp.exp2(squared * ratio)
            weight = depth * bond / both_load
            pull = weight * squared * rho
            pull_high = pull.astype(jnp.bfloat16)
            pulls[step, :, 0:TILE] = pull_high
            pulls[step, :, TILE:] = (pull - pull_high.astype(jnp.float32)).astype(jnp.bfloat16)
            same = jnp.where(first == second, 1.0, 0.0)
            update = fold(weight) - same * self_weight[local_first]
            energy[local_first] = energy[local_first] + update
        for step in range(size):
            first, second = pair(step)
            form = force_form(left_at(second), sub_index)
            sums = jnp.dot(form, pulls[step], preferred_element_type=jnp.float32)
            local_first = jnp.maximum(first - own_base, 0)
            total[local_first] = total[local_first] + sums

    def second_group(group, carry):
        second_pass(group * SMALL, SMALL)
        return carry

    def second_large(group, carry):
        second_pass(group * MIDDLE, MIDDLE)
        return carry

    middles = (own_count + MIDDLE - SMALL - 1) // MIDDLE
    lax.fori_loop(0, middles, second_large, 0)
    lax.fori_loop(middles * (MIDDLE // SMALL), (own_count + SMALL - 1) // SMALL, second_group, 0)

    for block in range(blocks_dev):
        both = total[block + 1]
        sums = both[:, :TILE] + both[:, TILE:]
        here = left_at(own_base + block + 1)
        lanes = slice(block * TILE, (block + 1) * TILE)
        for d in range(3):
            moment = sums[d : d + 1] + sums[8 + d : 9 + d] + sums[11 + d : 12 + d]
            out[d : d + 1, lanes] = (-6.0 / LOG2E) * (moment - here[d : d + 1] * sums[4:5])
        out[3:4, lanes] = -jnp.sum(energy[block + 1], axis=0, keepdims=True)


def local(order, positions, types, radius_type, valence_type, bond_depth, pair_tiles, tile_count):
    atom_dev = positions.shape[1]
    blocks_dev = atom_dev // TILE
    rows = lax.axis_size("row")
    cols = lax.axis_size("col")
    slots = rows * cols
    blocks = slots * blocks_dev
    tiles_dev = pair_tiles.shape[2]

    smem = pl.BlockSpec(memory_space=pltpu.SMEM)
    vmem = pl.BlockSpec(memory_space=pltpu.VMEM)
    packed = pl.pallas_call(
        functools.partial(pack, order),
        out_shape=pltpu.VMEM((5 * SUB, TILE), jnp.float32),
        in_specs=[smem, vmem, vmem, vmem],
        out_specs=vmem,
    )(tile_count, positions, types.reshape(blocks_dev, TILE), jnp.transpose(pair_tiles[0, 0]))
    elements = radius_type.shape[0]
    squares = (elements * elements, SUB, TILE)
    stores = pl.pallas_call(
        functools.partial(tables, elements),
        out_shape=(
            pltpu.VMEM(squares, jnp.float32),
            pltpu.VMEM(squares, jnp.float32),
            pltpu.VMEM((elements, SUB, TILE), jnp.float32),
        ),
        in_specs=[smem, smem, smem],
        out_specs=(vmem, vmem, vmem),
    )(radius_type, valence_type, bond_depth)

    gathered = packed
    for bit in order[0]:
        other = lax.ppermute(gathered, "col", [(i, i ^ bit) for i in range(cols)])
        gathered = jnp.concatenate([gathered, other], axis=0)
    inner = cols >> len(order[0])
    groups = [
        [row * cols + start + k for row in range(rows) for k in range(inner)] for start in range(0, cols, inner)
    ]
    gathered = lax.all_gather(gathered, ("row", "col"), axis=0, axis_index_groups=groups, tiled=True)

    gathered = pltpu.with_memory_space_constraint(gathered, pltpu.VMEM)
    stores = [pltpu.with_memory_space_constraint(store, pltpu.VMEM) for store in stores]
    shift = (blocks + 1).bit_length()
    chunks = -(-slots * tiles_dev // (SUB * TILE)) * SUB
    own_chunks = -(-cols * tiles_dev // (SUB * TILE)) * SUB
    return pl.pallas_call(
        functools.partial(kernel, order, elements, shift),
        out_shape=jax.ShapeDtypeStruct((4, atom_dev), jnp.float32),
        in_specs=[vmem, vmem, vmem, vmem],
        out_specs=vmem,
        scratch_shapes=[
            pltpu.VMEM((blocks * SUB + SUB, TILE), jnp.float32),
            pltpu.VMEM((blocks * SUB + SUB, TILE), jnp.float32),
            pltpu.VMEM((blocks * SUB + SUB, TILE), jnp.float32),
            pltpu.VMEM((blocks + 1, SUB, TILE), jnp.float32),
            pltpu.VMEM((blocks_dev + 1, 10 * SUB, 4 * TILE), jnp.bfloat16),
            pltpu.VMEM((blocks_dev + 1, SUB, TILE), jnp.float32),
            pltpu.VMEM((blocks_dev + 1, 2 * SUB, 2 * TILE), jnp.float32),
            pltpu.VMEM((blocks_dev + 1, SUB, TILE), jnp.float32),
            pltpu.VMEM((MIDDLE, TILE, 2 * TILE), jnp.bfloat16),
            pltpu.VMEM((slots, TILE), jnp.float32),
            pltpu.VMEM((slots, TILE), jnp.float32),
            pltpu.VMEM((slots, TILE), jnp.float32),
            pltpu.VMEM((TILE, TILE), jnp.float32),
            pltpu.VMEM((own_chunks, TILE), jnp.int32),
            pltpu.VMEM((chunks, TILE), jnp.int32),
            pltpu.SMEM((own_chunks, TILE), jnp.int32),
            pltpu.SMEM((chunks, TILE), jnp.int32),
            pltpu.SemaphoreType.DMA,
            pltpu.SemaphoreType.DMA,
            pltpu.SemaphoreType.DMA,
        ],
        compiler_params=pltpu.CompilerParams(vmem_limit_bytes=56 * 1024 * 1024),
    )(*stores, gathered)


def solution(mesh):
    order = stage_bits(mesh.shape["col"], mesh.shape["row"])
    in_specs = (
        P(None, ("row", "col")),
        P(("row", "col")),
        P(),
        P(),
        P(),
        P("row", "col", None, None),
        P("row", "col"),
    )
    out_specs = P(None, ("row", "col"))
    return jax.shard_map(
        functools.partial(local, order), mesh=mesh, in_specs=in_specs, out_specs=out_specs, check_vma=False
    )
```
